32 devices in a mesh: section: 4 (over y, x), batch: 8 (over z, core).
Axes of the slice: x: 2, y: 2, z: 4, core: 2. Of those that a mesh axis runs over, the one named last changes fastest.
Arguments:
- frames_in: bfloat16 [4096, 1024], P('batch'), may hold values from -6 to 6
- cotangent: bfloat16 [4096, 1024], P('batch'), may hold values from -6 to 6
- qkv_weight: bfloat16 [4, 1024, 3072], P('section'), may hold values from -0.1875 to 0.1875
- out_weight: bfloat16 [4, 1024, 1024], P('section'), may hold values from -1 to 1
- up_weight: bfloat16 [4, 1024, 4096], P('section'), may hold values from -0.1875 to 0.1875
- down_weight: bfloat16 [4, 4096, 1024], P('section'), may hold values from -0.09375 to 0.09375
- norm_table: float32 [4, 32, 1024], P('section'), may hold values from -0.5 to 0.5
- lengths: int32 [32], P('batch'), may hold values from 75 to 128, as said below
- codebooks: int32 [32], P('batch'), may hold values from 1 to 7
Outputs:
- layer_outputs: bfloat16 [4, 4096, 1024], P('section', 'batch')
- input_grads: bfloat16 [4, 4096, 1024], P('section', 'batch')
- grad_qkv: float32 [4, 1024, 3072], P('section', 'batch')
- grad_out: float32 [4, 1024, 1024], P('section', 'batch')
- grad_up: float32 [4, 1024, 4096], P('section', 'batch')
- grad_down: float32 [4, 4096, 1024], P('section', None, 'batch')
- grad_norms: float32 [4, 32, 1024], P('section', None, 'batch')
The draws below stay inside these ranges and needn't reach their ends.
Inputs may be any that keep to these rules, and one draw needn't show every extreme that they name: `lengths`: every utterance has at least 75 live frames; in every draw some utterance has all 128. `codebooks`: the codebook section that the NAR layers are conditioned on.
All inputs are finite; a program needn't handle non-finite values.
Results may differ from the reference program's by a relative error of at most 0.017.
Values may be sent and summed in bfloat16 or wider, within the bound.
No kernel may reach another device: no remote copies, remote signals or barrier semaphores. Data moves between devices by JAX's collectives and lax.ppermute only.
A program may use at most 320 MiB of HBM per device.

```python
import jax
import jax.numpy as jnp
from jax import lax

D = 1024
HEADS = 16
FF = 4096
CB = 8
PAD = 128
MINLEN = 75
UTTS = 32
TOKENS = 4096
N_SECTION = 4


def draw_lengths(key, part):
    key = jax.random.fold_in(key, 11)
    key_base, key_top = jax.random.split(key)
    base_lengths = jax.random.randint(key_base, (UTTS,), MINLEN, PAD + 1)
    longest_at = jax.random.randint(key_top, (), 0, UTTS)
    return jnp.where(jnp.arange(UTTS) == longest_at, PAD, base_lengths).astype(jnp.int32)


def plant(drawn, rng, low, top_value):
    dims = drawn.shape
    spot = [jax.random.randint(jax.random.fold_in(rng, axis), (), 0, dims[axis]) for axis in range(len(dims))]
    drawn = drawn.at[tuple(spot)].set(low)
    longest = dims.index(max(dims))
    spot[longest] = (spot[longest] + 1) % dims[longest]
    return drawn.at[tuple(spot)].set(top_value)


def shard_levels(own_key, shape, cuts, least, largest):
    loudness = 1.0
    for dim, parts in cuts:
        draws = jax.random.uniform(jax.random.fold_in(jax.random.fold_in(own_key, 6), dim), (parts,), jnp.float32, least / len(cuts), largest / len(cuts))
        loudness = loudness * jnp.repeat(jnp.exp(draws), shape[dim] // parts).reshape((-1,) + (1,) * (len(shape) - 1 - dim))
    return loudness


def normal_values(stream_key, shape, spread, most, cuts=(), held_as=jnp.bfloat16):
    values = jax.random.normal(stream_key, shape, jnp.float32) * spread
    if len(cuts) > 0:
        values = shard_levels(stream_key, shape, cuts, -0.22, 0.18) * values
    return jnp.clip(values, min=-most, max=most).astype(held_as)


def setup_inputs(seed: int = 0) -> dict:
    streams_of = jax.random.split(jax.random.key(seed), 10)
    frames_in = normal_values(streams_of[0], (TOKENS, D), 1.0, 6.0, ((0, 8),))
    cotangent = normal_values(streams_of[1], (TOKENS, D), 1.0, 6.0, ((0, 8),))
    qkv_weight = normal_values(streams_of[2], (N_SECTION, D, 3 * D), D ** -0.5, 0.1875, ((0, 4),))
    out_weight = normal_values(streams_of[3], (N_SECTION, D, D), (D // 32) ** -0.5, 1.0, ((0, 4),))
    up_weight = normal_values(streams_of[4], (N_SECTION, D, FF), D ** -0.5, 0.1875, ((0, 4),))
    down_weight = normal_values(streams_of[5], (N_SECTION, FF, D), FF ** -0.5, 0.09375, ((0, 4),))
    norm_table = jnp.clip(jax.random.uniform(streams_of[6], (N_SECTION, 4 * CB, D), jnp.float32, -0.5, 0.5) * shard_levels(streams_of[6], (N_SECTION, 4 * CB, D), ((0, 4),), -0.4, 0.0), -0.5, 0.5)
    lengths = draw_lengths(jax.random.fold_in(streams_of[9], 71), 0)
    codebooks = plant(jax.random.randint(streams_of[8], (UTTS,), 1, CB), jax.random.fold_in(streams_of[8], 1), 1, CB - 1).astype(jnp.int32)
    return {"frames_in": frames_in, "cotangent": cotangent, "qkv_weight": qkv_weight, "out_weight": out_weight, "up_weight": up_weight, "down_weight": down_weight, "norm_table": norm_table, "lengths": lengths, "codebooks": codebooks}


@jax.custom_vjp
def low(v):
    return lax.optimization_barrier(v.astype(jnp.bfloat16)).astype(jnp.float32)

@jax.custom_vjp
def low_back(v):
    return v

def low_keep(v):
    return (low(v), None)

def low_pass(kept, grad):
    return (grad,)

def back_keep(v):
    return (v, None)

def back_low(kept, grad):
    return (low(grad),)
low.defvjp(low_keep, low_pass)
low_back.defvjp(back_keep, back_low)
epsilon = 1e-05
masked_score = -1e+30

def product(left_side, right_side):
    return jnp.dot(left_side, right_side, precision=lax.Precision.HIGHEST)

def normalize(values, gain_row, shift_row):
    centre = values - lax.optimization_barrier(jnp.mean(values, axis=-1, keepdims=True))
    reciprocal = lax.rsqrt(lax.optimization_barrier(jnp.mean(centre * centre, axis=-1, keepdims=True)) + epsilon)
    return centre * reciprocal * (1.0 + gain_row) + shift_row

def decoder_layer(inputs, qkv_weight, out_weight, up_weight, down_weight, norm_rows, length, is_nar):
    frames, features = inputs.shape
    head_size = features // HEADS
    normed_one = low(normalize(inputs, norm_rows[0], norm_rows[1]))
    packed = low_back(low(product(normed_one, qkv_weight)))
    heads_split = packed.reshape(frames, 3, HEADS, head_size)
    query_heads, key_heads, value_heads = (heads_split[:, 0], heads_split[:, 1], heads_split[:, 2])
    inv_root = head_size ** (-0.5)
    scores = low_back(jnp.einsum('qhd,khd->hqk', query_heads, key_heads, precision=lax.Precision.HIGHEST) * inv_root)
    positions = jnp.arange(frames, dtype=jnp.int32)
    causal = positions[None, :] <= positions[:, None]
    allowed = (positions[None, :] < length) & jnp.logical_or(is_nar, causal)
    scores = jnp.where(allowed[None], scores, masked_score)
    row_max = lax.optimization_barrier(jnp.max(scores, axis=-1, keepdims=True))
    exp_scores = jnp.exp(scores - row_max)
    attn_probs = low(exp_scores / lax.optimization_barrier(jnp.sum(exp_scores, axis=-1, keepdims=True)))
    attn_mixed = jnp.einsum('hqk,khd->qhd', attn_probs, value_heads, precision=lax.Precision.HIGHEST)
    attended = low_back(low(attn_mixed.reshape(frames, features)))
    hidden = inputs + low_back(product(attended, out_weight))
    normed_two = low(normalize(hidden, norm_rows[2], norm_rows[3]))
    upward = low_back(product(normed_two, up_weight))
    activated = low(jax.nn.gelu(upward))
    return hidden + low_back(product(activated, down_weight))

def one_utterance(weights, first_input, shifts, length, codebook):
    qkv_weight, out_weight, up_weight, down_weight, tables = weights
    current = first_input
    outputs = []
    for layer_id in range(N_SECTION):
        is_nar = layer_id % 2 == 1
        row_index = codebook * (layer_id % 2)
        norm_rows = lax.dynamic_slice_in_dim(tables[layer_id], row_index * 4, 4, 0)
        layer_entry = low_back(low(current) + shifts[layer_id])
        current = decoder_layer(layer_entry, qkv_weight[layer_id], out_weight[layer_id], up_weight[layer_id], down_weight[layer_id], norm_rows, length, is_nar)
        outputs.append(low(current))
    return jnp.stack(outputs)

def reference(frames_in, cotangent, qkv_weight, out_weight, up_weight, down_weight, norm_table, lengths, codebooks):
    frames = PAD
    utterances = lengths.shape[0]
    features = frames_in.shape[1]
    weights = (qkv_weight.astype(jnp.float32), out_weight.astype(jnp.float32), up_weight.astype(jnp.float32), down_weight.astype(jnp.float32), norm_table.astype(jnp.float32))
    inputs_all = frames_in.astype(jnp.float32).reshape(utterances, frames, features)
    shifts = jnp.zeros((utterances, N_SECTION, frames, features), jnp.float32)
    checked = jax.checkpoint(one_utterance)

    def everything(weights, shifts):

        def scan_step(carried, utterance):
            first_input, shift_rows, length, codebook = utterance
            return (carried, checked(weights, first_input, shift_rows, length, codebook))
        return lax.scan(scan_step, jnp.zeros((), jnp.int32), (inputs_all, shifts, lengths, codebooks))[1]
    outputs, pullback = jax.vjp(everything, weights, shifts)
    live_rows = jnp.arange(frames, dtype=jnp.int32)[None, :] < lengths[:, None]
    last_grads = jnp.where(live_rows[:, :, None], cotangent.astype(jnp.float32).reshape(utterances, frames, features), 0.0)
    seed_grads = jnp.zeros_like(outputs).at[:, N_SECTION - 1].set(last_grads)
    weight_grads, shift_grads = pullback(seed_grads)
    layer_outputs = outputs.transpose(1, 0, 2, 3).reshape(N_SECTION, utterances * frames, features).astype(jnp.bfloat16)
    input_grads = shift_grads.transpose(1, 0, 2, 3).reshape(N_SECTION, utterances * frames, features).astype(jnp.bfloat16)
    return (layer_outputs, input_grads, weight_grads[0], weight_grads[1], weight_grads[2], weight_grads[3], weight_grads[4])
```

```python
import functools

import jax
import jax.numpy as jnp
from jax import lax
from jax.experimental import pallas as pl
from jax.experimental.pallas import tpu as pltpu
from jax.sharding import PartitionSpec as P

HEADS = 16
GROUP = 4
BLOCK = 512
SKEW = 2

epsilon = 1e-05
masked_score = -1e30
BF16 = jnp.bfloat16
F32 = jnp.float32

in_vmem = pl.BlockSpec(memory_space=pltpu.VMEM)
in_smem = pl.BlockSpec(memory_space=pltpu.SMEM)
anywhere = pl.BlockSpec(memory_space=pl.ANY)


def product(left, right):
    return lax.dot_general(left, right, (((1,), (0,)), ((), ())), preferred_element_type=F32)


def product_last(left, right):
    return lax.dot_general(left, right, (((1,), (1,)), ((), ())), preferred_element_type=F32)


def product_first(left, right):
    return lax.dot_general(left, right, (((0,), (0,)), ((), ())), preferred_element_type=F32)


def normalize(values):
    centre = values - jnp.mean(values, axis=-1, keepdims=True)
    reciprocal = lax.rsqrt(jnp.mean(centre * centre, axis=-1, keepdims=True) + epsilon)
    return centre * reciprocal, reciprocal


def normalize_back(gradient, normal_part, reciprocal, gain_row):
    scaled = gradient * (1.0 + gain_row)
    centred = scaled - jnp.mean(scaled, axis=-1, keepdims=True)
    return reciprocal * (
        centred - normal_part * jnp.mean(scaled * normal_part, axis=-1, keepdims=True)
    )


def gelu_and_slope(u):
    root = 0.7978845608028654
    square = u * u
    bent = jnp.tanh(root * u * (1.0 + 0.044715 * square))
    half = 0.5 * (1.0 + bent)
    slope = half + 0.5 * u * (1.0 - bent * bent) * (root * (1.0 + 3 * 0.044715 * square))
    return u * half, slope


def stacked_heads(block, head_size):
    owner = lax.broadcasted_iota(jnp.int32, block.shape, 1) // head_size
    zero = jnp.zeros_like(block)
    return jnp.concatenate([jnp.where(owner == h, block, zero) for h in range(GROUP)], axis=0)


def beside(stack, frames):
    return jnp.concatenate([stack[h * frames : (h + 1) * frames] for h in range(GROUP)], axis=1)


FWD_KEPT = (
    "layer_out", "entry", "normed_one", "packed", "probs", "attended", "hidden", "normed_two",
    "activated", "slope",
)
BWD_KEPT = ("grad_in", "grad_packed", "grad_attn", "grad_up", "grad_y", "row_grads")
WEIGHTS = ("qkv", "out", "up", "down")


def shapes_of(micros, frames, features, hidden):
    return {
        "layer_out": ((micros, frames, features), BF16),
        "entry": ((micros, frames, features), BF16),
        "normed_one": ((micros, frames, features), BF16),
        "packed": ((micros, frames, 3 * features), BF16),
        "probs": ((micros, HEADS * frames, frames), BF16),
        "attended": ((micros, frames, features), BF16),
        "hidden": ((micros, frames, features), F32),
        "normed_two": ((micros, frames, features), BF16),
        "activated": ((micros, frames, hidden), BF16),
        "slope": ((micros, frames, hidden), BF16),
        "grad_in": ((micros, frames, features), BF16),
        "grad_packed": ((micros, frames, 3 * features), BF16),
        "grad_attn": ((micros, frames, features), BF16),
        "grad_up": ((micros, frames, hidden), BF16),
        "grad_y": ((micros, frames, features), BF16),
        "row_grads": ((micros, 4, features), F32),
    }


def tick_kernel(names_in, names_out, names_scratch, moment, first, has_fwd, has_bwd, *refs):
    n_in, n_out = len(names_in), len(names_out)
    ins = dict(zip(names_in, refs[:n_in]))
    outs = dict(zip(names_out, refs[n_in : n_in + n_out]))
    scr = dict(zip(names_scratch, refs[n_in + n_out :]))
    sems = scr["sems"]
    flag = ins["flags"]
    frames, features = scr["entry"].shape
    hidden_units = scr["slope"].shape[1]
    head_size = features // HEADS
    inv_root = head_size ** (-0.5)
    group_width = GROUP * head_size

    def kept(name):
        return outs[name] if name in outs else ins[name]

    table = outs["table"] if first else ins["table"]
    weight = {w: (outs[w] if first else ins[w]) for w in WEIGHTS} if has_fwd else {}
    turned = {w: outs.get("t_" + w) for w in WEIGHTS}
    back_weight = {w: ins.get("t_" + w) for w in WEIGHTS}

    fwd_on, fwd_slot, fwd_len, fwd_row = (flag[moment, i] for i in range(4))
    bwd_on, bwd_slot, bwd_len, bwd_row = (flag[moment, 4 + i] for i in range(4))
    is_nar, at_start, at_end, piece = (flag[moment, 8 + i] for i in range(4))

    loads = {}
    if first:
        for i, w in enumerate(WEIGHTS + ("table",)):
            loads[w] = pltpu.make_async_copy(ins["given_" + w], outs[w], sems.at[i])
    started = 0
    if first:
        for w in ("table",) + WEIGHTS:
            loads[w].start()
        started = len(loads)

    def ready(w):
        if first:
            loads[w].wait()

    if has_fwd:

        @pl.when(fwd_on == 1)
        def forward():
            pending = []

            def save(name):
                copy = pltpu.make_async_copy(
                    scr[name], kept(name).at[fwd_slot], sems.at[started + len(pending)]
                )
                copy.start()
                pending.append(copy)

            @pl.when(at_start == 1)
            def own_input():
                pltpu.sync_copy(ins["frames_in"].at[fwd_slot], scr["entry"])

            @pl.when(at_start == 0)
            def passed_input():
                scr["entry"][...] = ins["incoming"][...]

            save("entry")
            ready("table")
            rows = table[fwd_row]
            residual = scr["entry"][...].astype(F32)
            normal_one, _ = normalize(residual)
            scr["normed_one"][...] = (normal_one * (1.0 + rows[0:1]) + rows[1:2]).astype(BF16)
            save("normed_one")
            ready("qkv")
            for j in range(0, 3 * features, BLOCK):
                scr["packed"][:, j : j + BLOCK] = product(
                    scr["normed_one"][...], weight["qkv"][:, j : j + BLOCK]
                ).astype(BF16)
            save("packed")
            tall = (GROUP * frames, frames)
            query_ids = lax.rem(lax.broadcasted_iota(jnp.int32, tall, 0), frames)
            key_ids = lax.broadcasted_iota(jnp.int32, tall, 1)
            allowed = (key_ids < fwd_len) & (key_ids <= query_ids + is_nar * frames)
            for g in range(HEADS // GROUP):
                lo, hi = g * group_width, (g + 1) * group_width
                queries = stacked_heads(scr["packed"][:, lo:hi], head_size)
                keys = scr["packed"][:, features + lo : features + hi]
                values = stacked_heads(
                    scr["packed"][:, 2 * features + lo : 2 * features + hi], head_size
                )
                scores = jnp.where(allowed, product_last(queries, keys) * inv_root, masked_score)
                exp_scores = jnp.exp(scores - jnp.max(scores, axis=-1, keepdims=True))
                total = jnp.sum(exp_scores, axis=-1, keepdims=True)
                probs = (exp_scores / total).astype(BF16)
                scr["probs"][g * GROUP * frames : (g + 1) * GROUP * frames, :] = probs
                scr["attended"][:, lo:hi] = product(beside(probs, frames), values).astype(BF16)
            save("probs")
            save("attended")
            ready("out")
            for j in range(0, features, BLOCK):
                scr["hidden"][:, j : j + BLOCK] = residual[:, j : j + BLOCK] + product(
                    scr["attended"][...], weight["out"][:, j : j + BLOCK]
                )
            save("hidden")
            normal_two, _ = normalize(scr["hidden"][...])
            scr["normed_two"][...] = (normal_two * (1.0 + rows[2:3]) + rows[3:4]).astype(BF16)
            save("normed_two")
            ready("up")
            for j in range(0, hidden_units, BLOCK):
                act, slope = gelu_and_slope(
                    product(scr["normed_two"][...], weight["up"][:, j : j + BLOCK])
                )
                scr["activated"][:, j : j + BLOCK] = act.astype(BF16)
                scr["slope"][:, j : j + BLOCK] = slope.astype(BF16)
            save("activated")
            save("slope")
            ready("down")
            for j in range(0, features, BLOCK):
                outs["outgoing"][:, j : j + BLOCK] = (
                    scr["hidden"][:, j : j + BLOCK]
                    + product(scr["activated"][...], weight["down"][:, j : j + BLOCK])
                ).astype(BF16)
            last = pltpu.make_async_copy(
                outs["outgoing"], kept("layer_out").at[fwd_slot], sems.at[started + len(pending)]
            )
            last.start()
            pending.append(last)
            for copy in pending:
                copy.wait()

        @pl.when(fwd_on == 0)
        def turn_weights():
            for w in WEIGHTS + ("table",):
                ready(w)
            side = 256
            ones = (
                lax.broadcasted_iota(jnp.int32, (side, side), 0)
                == lax.broadcasted_iota(jnp.int32, (side, side), 1)
            ).astype(BF16)

            def turn(source, target, row0, col0):
                def strip(i):
                    r = pl.multiple_of(row0 + i * side, side)
                    return pltpu.make_async_copy(
                        scr["strips"].at[i],
                        target.at[pl.ds(col0, features), pl.ds(r, side)],
                        sems.at[started + i],
                    )

                def one_strip(i, carry):
                    r = pl.multiple_of(row0 + i * side, side)
                    for c in range(0, features, side):
                        scr["strips"][i, c : c + side, :] = product_last(
                            ones, source[pl.ds(r, side), col0 + c : col0 + c + side]
                        ).astype(BF16)
                    strip(i).start()
                    return carry

                lax.fori_loop(0, features // side, one_strip, 0)
                for i in range(features // side):
                    strip(i).wait()

            units = []
            for w in WEIGHTS:
                total_rows, total_cols = weight[w].shape
                for r in range(0, total_rows, features):
                    for c in range(0, total_cols, features):
                        units.append((w, r, c))
            pieces = SKEW * 2
            for k in range(pieces):

                @pl.when(piece == k)
                def one_piece(k=k):
                    for w, r, c in units[k::pieces]:
                        turn(weight[w], turned[w], r, c)

    if has_bwd:

        @pl.when(bwd_on == 1)
        def backward():
            base = started
            fetches = {}
            for name in ("slope", "hidden", "packed", "probs", "entry"):
                fetches[name] = pltpu.make_async_copy(
                    kept(name).at[bwd_slot], scr[name], sems.at[base + len(fetches)]
                )
            fetch_needed = fwd_on == 0 if has_fwd else bwd_on == 1

            @pl.when(fetch_needed)
            def fetch():
                for copy in fetches.values():
                    copy.start()

            def fetched(name):
                @pl.when(fetch_needed)
                def arrived():
                    fetches[name].wait()

            pending = []

            def save(name):
                copy = pltpu.make_async_copy(
                    scr[name],
                    kept(name).at[bwd_slot],
                    sems.at[base + len(fetches) + len(pending)],
                )
                copy.start()
                pending.append(copy)

            @pl.when(at_end == 1)
            def own_cotangent():
                pltpu.sync_copy(ins["cotangent"].at[bwd_slot], scr["grad_y"])
                live = lax.broadcasted_iota(jnp.int32, (frames, features), 0) < bwd_len
                scr["grad_y"][...] = jnp.where(
                    live, scr["grad_y"][...], jnp.zeros((frames, features), BF16)
                )

            @pl.when(at_end == 0)
            def passed_gradient():
                scr["grad_y"][...] = ins["arriving"][...]

            save("grad_y")
            rows = table[bwd_row]
            fetched("slope")
            for j in range(0, hidden_units, BLOCK):
                grad_act = product(scr["grad_y"][...], back_weight["down"][:, j : j + BLOCK])
                scr["grad_up"][:, j : j + BLOCK] = (
                    grad_act * scr["slope"][:, j : j + BLOCK].astype(F32)
                ).astype(BF16)
            save("grad_up")
            for j in range(0, features, BLOCK):
                scr["wide"][:, j : j + BLOCK] = product(
                    scr["grad_up"][...], back_weight["up"][:, j : j + BLOCK]
                )
            fetched("hidden")
            normal_two, recip_two = normalize(scr["hidden"][...])
            grad_two = scr["wide"][...]
            scr["row_grads"][2:3, :] = jnp.sum(grad_two * normal_two, axis=0, keepdims=True)
            scr["row_grads"][3:4, :] = jnp.sum(grad_two, axis=0, keepdims=True)
            grad_hidden = scr["grad_y"][...].astype(F32) + normalize_back(
                grad_two, normal_two, recip_two, rows[2:3]
            )
            scr["grad_hidden"][...] = grad_hidden
            scr["grad_attn"][...] = grad_hidden.astype(BF16)
            save("grad_attn")
            for j in range(0, features, BLOCK):
                scr["mixed"][:, j : j + BLOCK] = product(
                    scr["grad_attn"][...], back_weight["out"][:, j : j + BLOCK]
                ).astype(BF16)
            fetched("packed")
            fetched("probs")
            for g in range(HEADS // GROUP):
                lo, hi = g * group_width, (g + 1) * group_width
                queries = stacked_heads(scr["packed"][:, lo:hi], head_size)
                keys = stacked_heads(scr["packed"][:, features + lo : features + hi], head_size)
                values = scr["packed"][:, 2 * features + lo : 2 * features + hi]
                mixed = stacked_heads(scr["mixed"][:, lo:hi], head_size)
                probs = scr["probs"][g * GROUP * frames : (g + 1) * GROUP * frames, :]
                wide_probs = probs.astype(F32)
                grad_probs = product_last(mixed, values)
                inner = jnp.sum(wide_probs * grad_probs, axis=-1, keepdims=True)
                grad_scores = (wide_probs * (grad_probs - inner)).astype(BF16)
                scr["grad_packed"][:, lo:hi] = (
                    product(beside(grad_scores, frames), keys) * inv_root
                ).astype(BF16)
                scr["grad_packed"][:, features + lo : features + hi] = (
                    product_first(grad_scores, queries) * inv_root
                ).astype(BF16)
                scr["grad_packed"][:, 2 * features + lo : 2 * features + hi] = product_first(
                    probs, mixed
                ).astype(BF16)
            save("grad_packed")
            for j in range(0, features, BLOCK):
                scr["wide"][:, j : j + BLOCK] = product(
                    scr["grad_packed"][...], back_weight["qkv"][:, j : j + BLOCK]
                )
            fetched("entry")
            normal_one, recip_one = normalize(scr["entry"][...].astype(F32))
            grad_one = scr["wide"][...]
            scr["row_grads"][0:1, :] = jnp.sum(grad_one * normal_one, axis=0, keepdims=True)
            scr["row_grads"][1:2, :] = jnp.sum(grad_one, axis=0, keepdims=True)
            save("row_grads")
            outs["returning"][...] = (
                scr["grad_hidden"][...]
                + normalize_back(grad_one, normal_one, recip_one, rows[0:1])
            ).astype(BF16)
            last = pltpu.make_async_copy(
                outs["returning"],
                kept("grad_in").at[bwd_slot],
                sems.at[base + len(fetches) + len(pending)],
            )
            last.start()
            pending.append(last)
            for copy in pending:
                copy.wait()


def run_tick(moment, state, flags, incoming, arriving, frames_in, cotangent, given, sizes,
             has_fwd, has_bwd):
    micros, frames, features, hidden_units = sizes
    shapes = shapes_of(*sizes)
    first = "qkv" not in state
    vmem = lambda x: pltpu.with_memory_space_constraint(x, pltpu.VMEM)

    names_in, args, specs_in = [], [], []
    names_out, out_shape, specs_out, aliases = [], [], [], {}

    def take(name, value, spec):
        names_in.append(name)
        args.append(value)
        specs_in.append(spec)

    def give(name, shape, spec):
        names_out.append(name)
        out_shape.append(shape)
        specs_out.append(spec)

    take("flags", flags, in_smem)
    resident = {"table": given["table"].shape, **{w: given[w].shape for w in WEIGHTS}}
    if first:
        for w, value in given.items():
            take("given_" + w, value, anywhere)
        for w, shape in resident.items():
            give(w, pltpu.VMEM(shape, given[w].dtype), in_vmem)
        for w in WEIGHTS:
            give("t_" + w, pltpu.VMEM(given[w].shape[::-1], BF16), anywhere)
    else:
        for w in resident:
            if w == "table" or has_fwd:
                take(w, vmem(state[w]), in_vmem)
        for w in WEIGHTS:
            if not has_fwd:
                take("t_" + w, vmem(state["t_" + w]), in_vmem)
                continue
            aliases[len(args)] = len(names_out)
            take("t_" + w, vmem(state["t_" + w]), in_vmem if has_bwd else anywhere)
            give("t_" + w, pltpu.VMEM(given[w].shape[::-1], BF16), anywhere)
    if has_fwd:
        take("incoming", incoming, in_vmem)
        take("frames_in", frames_in, anywhere)
    if has_bwd:
        take("arriving", arriving, in_vmem)
        take("cotangent", cotangent, anywhere)

    def keep(name, written):
        shape, dtype = shapes[name]
        if name in state:
            take(name, pltpu.with_memory_space_constraint(state[name], pltpu.HBM), anywhere)
            if written:
                aliases[len(args) - 1] = len(names_out)
        if written:
            give(name, pltpu.HBM(shape, dtype), anywhere)

    read_back = ("entry", "packed", "probs", "hidden", "slope")
    for name in FWD_KEPT:
        if has_fwd or (has_bwd and name in read_back):
            keep(name, has_fwd)
    if has_bwd:
        for name in BWD_KEPT:
            keep(name, True)
    if has_fwd:
        give("outgoing", jax.ShapeDtypeStruct((frames, features), BF16), in_vmem)
    if has_bwd:
        give("returning", jax.ShapeDtypeStruct((frames, features), BF16), in_vmem)

    scratch = {name: shapes[name] for name in ("entry", "packed", "probs", "hidden", "slope")}
    if has_fwd:
        for name in ("normed_one", "attended", "normed_two", "activated"):
            scratch[name] = shapes[name]
        scratch["strips"] = ((0, features // 256, features, 256), BF16)
    if has_bwd:
        for name in ("grad_packed", "grad_attn", "grad_up", "grad_y", "row_grads"):
            scratch[name] = shapes[name]
        scratch["wide"] = scratch["grad_hidden"] = shapes["hidden"]
        scratch["mixed"] = shapes["entry"]
    names_scratch = list(scratch) + ["sems"]
    scratch_shapes = [pltpu.VMEM(shape[1:], dtype) for shape, dtype in scratch.values()]
    scratch_shapes.append(pltpu.SemaphoreType.DMA((24,)))

    weight_count = sum(given[w].size for w in WEIGHTS)
    results = pl.pallas_call(
        functools.partial(
            tick_kernel, names_in, names_out, names_scratch, moment, first, has_fwd, has_bwd
        ),
        out_shape=out_shape,
        in_specs=specs_in,
        out_specs=specs_out,
        scratch_shapes=scratch_shapes,
        input_output_aliases=aliases,
        compiler_params=pltpu.CompilerParams(vmem_limit_bytes=14 * 2**20),
        cost_estimate=pl.CostEstimate(
            flops=2 * frames * weight_count * (has_fwd + has_bwd),
            bytes_accessed=8 * 2**20,
            transcendentals=0,
        ),
        name="tick",
    )(*args)
    state = dict(state)
    for name, value in zip(names_out, results):
        state[name] = value
    return state


def per_device(
    frames_in, cotangent, qkv_weight, out_weight, up_weight, down_weight, norm_table, lengths,
    codebooks,
):
    sections = lax.axis_size("section")
    section = lax.axis_index("section")
    micros = lengths.shape[0]
    tokens, features = frames_in.shape
    frames = tokens // micros
    hidden_units = up_weight.shape[2]
    sizes = (micros, frames, features, hidden_units)
    is_nar = section % 2
    given = {
        "table": norm_table[0].reshape(-1, 4, features),
        "qkv": qkv_weight[0],
        "out": out_weight[0],
        "up": up_weight[0],
        "down": down_weight[0],
    }
    frames_all = frames_in.reshape(micros, frames, features)
    cot_all = cotangent.reshape(micros, frames, features)
    rows_used = codebooks * is_nar

    fwd_ticks = micros + SKEW * (sections - 1)
    bwd_start = SKEW * (sections - 1)
    ticks = fwd_ticks + bwd_start

    moments = jnp.arange(ticks, dtype=jnp.int32)
    fwd_id = moments - SKEW * section
    bwd_id = moments - bwd_start - SKEW * (sections - 1 - section)

    def choose(ids):
        on = (ids >= 0) & (ids < micros)
        slot = jnp.clip(ids, 0, micros - 1)
        return [on.astype(jnp.int32), slot, lengths[slot], rows_used[slot]]

    piece = jnp.where(fwd_id < 0, moments, moments - micros)
    same = lambda v: jnp.full((ticks,), v, jnp.int32)
    flags = jnp.stack(
        choose(fwd_id)
        + choose(bwd_id)
        + [
            same(is_nar),
            same(section == 0),
            same(section == sections - 1),
            piece.astype(jnp.int32),
        ],
        axis=1,
    )

    nothing = jnp.zeros((frames, features), BF16)
    incoming = [nothing] * (ticks + SKEW)
    arriving = [nothing] * (ticks + SKEW)
    state = {}
    for moment in range(ticks):
        has_fwd = moment < fwd_ticks
        has_bwd = moment >= bwd_start
        state = run_tick(
            moment, state, flags, incoming[moment], arriving[moment], frames_all, cot_all, given,
            sizes, has_fwd, has_bwd,
        )
        onward = [
            (s, s + 1) for s in range(sections - 1) if 0 <= moment - SKEW * s < micros
        ]
        if onward:
            incoming[moment + SKEW] = lax.ppermute(state["outgoing"], "section", onward)
        backward = [
            (s, s - 1)
            for s in range(1, sections)
            if 0 <= moment - bwd_start - SKEW * (sections - 1 - s) < micros
        ]
        if backward:
            arriving[moment + SKEW] = lax.ppermute(state["returning"], "section", backward)

    flat = lambda name: state[name].reshape(tokens, -1)
    chosen = lax.broadcasted_iota(jnp.int32, (norm_table.shape[1] // 4, micros), 0) == rows_used
    table_grad = jnp.sum(
        jnp.where(chosen[:, :, None, None], state["row_grads"][None], 0.0), axis=1
    ).reshape(norm_table.shape[1:])

    def summed(left, right, dimension):
        local = product_first(flat(left), flat(right)).astype(BF16)
        return lax.psum_scatter(
            local, "batch", scatter_dimension=dimension, tiled=True
        ).astype(F32)

    grad_down = summed("activated", "grad_y", 1)
    grad_up = summed("normed_two", "grad_up", 0)
    grad_out = summed("attended", "grad_attn", 0)
    grad_qkv = summed("normed_one", "grad_packed", 0)
    grad_norms = lax.psum_scatter(table_grad, "batch", scatter_dimension=1, tiled=True)
    return (
        state["layer_out"].reshape(1, tokens, features),
        state["grad_in"].reshape(1, tokens, features),
        grad_qkv[None],
        grad_out[None],
        grad_up[None],
        grad_down[None],
        grad_norms[None],
    )


def solution(mesh):
    in_specs = (
        P("batch", None),
        P("batch", None),
        P("section", None, None),
        P("section", None, None),
        P("section", None, None),
        P("section", None, None),
        P("section", None, None),
        P("batch"),
        P("batch"),
    )
    out_specs = (
        P("section", "batch", None),
        P("section", "batch", None),
        P("section", "batch", None),
        P("section", "batch", None),
        P("section", "batch", None),
        P("section", None, "batch"),
        P("section", None, "batch"),
    )
    return jax.shard_map(
        per_device, mesh=mesh, in_specs=in_specs, out_specs=out_specs, check_vma=False
    )
```

```python
import functools
from typing import Any, NamedTuple

import jax
import jax.numpy as jnp
from jax import lax
from jax.experimental import pallas as pl
from jax.experimental.pallas import tpu as pltpu
from jax.sharding import PartitionSpec as P

HEADS = 16
GROUP = 4
BLOCK = 512
LANES = 128
CORES = 2
LINE = 4

epsilon = 1e-05
masked_score = -1e30
BF16 = jnp.bfloat16
F32 = jnp.float32

in_vmem = pl.BlockSpec(memory_space=pltpu.VMEM)
in_smem = pl.BlockSpec(memory_space=pltpu.SMEM)
anywhere = pl.BlockSpec(memory_space=pl.ANY)


class Weights(NamedTuple):
    qkv: Any
    out: Any
    up: Any
    down: Any


class Reread(NamedTuple):
    entry: Any
    packed: Any
    probs: Any
    hidden: Any
    slope: Any


class Kept(NamedTuple):
    layer_out: Any
    left_keep: Any
    left_send: Any
    act_keep: Any
    act_send: Any


class Back(NamedTuple):
    grad_in: Any
    grad_y: Any
    grad_up: Any
    grad_attn: Any
    grad_packed: Any
    row_grads: Any


def product(left, right):
    return lax.dot_general(left, right, (((1,), (0,)), ((), ())), preferred_element_type=F32)


def product_last(left, right):
    return lax.dot_general(left, right, (((1,), (1,)), ((), ())), preferred_element_type=F32)


def product_first(left, right):
    return lax.dot_general(left, right, (((0,), (0,)), ((), ())), preferred_element_type=F32)


def normalize(values):
    centre = values - jnp.mean(values, axis=-1, keepdims=True)
    reciprocal = lax.rsqrt(jnp.mean(centre * centre, axis=-1, keepdims=True) + epsilon)
    return centre * reciprocal, reciprocal


def normalize_back(gradient, normal_part, reciprocal, gain_row):
    scaled = gradient * (1.0 + gain_row)
    centred = scaled - jnp.mean(scaled, axis=-1, keepdims=True)
    return reciprocal * (
        centred - normal_part * jnp.mean(scaled * normal_part, axis=-1, keepdims=True)
    )


def gelu_and_slope(u):
    root = 0.7978845608028654
    square = u * u
    bent = jnp.tanh(root * u * (1.0 + 0.044715 * square))
    half = 0.5 * (1.0 + bent)
    slope = half + 0.5 * u * (1.0 - bent * bent) * (root * (1.0 + 3 * 0.044715 * square))
    return u * half, slope


def stacked_heads(block, head_size):
    owner = lax.broadcasted_iota(jnp.int32, block.shape, 1) // head_size
    zero = jnp.zeros_like(block)
    return jnp.concatenate([jnp.where(owner == h, block, zero) for h in range(GROUP)], axis=0)


def beside(stack, frames):
    return jnp.concatenate([stack[h * frames : (h + 1) * frames] for h in range(GROUP)], axis=1)


def table_rows(table, code):
    pair = table[pl.ds(pl.multiple_of((code // 2) * 8, 8), 8), :]
    return jnp.where(code % 2 == 1, pair[4:8], pair[0:4])


class Saver:
    def __init__(self, sems, base):
        self.sems, self.base, self.pending = sems, base, []

    def __call__(self, source, target):
        copy = pltpu.make_async_copy(source, target, self.sems.at[self.base + len(self.pending)])
        copy.start()
        self.pending.append(copy)

    def wait(self):
        for copy in self.pending:
            copy.wait()


def turn(source, target, row0, col0, side_by, strips, sems, base):
    side = 256
    ones = (
        lax.broadcasted_iota(jnp.int32, (side, side), 0)
        == lax.broadcasted_iota(jnp.int32, (side, side), 1)
    ).astype(BF16)

    slots = strips.shape[0]
    count = side_by // side

    def strip(i):
        r = pl.multiple_of(row0 + i * side, side)
        return pltpu.make_async_copy(
            strips.at[i % slots],
            target.at[pl.ds(col0, side_by), pl.ds(r, side)],
            sems.at[base + i % slots],
        )

    def one_strip(i, carry):
        @pl.when(i >= slots)
        def slot_is_free():
            strip(i - slots).wait()

        r = pl.multiple_of(row0 + i * side, side)
        for c in range(0, side_by, side):
            strips[i % slots, c : c + side, :] = product_last(
                ones, source[pl.ds(r, side), col0 + c : col0 + c + side]
            ).astype(BF16)
        strip(i).start()
        return carry

    lax.fori_loop(0, count, one_strip, 0)
    for i in range(count - slots, count):
        strip(i).wait()


class Plan(NamedTuple):
    sections: int
    micros: int
    frames: int
    features: int
    hidden_units: int
    rows: int

    def fwd_ticks(self):
        return self.micros + self.sections - 1

    def ticks(self):
        return self.micros + 2 * (self.sections - 1)

    def fwd_id(self, tick, section):
        return tick - section

    def bwd_id(self, tick, section):
        return tick - 2 * (self.sections - 1) + section


def forward_kernel(plan, tick, has_incoming, loads_weights, *refs):
    refs = list(refs)
    take = lambda n: [refs.pop(0) for _ in range(n)]
    if loads_weights:
        lengths, codebooks, given_table = take(3)
        given = Weights(*take(4))
    else:
        info, table = take(2)
        weight = Weights(*take(4))
        take(4)
    incoming = take(1)[0] if has_incoming else None
    (frames_in,) = take(1)
    if loads_weights:
        info, table = take(2)
        weight = Weights(*take(4))
    else:
        take(len(Reread._fields) + len(Kept._fields))
    turned = Weights(*take(4))
    reread = Reread(*take(5))
    kept = Kept(*take(5))
    (outgoing,) = take(1)
    entry, packed, probs, hidden, slope, normed, left, attended, act, strips, sems = refs

    micros, frames, features, hidden_units, rows_kept = plan[1:]
    head_size = features // HEADS
    group_width = GROUP * head_size
    section = lax.axis_index("section")
    core = lax.axis_index("batch") % CORES
    is_nar = section % 2
    micro = plan.fwd_id(tick, section)
    active = (micro >= 0) & (micro < micros)
    slot = jnp.clip(micro, 0, micros - 1)

    loads = []
    if loads_weights:
        for i in range(micros):
            info[i] = lengths[i]
            info[micros + i] = codebooks[i]
        pairs = [(given_table, table)] + list(zip(given, weight))
        for i, (source, target) in enumerate(pairs):
            loads.append(pltpu.make_async_copy(source, target, sems.at[i]))
            loads[i].start()
    base = len(loads)

    def ready(i):
        if loads_weights:
            loads[i].wait()

    @pl.when(active)
    def forward():
        save = Saver(sems, base)
        length = info[slot]
        code = info[micros + slot] * is_nar

        def own_input():
            pltpu.sync_copy(frames_in.at[slot], entry)

        if has_incoming:
            pl.when(section == 0)(own_input)

            @pl.when(section != 0)
            def passed_input():
                entry[...] = incoming[...]

        else:
            own_input()

        save(entry, reread.entry.at[slot])
        share = features // CORES

        def share_columns(source, first):
            for b in range(features // rows_kept):
                at = first + (b // CORES) * rows_kept
                left[b % CORES, :, at : at + rows_kept] = source[
                    :, b * rows_kept : (b + 1) * rows_kept
                ]

        ready(0)
        rows = table_rows(table, code)
        residual = entry[...].astype(F32)
        normal_one, _ = normalize(residual)
        normed[...] = (normal_one * (1.0 + rows[0:1]) + rows[1:2]).astype(BF16)
        share_columns(normed, 0)
        ready(1)
        for j in range(0, 3 * features, BLOCK):
            packed[:, j : j + BLOCK] = product(normed[...], weight.qkv[:, j : j + BLOCK]).astype(
                BF16
            )
        save(packed, reread.packed.at[slot])
        tall = (GROUP * frames, frames)
        query_ids = lax.rem(lax.broadcasted_iota(jnp.int32, tall, 0), frames)
        key_ids = lax.broadcasted_iota(jnp.int32, tall, 1)
        allowed = (key_ids < length) & (key_ids <= query_ids + is_nar * frames)
        inv_root = head_size ** (-0.5)
        for g in range(HEADS // GROUP):
            lo, hi = g * group_width, (g + 1) * group_width
            queries = stacked_heads(packed[:, lo:hi], head_size)
            keys = packed[:, features + lo : features + hi]
            values = stacked_heads(packed[:, 2 * features + lo : 2 * features + hi], head_size)
            scores = jnp.where(allowed, product_last(queries, keys) * inv_root, masked_score)
            exp_scores = jnp.exp(scores - jnp.max(scores, axis=-1, keepdims=True))
            total = jnp.sum(exp_scores, axis=-1, keepdims=True)
            group_probs = (exp_scores / total).astype(BF16)
            probs[g * GROUP * frames : (g + 1) * GROUP * frames, :] = group_probs
            attended[:, lo:hi] = product(beside(group_probs, frames), values).astype(BF16)
        save(probs, reread.probs.at[slot])
        share_columns(attended, share)
        ready(2)
        for j in range(0, features, BLOCK):
            hidden[:, j : j + BLOCK] = residual[:, j : j + BLOCK] + product(
                attended[...], weight.out[:, j : j + BLOCK]
            )
        save(hidden, reread.hidden.at[slot])
        normal_two, _ = normalize(hidden[...])
        normed[...] = (normal_two * (1.0 + rows[2:3]) + rows[3:4]).astype(BF16)
        share_columns(normed, 2 * share)
        save(left.at[core], kept.left_keep.at[slot])
        save(left.at[1 - core], kept.left_send.at[slot])
        ready(3)
        half = hidden_units // CORES
        for j in range(0, hidden_units, BLOCK):
            value, gradient = gelu_and_slope(product(normed[...], weight.up[:, j : j + BLOCK]))
            act[j // half, :, j % half : j % half + BLOCK] = value.astype(BF16)
            slope[:, j : j + BLOCK] = gradient.astype(BF16)
        save(slope, reread.slope.at[slot])
        save(act.at[core], kept.act_keep.at[slot])
        save(act.at[1 - core], kept.act_send.at[slot])
        ready(4)
        for j in range(0, features, BLOCK):
            added = hidden[:, j : j + BLOCK]
            for c in range(CORES):
                added += product(act[c], weight.down[c * half : (c + 1) * half, j : j + BLOCK])
            outgoing[:, j : j + BLOCK] = added.astype(BF16)
        save(outgoing, kept.layer_out.at[slot])
        save.wait()

    units = []
    for source, target in zip(weight, turned):
        total_rows, total_cols = source.shape
        for r in range(0, total_rows, features):
            for c in range(0, total_cols, features):
                units.append((source, target, r, c))
    pieces = 2
    piece = jnp.where(micro < 0, tick, micro - micros + section)

    @pl.when(jnp.logical_not(active))
    def wait_for_weights():
        for i in range(base):
            ready(i)

    for k in range(pieces):

        @pl.when(jnp.logical_not(active) & (piece == k))
        def one_piece(k=k):
            for source, target, r, c in units[k::pieces]:
                turn(source, target, r, c, features, strips, sems, base)


def backward_kernel(plan, tick, has_arriving, first, *refs):
    refs = list(refs)
    take = lambda n: [refs.pop(0) for _ in range(n)]
    info, table = take(2)
    turned = Weights(*take(4))
    take(4)
    arriving = take(1)[0] if has_arriving else None
    (cotangent,) = take(1)
    take(len(Reread._fields))
    if not first:
        take(len(Back._fields))
    reread = Reread(*take(5))
    back = Back(*take(6))
    (returning,) = take(1)
    (entry, packed, probs, hidden, slope, grad_y, grad_up, wide, grad_hidden, grad_attn, mixed,
     grad_packed, row_grads, sems) = refs

    micros, frames, features, hidden_units, _ = plan[1:]
    head_size = features // HEADS
    group_width = GROUP * head_size
    section = lax.axis_index("section")
    is_nar = section % 2
    micro = plan.bwd_id(tick, section)
    active = (micro >= 0) & (micro < micros)
    slot = jnp.clip(micro, 0, micros - 1)

    @pl.when(active)
    def backward():
        length = info[slot]
        code = info[micros + slot] * is_nar
        fetches = []
        for i, target in enumerate((entry, packed, probs, hidden, slope)):
            fetches.append(pltpu.make_async_copy(reread[i].at[slot], target, sems.at[i]))
        for i in (4, 3, 1, 2, 0):
            fetches[i].start()
        save = Saver(sems, len(fetches))

        def own_cotangent():
            pltpu.sync_copy(cotangent.at[slot], grad_y)
            live = lax.broadcasted_iota(jnp.int32, (frames, features), 0) < length
            grad_y[...] = jnp.where(live, grad_y[...], jnp.zeros((frames, features), BF16))

        if has_arriving:
            pl.when(section == plan.sections - 1)(own_cotangent)

            @pl.when(section != plan.sections - 1)
            def passed_gradient():
                grad_y[...] = arriving[...]

        else:
            own_cotangent()

        save(grad_y, back.grad_y.at[slot])
        rows = table_rows(table, code)
        fetches[4].wait()
        for j in range(0, hidden_units, BLOCK):
            grad_act = product(grad_y[...], turned.down[:, j : j + BLOCK])
            grad_up[:, j : j + BLOCK] = (
                grad_act * slope[:, j : j + BLOCK].astype(F32)
            ).astype(BF16)
        save(grad_up, back.grad_up.at[slot])
        for j in range(0, features, BLOCK):
            wide[:, j : j + BLOCK] = product(grad_up[...], turned.up[:, j : j + BLOCK])
        fetches[3].wait()
        normal_two, recip_two = normalize(hidden[...])
        grad_two = wide[...]
        row_grads[2:3, :] = jnp.sum(grad_two * normal_two, axis=0, keepdims=True)
        row_grads[3:4, :] = jnp.sum(grad_two, axis=0, keepdims=True)
        grad_hidden[...] = grad_y[...].astype(F32) + normalize_back(
            grad_two, normal_two, recip_two, rows[2:3]
        )
        grad_attn[...] = grad_hidden[...].astype(BF16)
        save(grad_attn, back.grad_attn.at[slot])
        for j in range(0, features, BLOCK):
            mixed[:, j : j + BLOCK] = product(
                grad_attn[...], turned.out[:, j : j + BLOCK]
            ).astype(BF16)
        fetches[1].wait()
        fetches[2].wait()
        inv_root = head_size ** (-0.5)
        for g in range(HEADS // GROUP):
            lo, hi = g * group_width, (g + 1) * group_width
            queries = stacked_heads(packed[:, lo:hi], head_size)
            keys = stacked_heads(packed[:, features + lo : features + hi], head_size)
            values = packed[:, 2 * features + lo : 2 * features + hi]
            group_mixed = stacked_heads(mixed[:, lo:hi], head_size)
            group_probs = probs[g * GROUP * frames : (g + 1) * GROUP * frames, :]
            wide_probs = group_probs.astype(F32)
            grad_probs = product_last(group_mixed, values)
            inner = jnp.sum(wide_probs * grad_probs, axis=-1, keepdims=True)
            grad_scores = (wide_probs * (grad_probs - inner)).astype(BF16)
            grad_packed[:, lo:hi] = (
                product(beside(grad_scores, frames), keys) * inv_root
            ).astype(BF16)
            grad_packed[:, features + lo : features + hi] = (
                product_first(grad_scores, queries) * inv_root
            ).astype(BF16)
            grad_packed[:, 2 * features + lo : 2 * features + hi] = product_first(
                group_probs, group_mixed
            ).astype(BF16)
        save(grad_packed, back.grad_packed.at[slot])
        for j in range(0, features, BLOCK):
            wide[:, j : j + BLOCK] = product(grad_packed[...], turned.qkv[:, j : j + BLOCK])
        fetches[0].wait()
        normal_one, recip_one = normalize(entry[...].astype(F32))
        grad_one = wide[...]
        row_grads[0:1, :] = jnp.sum(grad_one * normal_one, axis=0, keepdims=True)
        row_grads[1:2, :] = jnp.sum(grad_one, axis=0, keepdims=True)
        save(row_grads, back.row_grads.at[slot])
        returning[...] = (
            grad_hidden[...] + normalize_back(grad_one, normal_one, recip_one, rows[0:1])
        ).astype(BF16)
        save(returning, back.grad_in.at[slot])
        save.wait()


def shapes_of(plan):
    micros, frames, features, hidden_units, _ = plan[1:]
    own = (micros, frames)
    reread = Reread(
        entry=(own + (features,), BF16),
        packed=(own + (3 * features,), BF16),
        probs=((micros, HEADS * frames, frames), BF16),
        hidden=(own + (features,), F32),
        slope=(own + (hidden_units,), BF16),
    )
    share = (own + (3 * features // CORES,), BF16)
    half = (own + (hidden_units // CORES,), BF16)
    kept = Kept((own + (features,), BF16), share, share, half, half)
    wide = (own + (features,), BF16)
    back = Back(
        grad_in=wide,
        grad_y=wide,
        grad_up=(own + (hidden_units,), BF16),
        grad_attn=wide,
        grad_packed=(own + (3 * features,), BF16),
        row_grads=((micros, 4, features), F32),
    )
    return reread, kept, back


def scratch_of(shapes):
    return [pltpu.VMEM(shape[1:], dtype) for shape, dtype in shapes]


class Call:
    def __init__(self):
        self.args, self.in_specs, self.out_shape, self.out_specs = [], [], [], []
        self.aliases = {}

    def take(self, values, spec, space=None):
        for value in values:
            if space is not None:
                value = pltpu.with_memory_space_constraint(value, space)
            self.args.append(value)
            self.in_specs.append(spec)

    def give(self, shapes, spec, space, updates=None):
        for i, (shape, dtype) in enumerate(shapes):
            if updates is not None:
                self.aliases[updates + i] = len(self.out_shape)
            self.out_shape.append(space(shape, dtype))
            self.out_specs.append(spec)

    def run(self, body, scratch, flops):
        return list(
            pl.pallas_call(
                body,
                out_shape=self.out_shape,
                in_specs=self.in_specs,
                out_specs=self.out_specs,
                scratch_shapes=scratch,
                input_output_aliases=self.aliases,
                compiler_params=pltpu.CompilerParams(vmem_limit_bytes=10 * 2**20),
                cost_estimate=pl.CostEstimate(
                    flops=flops, bytes_accessed=2**22, transcendentals=0
                ),
            )(*self.args)
        )


def like(arrays):
    return [(x.shape, x.dtype) for x in arrays]


class State(NamedTuple):
    numbers: Any
    info: Any
    table: Any
    weights: Any
    turned: Any = None
    reread: Any = None
    kept: Any = None
    back: Any = None


def run_forward(plan, tick, state, incoming, frames_in):
    reread_shapes, kept_shapes, _ = shapes_of(plan)
    first = state.turned is None
    at_turned = at_kept = None
    call = Call()
    if first:
        call.take(state.numbers, in_smem)
        call.take([state.table], anywhere)
        call.take(state.weights, anywhere)
    else:
        call.take([state.info], in_smem, pltpu.SMEM)
        call.take([state.table], in_vmem, pltpu.VMEM)
        call.take(state.weights, in_vmem, pltpu.VMEM)
        at_turned = len(call.args)
        call.take(state.turned, anywhere, pltpu.VMEM)
    if incoming is not None:
        call.take([incoming], in_vmem, pltpu.VMEM)
    call.take([frames_in], anywhere)
    if first:
        call.give([((2 * plan.micros,), jnp.int32)], in_smem, pltpu.SMEM)
        call.give(like([state.table]), in_vmem, pltpu.VMEM)
        call.give(like(state.weights), in_vmem, pltpu.VMEM)
    else:
        at_kept = len(call.args)
        call.take(state.reread + state.kept, anywhere, pltpu.HBM)
    call.give([(w.shape[::-1], BF16) for w in state.weights], anywhere, pltpu.VMEM, at_turned)
    call.give(reread_shapes + kept_shapes, anywhere, pltpu.HBM, at_kept)
    call.give([((plan.frames, plan.features), BF16)], in_vmem, pltpu.VMEM)
    scratch = scratch_of(reread_shapes) + [
        pltpu.VMEM((plan.frames, plan.features), BF16),
        pltpu.VMEM((CORES, plan.frames, 3 * plan.features // CORES), BF16),
        pltpu.VMEM((plan.frames, plan.features), BF16),
        pltpu.VMEM((CORES, plan.frames, plan.hidden_units // CORES), BF16),
        pltpu.VMEM((2, plan.features, 256), BF16),
        pltpu.SemaphoreType.DMA((24,)),
    ]
    flops = 2 * plan.frames * sum(w.size for w in state.weights)
    body = functools.partial(forward_kernel, plan, tick, incoming is not None, first)
    got = call.run(body, scratch, flops)
    if first:
        state = state._replace(info=got[0], table=got[1], weights=Weights(*got[2:6]))
        got = got[6:]
    state = state._replace(
        turned=Weights(*got[:4]), reread=Reread(*got[4:9]), kept=Kept(*got[9:14])
    )
    return state, got[14]


def run_backward(plan, tick, state, arriving, cotangent):
    reread_shapes, _, back_shapes = shapes_of(plan)
    first = state.back is None
    call = Call()
    call.take([state.info], in_smem, pltpu.SMEM)
    call.take([state.table], in_vmem, pltpu.VMEM)
    call.take(state.turned, in_vmem, pltpu.VMEM)
    call.take(state.weights, anywhere, pltpu.VMEM)
    if arriving is not None:
        call.take([arriving], in_vmem, pltpu.VMEM)
    call.take([cotangent], anywhere)
    at_reread = len(call.args)
    call.take(state.reread, anywhere, pltpu.HBM)
    at_back = None
    if not first:
        at_back = len(call.args)
        call.take(state.back, anywhere, pltpu.HBM)
    call.give(reread_shapes, anywhere, pltpu.HBM, at_reread)
    call.give(back_shapes, anywhere, pltpu.HBM, at_back)
    call.give([((plan.frames, plan.features), BF16)], in_vmem, pltpu.VMEM)
    narrow = pltpu.VMEM((plan.frames, plan.features), BF16)
    full = pltpu.VMEM((plan.frames, plan.features), F32)
    scratch = scratch_of(reread_shapes) + [
        narrow,
        pltpu.VMEM((plan.frames, plan.hidden_units), BF16),
        full,
        full,
        narrow,
        narrow,
        pltpu.VMEM((plan.frames, 3 * plan.features), BF16),
        pltpu.VMEM((4, plan.features), F32),
        pltpu.SemaphoreType.DMA((16,)),
    ]
    flops = 2 * plan.frames * sum(w.size for w in state.turned)
    body = functools.partial(backward_kernel, plan, tick, arriving is not None, first)
    got = call.run(body, scratch, flops)
    return state._replace(reread=Reread(*got[:5]), back=Back(*got[5:11])), got[11]


def weight_grad_kernel(count, first_column, width, *refs):
    lefts, rights, out = refs[:count], refs[count : 2 * count], refs[2 * count]
    stage, turned, sems = refs[2 * count + 1 :]
    micros, frames, step = rights[0].shape

    @pl.when(pl.program_id(0) == 0)
    def turn_lefts():
        copies = []
        for i, left in enumerate(lefts):
            part = left.at[:, :, pl.ds(first_column, width)]
            copies.append(pltpu.make_async_copy(part, stage.at[i], sems.at[i]))
            copies[i].start()
        for i in range(count):
            copies[i].wait()
            for m in range(micros):
                turned[i, :, m * frames : (m + 1) * frames] = stage[i, m].T

    total = None
    for i in range(count):
        term = product(turned[i], rights[i][...].reshape(micros * frames, step))
        total = term if total is None else total + term
    out[...] = total.astype(BF16)


def weight_grad(lefts, rights, first_column, width):
    count = len(lefts)
    micros, frames, columns = rights[0].shape
    step = min(columns, BLOCK)
    return pl.pallas_call(
        functools.partial(weight_grad_kernel, count, first_column, width),
        grid=(columns // step,),
        out_shape=jax.ShapeDtypeStruct((width, columns), BF16),
        in_specs=[anywhere] * count
        + [pl.BlockSpec((micros, frames, step), lambda j: (0, 0, j))] * count,
        out_specs=pl.BlockSpec((width, step), lambda j: (0, j)),
        scratch_shapes=[
            pltpu.VMEM((count, micros, frames, width), BF16),
            pltpu.VMEM((count, width, micros * frames), BF16),
            pltpu.SemaphoreType.DMA((count,)),
        ],
        compiler_params=pltpu.CompilerParams(vmem_limit_bytes=12 * 2**20),
        cost_estimate=pl.CostEstimate(
            flops=2 * count * micros * frames * width * columns,
            bytes_accessed=2 * width * columns,
            transcendentals=0,
        ),
    )(*lefts, *rights)


def pick(parts, index):
    return lax.dynamic_index_in_dim(parts, index, 0, keepdims=False)


def line_sum(parts, chip, chips):
    def hop(value, sends, by):
        pairs = []
        for z in range(chips):
            if 0 <= z + by < chips and sends(z):
                pairs += [(CORES * z + c, CORES * (z + by) + c) for c in range(CORES)]
        return lax.ppermute(value, "batch", pairs)

    last = chips - 1
    up = pick(parts, jnp.minimum(chip + last, last))
    down = pick(parts, jnp.maximum(chip - last, 0))
    for k in range(1, chips):
        came_up = hop(up, lambda z: z < k, 1).astype(F32)
        came_down = hop(down, lambda z: z > last - k, -1).astype(F32)
        if k < last:
            here_up = pick(parts, jnp.minimum(chip + last - k, last)).astype(F32)
            here_down = pick(parts, jnp.maximum(chip - last + k, 0)).astype(F32)
            up = (here_up + came_up).astype(BF16)
            down = (here_down + came_down).astype(BF16)
    return pick(parts, chip).astype(F32) + came_up + came_down


def table_gradient(row_grads, codes, blocks):
    chosen = lax.broadcasted_iota(jnp.int32, (blocks, codes.shape[0]), 0) == codes
    return jnp.sum(jnp.where(chosen[:, :, None, None], row_grads[None], 0.0), axis=1)


def sums_by_hops(plan, kept, back, table_grad, batch, index):
    chips = batch // CORES
    core, chip = index % CORES, index // CORES
    features, hidden_units = plan.features, plan.hidden_units
    share = features // CORES
    rows = plan.rows
    swap = lambda x: lax.ppermute(x, "batch", [(b, b ^ 1) for b in range(batch)])

    left_peer = swap(kept.left_send)
    act_peer = swap(kept.act_send)
    y_peer = swap(back.grad_y)
    up_peer = swap(back.grad_up)
    attn_peer = swap(back.grad_attn)
    packed_peer = swap(back.grad_packed)

    lefts = [kept.left_keep, left_peer]
    down = weight_grad([back.grad_y, y_peer], [kept.act_keep, act_peer], 0, features)
    up = weight_grad(lefts, [back.grad_up, up_peer], 2 * share, share)
    out = weight_grad(lefts, [back.grad_attn, attn_peer], share, share)
    qkv = weight_grad(lefts, [back.grad_packed, packed_peer], 0, share)

    norms = table_grad.reshape(-1, chips, CORES, rows).transpose(2, 1, 0, 3)
    norms = pick(norms, core) + swap(pick(norms, 1 - core))

    down = line_sum(down.reshape(chips, CORES * rows, hidden_units // CORES), chip, chips)
    up = line_sum(up.reshape(chips, rows, hidden_units), chip, chips)
    qkv = line_sum(qkv.reshape(chips, rows, 3 * features), chip, chips)
    out = line_sum(out.reshape(chips, rows, features), chip, chips)
    norms = line_sum(norms, chip, chips)

    own_rows = lax.dynamic_slice_in_dim(down, core * rows, rows, 0)
    peer_rows = swap(lax.dynamic_slice_in_dim(down, (1 - core) * rows, rows, 0).astype(BF16))
    peer_rows = peer_rows.astype(F32)
    first = jnp.where(core == 0, own_rows, peer_rows)
    second = jnp.where(core == 0, peer_rows, own_rows)
    down = jnp.concatenate([first, second], axis=1).T
    return qkv, out, up, down, norms


def sums_by_scatter(plan, kept, back, table_grad, index):
    features = plan.features
    share = features // CORES
    core = index % CORES

    def local(right, column):
        mine = weight_grad([kept.left_keep], [right], column, share)
        other = weight_grad([kept.left_send], [right], column, share)
        even, odd = jnp.where(core == 0, mine, other), jnp.where(core == 0, other, mine)
        blocks = [x.reshape(-1, 1, plan.rows, x.shape[1]) for x in (even, odd)]
        return jnp.concatenate(blocks, axis=1).reshape(features, -1)

    def scattered(x, dimension):
        return lax.psum_scatter(
            x, "batch", scatter_dimension=dimension, tiled=True
        ).astype(F32)

    mine = weight_grad([back.grad_y], [kept.act_keep], 0, features)
    other = weight_grad([back.grad_y], [kept.act_send], 0, features)
    even, odd = jnp.where(core == 0, mine, other), jnp.where(core == 0, other, mine)
    down = jnp.concatenate([even, odd], axis=1)
    return (
        scattered(local(back.grad_packed, 0), 0),
        scattered(local(back.grad_attn, share), 0),
        scattered(local(back.grad_up, 2 * share), 0),
        scattered(down, 0).T,
        scattered(table_grad, 1),
    )


def per_device(
    frames_in, cotangent, qkv_weight, out_weight, up_weight, down_weight, norm_table, lengths,
    codebooks,
):
    sections = lax.axis_size("section")
    batch = lax.axis_size("batch")
    section = lax.axis_index("section")
    micros = lengths.shape[0]
    tokens, features = frames_in.shape
    frames = tokens // micros
    plan = Plan(
        sections, micros, frames, features, up_weight.shape[2], max(features // batch, LANES)
    )
    frames_all = frames_in.reshape(micros, frames, features)
    cot_all = cotangent.reshape(micros, frames, features)

    state = State(
        numbers=[lengths, codebooks],
        info=None,
        table=norm_table[0],
        weights=Weights(qkv_weight[0], out_weight[0], up_weight[0], down_weight[0]),
    )
    incoming = arriving = None
    working = lambda micro: 0 <= micro < micros
    for tick in range(plan.ticks()):
        sent = returned = None
        if tick < plan.fwd_ticks():
            state, output = run_forward(plan, tick, state, incoming, frames_all)
            onward = [
                (s, s + 1) for s in range(sections - 1) if working(plan.fwd_id(tick, s))
            ]
            if onward:
                sent = lax.ppermute(output, "section", onward)
        if tick >= sections - 1:
            state, output = run_backward(plan, tick, state, arriving, cot_all)
            backward = [
                (s, s - 1) for s in range(1, sections) if working(plan.bwd_id(tick, s))
            ]
            if backward:
                returned = lax.ppermute(output, "section", backward)
        incoming, arriving = sent, returned

    blocks = norm_table.shape[1] // 4
    codes = codebooks * (section % 2)
    table_grad = table_gradient(state.back.row_grads, codes, blocks).reshape(norm_table.shape[1:])
    index = lax.axis_index("batch")
    if batch % CORES == 0 and CORES < batch <= CORES * LINE:
        sums = sums_by_hops(plan, state.kept, state.back, table_grad, batch, index)
    else:
        sums = sums_by_scatter(plan, state.kept, state.back, table_grad, index)
    return (
        state.kept.layer_out.reshape(1, tokens, features),
        state.back.grad_in.reshape(1, tokens, features),
    ) + tuple(x[None] for x in sums)


def solution(mesh):
    section, batch = mesh.axis_names
    over_batch = P(batch)
    over_section = P(section)
    both = P(section, batch, None)
    columns = P(section, None, batch)
    in_specs = (over_batch,) * 2 + (over_section,) * 5 + (over_batch,) * 2
    out_specs = (both,) * 5 + (columns,) * 2
    return jax.shard_map(
        per_device, mesh=mesh, in_specs=in_specs, out_specs=out_specs, check_vma=False
    )
```

```python
import functools
from typing import Any, NamedTuple

import jax
import jax.numpy as jnp
from jax import lax
from jax.experimental import pallas as pl
from jax.experimental.pallas import tpu as pltpu
from jax.sharding import PartitionSpec as P

HEADS = 16
GROUP = 4
BLOCK = 512
LANES = 128
CORES = 2
LINE = 4

epsilon = 1e-05
masked_score = -1e30
BF16 = jnp.bfloat16
F32 = jnp.float32

in_vmem = pl.BlockSpec(memory_space=pltpu.VMEM)
in_smem = pl.BlockSpec(memory_space=pltpu.SMEM)
anywhere = pl.BlockSpec(memory_space=pl.ANY)


class Weights(NamedTuple):
    qkv: Any
    out: Any
    up: Any
    down: Any


class Reread(NamedTuple):
    entry: Any
    packed: Any
    probs: Any
    hidden: Any
    slope: Any


class Kept(NamedTuple):
    layer_out: Any
    left: Any
    act_early: Any
    act_late: Any


class Back(NamedTuple):
    grad_in: Any
    y_early: Any
    y_late: Any
    y_last: Any
    grad_up: Any
    grad_attn: Any
    grad_packed: Any
    row_grads: Any


def product(left, right):
    return lax.dot_general(left, right, (((1,), (0,)), ((), ())), preferred_element_type=F32)


def product_last(left, right):
    return lax.dot_general(left, right, (((1,), (1,)), ((), ())), preferred_element_type=F32)


def product_first(left, right):
    return lax.dot_general(left, right, (((0,), (0,)), ((), ())), preferred_element_type=F32)


def normalize(values):
    centre = values - jnp.mean(values, axis=-1, keepdims=True)
    reciprocal = lax.rsqrt(jnp.mean(centre * centre, axis=-1, keepdims=True) + epsilon)
    return centre * reciprocal, reciprocal


def normalize_back(gradient, normal_part, reciprocal, gain_row):
    scaled = gradient * (1.0 + gain_row)
    centred = scaled - jnp.mean(scaled, axis=-1, keepdims=True)
    return reciprocal * (
        centred - normal_part * jnp.mean(scaled * normal_part, axis=-1, keepdims=True)
    )


def gelu_and_slope(u):
    root = 0.7978845608028654
    square = u * u
    bent = jnp.tanh(root * u * (1.0 + 0.044715 * square))
    half = 0.5 * (1.0 + bent)
    slope = half + 0.5 * u * (1.0 - bent * bent) * (root * (1.0 + 3 * 0.044715 * square))
    return u * half, slope


def stacked_heads(block, head_size):
    owner = lax.broadcasted_iota(jnp.int32, block.shape, 1) // head_size
    zero = jnp.zeros_like(block)
    return jnp.concatenate([jnp.where(owner == h, block, zero) for h in range(GROUP)], axis=0)


def beside(stack, frames):
    return jnp.concatenate([stack[h * frames : (h + 1) * frames] for h in range(GROUP)], axis=1)


def table_rows(table, code):
    pair = table[pl.ds(pl.multiple_of((code // 2) * 8, 8), 8), :]
    return jnp.where(code % 2 == 1, pair[4:8], pair[0:4])


class Saver:
    def __init__(self, sems, base):
        self.sems, self.base, self.pending = sems, base, []

    def __call__(self, source, target):
        copy = pltpu.make_async_copy(source, target, self.sems.at[self.base + len(self.pending)])
        copy.start()
        self.pending.append(copy)

    def spread(self, source, buffers, spans, slot):
        sem = self.sems.at[self.base + len(self.pending)]
        copies = []
        for buffer, (first, end) in zip(buffers, spans):
            if buffer is None:
                continue
            place = jnp.clip(slot - first, 0, end - first - 1)
            copies.append(pltpu.make_async_copy(source, buffer.at[place], sem))
            pl.when((slot >= first) & (slot < end))(copies[-1].start)
        self.pending.append(copies[0])

    def wait(self):
        for copy in self.pending:
            copy.wait()


def turn(source, target, row0, col0, side_by, strips, sems, base):
    side = 256
    ones = (
        lax.broadcasted_iota(jnp.int32, (side, side), 0)
        == lax.broadcasted_iota(jnp.int32, (side, side), 1)
    ).astype(BF16)

    slots = strips.shape[0]
    count = side_by // side

    def strip(i):
        r = pl.multiple_of(row0 + i * side, side)
        return pltpu.make_async_copy(
            strips.at[i % slots],
            target.at[pl.ds(col0, side_by), pl.ds(r, side)],
            sems.at[base + i % slots],
        )

    def one_strip(i, carry):
        @pl.when(i >= slots)
        def slot_is_free():
            strip(i - slots).wait()

        r = pl.multiple_of(row0 + i * side, side)
        for c in range(0, side_by, side):
            strips[i % slots, c : c + side, :] = product_last(
                ones, source[pl.ds(r, side), col0 + c : col0 + c + side]
            ).astype(BF16)
        strip(i).start()
        return carry

    lax.fori_loop(0, count, one_strip, 0)
    for i in range(count - slots, count):
        strip(i).wait()


def split_columns(plan, core, source, target):
    width = plan.rows
    for b in range(plan.features // width):
        at = (b // CORES) * width
        which = jnp.where(core == b % CORES, 0, 1)
        target[which, :, at : at + width] = source[:, b * width : (b + 1) * width]


def last_y_kernel(plan, arriving, stored, _, y_last, sem):
    at_start = lax.axis_index("section") == 0

    @pl.when(at_start)
    def split():
        split_columns(plan, lax.axis_index("batch") % CORES, arriving, y_last.at[:, 0])

    @pl.when(jnp.logical_not(at_start))
    def fetch():
        copy = pltpu.make_async_copy(stored, y_last, sem)
        copy.start()
        copy.wait()


class Plan(NamedTuple):
    sections: int
    micros: int
    frames: int
    features: int
    hidden_units: int
    rows: int

    def fwd_ticks(self):
        return self.micros + self.sections - 1

    def ticks(self):
        return self.micros + 2 * (self.sections - 1)

    def act_spans(self):
        half = self.micros // 2
        return (0, half), (half, self.micros)

    def y_spans(self):
        half = self.micros // 2
        return (0, half), (half, self.micros - 1), (self.micros - 1, self.micros)

    def fwd_reaches(self, tick):
        low, high = tick - (self.sections - 1), tick
        return tuple(low < end and high >= first for first, end in self.act_spans())

    def bwd_reaches(self, tick):
        low, high = tick - 2 * (self.sections - 1), tick - (self.sections - 1)
        last = tick == self.ticks() - 1
        return tuple(low < end and high >= first and not last for first, end in self.y_spans())

    def fwd_id(self, tick, section):
        return tick - section

    def bwd_id(self, tick, section):
        return tick - 2 * (self.sections - 1) + section


def forward_kernel(plan, tick, has_incoming, loads_weights, *refs):
    refs = list(refs)
    take = lambda n: [refs.pop(0) for _ in range(n)]
    if loads_weights:
        lengths, codebooks, given_table = take(3)
        given = Weights(*take(4))
    else:
        info, table = take(2)
        weight = Weights(*take(4))
        take(4)
    incoming = take(1)[0] if has_incoming else None
    (frames_in,) = take(1)
    reaches = plan.fwd_reaches(tick)
    if loads_weights:
        info, table = take(2)
        weight = Weights(*take(4))
    else:
        take(len(Reread._fields) + 2)
        take(sum(now and had for now, had in zip(reaches, plan.fwd_reaches(tick - 1))))
    turned = Weights(*take(4))
    reread = Reread(*take(5))
    kept = Kept(*take(2), *[take(1)[0] if on else None for on in reaches])
    (outgoing,) = take(1)
    entry, packed, probs, hidden, slope, normed, left, attended, act, strips, sems = refs

    micros, frames, features, hidden_units, rows_kept = plan[1:]
    head_size = features // HEADS
    group_width = GROUP * head_size
    section = lax.axis_index("section")
    core = lax.axis_index("batch") % CORES
    is_nar = section % 2
    micro = plan.fwd_id(tick, section)
    active = (micro >= 0) & (micro < micros)
    slot = jnp.clip(micro, 0, micros - 1)

    loads = []
    if loads_weights:
        for i in range(micros):
            info[i] = lengths[i]
            info[micros + i] = codebooks[i]
        pairs = [(given_table, table)] + list(zip(given, weight))
        for i, (source, target) in enumerate(pairs):
            loads.append(pltpu.make_async_copy(source, target, sems.at[i]))
            loads[i].start()
    base = len(loads)

    def ready(i):
        if loads_weights:
            loads[i].wait()

    @pl.when(active)
    def forward():
        save = Saver(sems, base)
        length = info[slot]
        code = info[micros + slot] * is_nar

        def own_input():
            pltpu.sync_copy(frames_in.at[slot], entry)

        if has_incoming:
            pl.when(section == 0)(own_input)

            @pl.when(section != 0)
            def passed_input():
                entry[...] = incoming[...]

        else:
            own_input()

        save(entry, reread.entry.at[slot])
        share = features // CORES

        def share_columns(source, first):
            for b in range(features // rows_kept):
                at = first + (b // CORES) * rows_kept
                left[b % CORES, :, at : at + rows_kept] = source[
                    :, b * rows_kept : (b + 1) * rows_kept
                ]

        ready(0)
        rows = table_rows(table, code)
        residual = entry[...].astype(F32)
        normal_one, _ = normalize(residual)
        normed[...] = (normal_one * (1.0 + rows[0:1]) + rows[1:2]).astype(BF16)
        share_columns(normed, 0)
        ready(1)
        for j in range(0, 3 * features, BLOCK):
            packed[:, j : j + BLOCK] = product(normed[...], weight.qkv[:, j : j + BLOCK]).astype(
                BF16
            )
        save(packed, reread.packed.at[slot])
        tall = (GROUP * frames, frames)
        query_ids = lax.rem(lax.broadcasted_iota(jnp.int32, tall, 0), frames)
        key_ids = lax.broadcasted_iota(jnp.int32, tall, 1)
        allowed = (key_ids < length) & (key_ids <= query_ids + is_nar * frames)
        inv_root = head_size ** (-0.5)
        for g in range(HEADS // GROUP):
            lo, hi = g * group_width, (g + 1) * group_width
            queries = stacked_heads(packed[:, lo:hi], head_size)
            keys = packed[:, features + lo : features + hi]
            values = stacked_heads(packed[:, 2 * features + lo : 2 * features + hi], head_size)
            scores = jnp.where(allowed, product_last(queries, keys) * inv_root, masked_score)
            exp_scores = jnp.exp(scores - jnp.max(scores, axis=-1, keepdims=True))
            total = jnp.sum(exp_scores, axis=-1, keepdims=True)
            group_probs = (exp_scores / total).astype(BF16)
            probs[g * GROUP * frames : (g + 1) * GROUP * frames, :] = group_probs
            attended[:, lo:hi] = product(beside(group_probs, frames), values).astype(BF16)
        save(probs, reread.probs.at[slot])
        share_columns(attended, share)
        ready(2)
        for j in range(0, features, BLOCK):
            hidden[:, j : j + BLOCK] = residual[:, j : j + BLOCK] + product(
                attended[...], weight.out[:, j : j + BLOCK]
            )
        save(hidden, reread.hidden.at[slot])
        normal_two, _ = normalize(hidden[...])
        normed[...] = (normal_two * (1.0 + rows[2:3]) + rows[3:4]).astype(BF16)
        share_columns(normed, 2 * share)
        save(left.at[core], kept.left.at[0, slot])
        save(left.at[1 - core], kept.left.at[1, slot])
        ready(3)
        for j in range(0, hidden_units, BLOCK):
            value, gradient = gelu_and_slope(product(normed[...], weight.up[:, j : j + BLOCK]))
            act[:, j : j + BLOCK] = value.astype(BF16)
            slope[:, j : j + BLOCK] = gradient.astype(BF16)
        save(slope, reread.slope.at[slot])
        save.spread(act, (kept.act_early, kept.act_late), plan.act_spans(), slot)
        ready(4)
        for j in range(0, features, BLOCK):
            outgoing[:, j : j + BLOCK] = (
                hidden[:, j : j + BLOCK] + product(act[...], weight.down[:, j : j + BLOCK])
            ).astype(BF16)
        save(outgoing, kept.layer_out.at[slot])
        save.wait()

    units = []
    for source, target in zip(weight, turned):
        total_rows, total_cols = source.shape
        for r in range(0, total_rows, features):
            for c in range(0, total_cols, features):
                units.append((source, target, r, c))
    pieces = 2
    piece = jnp.where(micro < 0, tick, micro - micros + section)

    @pl.when(jnp.logical_not(active))
    def wait_for_weights():
        for i in range(base):
            ready(i)

    for k in range(pieces):

        @pl.when(jnp.logical_not(active) & (piece == k))
        def one_piece(k=k):
            for source, target, r, c in units[k::pieces]:
                turn(source, target, r, c, features, strips, sems, base)


def backward_kernel(plan, tick, has_arriving, first, unread, *refs):
    refs = list(refs)
    take = lambda n: [refs.pop(0) for _ in range(n)]
    info, table = take(2)
    turned = Weights(*take(4))
    take(unread)
    arriving = take(1)[0] if has_arriving else None
    (cotangent,) = take(1)
    take(len(Reread._fields))
    reaches = plan.bwd_reaches(tick)
    used = (True,) + reaches + (True,) * 4
    if not first:
        had = (True,) + plan.bwd_reaches(tick - 1) + (True,) * 4
        take(sum(u and h for u, h in zip(used, had)))
    reread = Reread(*take(5))
    back = Back(*[take(1)[0] if u else None for u in used])
    (returning,) = take(1)
    (entry, packed, probs, hidden, slope, grad_y, y_split, grad_up, wide, grad_hidden, grad_attn,
     mixed, grad_packed, row_grads, sems) = refs

    micros, frames, features, hidden_units, _ = plan[1:]
    head_size = features // HEADS
    group_width = GROUP * head_size
    section = lax.axis_index("section")
    core = lax.axis_index("batch") % CORES
    is_nar = section % 2
    micro = plan.bwd_id(tick, section)
    active = (micro >= 0) & (micro < micros)
    slot = jnp.clip(micro, 0, micros - 1)

    @pl.when(active)
    def backward():
        length = info[slot]
        code = info[micros + slot] * is_nar
        fetches = []
        for i, target in enumerate((entry, packed, probs, hidden, slope)):
            fetches.append(pltpu.make_async_copy(reread[i].at[slot], target, sems.at[i]))
        for i in (4, 3, 1, 2, 0):
            fetches[i].start()
        save = Saver(sems, len(fetches))

        def own_cotangent():
            pltpu.sync_copy(cotangent.at[slot], grad_y)
            live = lax.broadcasted_iota(jnp.int32, (frames, features), 0) < length
            grad_y[...] = jnp.where(live, grad_y[...], jnp.zeros((frames, features), BF16))

        if has_arriving:
            pl.when(section == plan.sections - 1)(own_cotangent)

            @pl.when(section != plan.sections - 1)
            def passed_gradient():
                grad_y[...] = arriving[...]

        else:
            own_cotangent()

        if any(reaches):
            split_columns(plan, core, grad_y, y_split)
            for c in range(CORES):
                places = [None if b is None else b.at[c] for b in back[1:4]]
                save.spread(y_split.at[c], places, plan.y_spans(), slot)
        rows = table_rows(table, code)
        fetches[4].wait()
        for j in range(0, hidden_units, BLOCK):
            grad_act = product(grad_y[...], turned.down[:, j : j + BLOCK])
            grad_up[:, j : j + BLOCK] = (
                grad_act * slope[:, j : j + BLOCK].astype(F32)
            ).astype(BF16)
        save(grad_up, back.grad_up.at[slot])
        for j in range(0, features, BLOCK):
            wide[:, j : j + BLOCK] = product(grad_up[...], turned.up[:, j : j + BLOCK])
        fetches[3].wait()
        normal_two, recip_two = normalize(hidden[...])
        grad_two = wide[...]
        row_grads[2:3, :] = jnp.sum(grad_two * normal_two, axis=0, keepdims=True)
        row_grads[3:4, :] = jnp.sum(grad_two, axis=0, keepdims=True)
        grad_hidden[...] = grad_y[...].astype(F32) + normalize_back(
            grad_two, normal_two, recip_two, rows[2:3]
        )
        grad_attn[...] = grad_hidden[...].astype(BF16)
        save(grad_attn, back.grad_attn.at[slot])
        for j in range(0, features, BLOCK):
            mixed[:, j : j + BLOCK] = product(
                grad_attn[...], turned.out[:, j : j + BLOCK]
            ).astype(BF16)
        fetches[1].wait()
        fetches[2].wait()
        inv_root = head_size ** (-0.5)
        for g in range(HEADS // GROUP):
            lo, hi = g * group_width, (g + 1) * group_width
            queries = stacked_heads(packed[:, lo:hi], head_size)
            keys = stacked_heads(packed[:, features + lo : features + hi], head_size)
            values = packed[:, 2 * features + lo : 2 * features + hi]
            group_mixed = stacked_heads(mixed[:, lo:hi], head_size)
            group_probs = probs[g * GROUP * frames : (g + 1) * GROUP * frames, :]
            wide_probs = group_probs.astype(F32)
            grad_probs = product_last(group_mixed, values)
            inner = jnp.sum(wide_probs * grad_probs, axis=-1, keepdims=True)
            grad_scores = (wide_probs * (grad_probs - inner)).astype(BF16)
            grad_packed[:, lo:hi] = (
                product(beside(grad_scores, frames), keys) * inv_root
            ).astype(BF16)
            grad_packed[:, features + lo : features + hi] = (
                product_first(grad_scores, queries) * inv_root
            ).astype(BF16)
            grad_packed[:, 2 * features + lo : 2 * features + hi] = product_first(
                group_probs, group_mixed
            ).astype(BF16)
        save(grad_packed, back.grad_packed.at[slot])
        for j in range(0, features, BLOCK):
            wide[:, j : j + BLOCK] = product(grad_packed[...], turned.qkv[:, j : j + BLOCK])
        fetches[0].wait()
        normal_one, recip_one = normalize(entry[...].astype(F32))
        grad_one = wide[...]
        row_grads[0:1, :] = jnp.sum(grad_one * normal_one, axis=0, keepdims=True)
        row_grads[1:2, :] = jnp.sum(grad_one, axis=0, keepdims=True)
        save(row_grads, back.row_grads.at[slot])
        returning[...] = (
            grad_hidden[...] + normalize_back(grad_one, normal_one, recip_one, rows[0:1])
        ).astype(BF16)
        save(returning, back.grad_in.at[slot])
        save.wait()


def shapes_of(plan):
    micros, frames, features, hidden_units, _ = plan[1:]
    own = (micros, frames)
    reread = Reread(
        entry=(own + (features,), BF16),
        packed=(own + (3 * features,), BF16),
        probs=((micros, HEADS * frames, frames), BF16),
        hidden=(own + (features,), F32),
        slope=(own + (hidden_units,), BF16),
    )
    def buffers(spans, before, columns):
        return [(before + (end - first, frames, columns), BF16) for first, end in spans]

    left = ((CORES,) + own + (3 * features // CORES,), BF16)
    kept = Kept((own + (features,), BF16), left, *buffers(plan.act_spans(), (), hidden_units))
    wide = (own + (features,), BF16)
    back = Back(
        wide,
        *buffers(plan.y_spans(), (CORES,), features // CORES),
        grad_up=(own + (hidden_units,), BF16),
        grad_attn=wide,
        grad_packed=(own + (3 * features,), BF16),
        row_grads=((micros, 4, features), F32),
    )
    return reread, kept, back


def scratch_of(shapes):
    return [pltpu.VMEM(shape[1:], dtype) for shape, dtype in shapes]


class Call:
    def __init__(self):
        self.args, self.in_specs, self.out_shape, self.out_specs = [], [], [], []
        self.aliases = {}

    def take(self, values, spec, space=None):
        for value in values:
            if space is not None:
                value = pltpu.with_memory_space_constraint(value, space)
            self.args.append(value)
            self.in_specs.append(spec)

    def give(self, shapes, spec, space, updates=None):
        for i, (shape, dtype) in enumerate(shapes):
            if updates is not None:
                self.aliases[updates + i] = len(self.out_shape)
            self.out_shape.append(space(shape, dtype))
            self.out_specs.append(spec)

    def update(self, arrays, shapes, used):
        arrays = arrays or (None,) * len(shapes)
        for array, shape, use in zip(arrays, shapes, used):
            if use and array is not None:
                self.take([array], anywhere, pltpu.HBM)
                self.give([shape], anywhere, pltpu.HBM, len(self.args) - 1)
            elif use:
                self.give([shape], anywhere, pltpu.HBM)

    def run(self, body, scratch, flops):
        return list(
            pl.pallas_call(
                body,
                out_shape=self.out_shape,
                in_specs=self.in_specs,
                out_specs=self.out_specs,
                scratch_shapes=scratch,
                input_output_aliases=self.aliases,
                compiler_params=pltpu.CompilerParams(vmem_limit_bytes=10 * 2**20),
                cost_estimate=pl.CostEstimate(
                    flops=flops, bytes_accessed=2**22, transcendentals=0
                ),
            )(*self.args)
        )


def updated(old, used, new):
    new = list(new)
    old = old or (None,) * len(used)
    return [new.pop(0) if u else o for o, u in zip(old, used)]


def like(arrays):
    return [(x.shape, x.dtype) for x in arrays]


class State(NamedTuple):
    numbers: Any
    info: Any
    table: Any
    weights: Any
    turned: Any = None
    reread: Any = None
    kept: Any = None
    back: Any = None


def run_forward(plan, tick, state, incoming, frames_in):
    reread_shapes, kept_shapes, _ = shapes_of(plan)
    first = state.turned is None
    at_turned = at_kept = None
    call = Call()
    if first:
        call.take(state.numbers, in_smem)
        call.take([state.table], anywhere)
        call.take(state.weights, anywhere)
    else:
        call.take([state.info], in_smem, pltpu.SMEM)
        call.take([state.table], in_vmem, pltpu.VMEM)
        call.take(state.weights, in_vmem, pltpu.VMEM)
        at_turned = len(call.args)
        call.take(state.turned, anywhere, pltpu.VMEM)
    if incoming is not None:
        call.take([incoming], in_vmem, pltpu.VMEM)
    call.take([frames_in], anywhere)
    if first:
        call.give([((2 * plan.micros,), jnp.int32)], in_smem, pltpu.SMEM)
        call.give(like([state.table]), in_vmem, pltpu.VMEM)
        call.give(like(state.weights), in_vmem, pltpu.VMEM)
    else:
        at_kept = len(call.args)
        call.take(state.reread, anywhere, pltpu.HBM)
    call.give([(w.shape[::-1], BF16) for w in state.weights], anywhere, pltpu.VMEM, at_turned)
    call.give(reread_shapes, anywhere, pltpu.HBM, at_kept)
    used = (True, True) + plan.fwd_reaches(tick)
    call.update(state.kept, kept_shapes, used)
    call.give([((plan.frames, plan.features), BF16)], in_vmem, pltpu.VMEM)
    scratch = scratch_of(reread_shapes) + [
        pltpu.VMEM((plan.frames, plan.features), BF16),
        pltpu.VMEM((CORES, plan.frames, 3 * plan.features // CORES), BF16),
        pltpu.VMEM((plan.frames, plan.features), BF16),
        pltpu.VMEM((plan.frames, plan.hidden_units), BF16),
        pltpu.VMEM((2, plan.features, 256), BF16),
        pltpu.SemaphoreType.DMA((24,)),
    ]
    flops = 2 * plan.frames * sum(w.size for w in state.weights)
    body = functools.partial(forward_kernel, plan, tick, incoming is not None, first)
    got = call.run(body, scratch, flops)
    if first:
        state = state._replace(info=got[0], table=got[1], weights=Weights(*got[2:6]))
        got = got[6:]
    kept = Kept(*updated(state.kept, used, got[9:-1]))
    return state._replace(turned=Weights(*got[:4]), reread=Reread(*got[4:9]), kept=kept), got[-1]


def run_backward(plan, tick, state, arriving, cotangent, after):
    reread_shapes, _, back_shapes = shapes_of(plan)
    first = state.back is None
    call = Call()
    call.take([state.info], in_smem, pltpu.SMEM)
    call.take([state.table], in_vmem, pltpu.VMEM)
    call.take(state.turned, in_vmem, pltpu.VMEM)
    staying = state.weights if tick < plan.ticks() - 1 else ()
    call.take(staying, anywhere, pltpu.VMEM)
    call.take(after, anywhere)
    unread = len(staying) + len(after)
    if arriving is not None:
        call.take([arriving], in_vmem, pltpu.VMEM)
    call.take([cotangent], anywhere)
    at_reread = len(call.args)
    call.take(state.reread, anywhere, pltpu.HBM)
    call.give(reread_shapes, anywhere, pltpu.HBM, at_reread)
    used = (True,) + plan.bwd_reaches(tick) + (True,) * 4
    call.update(state.back, back_shapes, used)
    call.give([((plan.frames, plan.features), BF16)], in_vmem, pltpu.VMEM)
    narrow = pltpu.VMEM((plan.frames, plan.features), BF16)
    full = pltpu.VMEM((plan.frames, plan.features), F32)
    scratch = scratch_of(reread_shapes) + [
        narrow,
        pltpu.VMEM((CORES, plan.frames, plan.features // CORES), BF16),
        pltpu.VMEM((plan.frames, plan.hidden_units), BF16),
        full,
        full,
        narrow,
        narrow,
        pltpu.VMEM((plan.frames, 3 * plan.features), BF16),
        pltpu.VMEM((4, plan.features), F32),
        pltpu.SemaphoreType.DMA((16,)),
    ]
    flops = 2 * plan.frames * sum(w.size for w in state.turned)
    body = functools.partial(backward_kernel, plan, tick, arriving is not None, first, unread)
    got = call.run(body, scratch, flops)
    back = Back(*updated(state.back, used, got[5:-1]))
    return state._replace(reread=Reread(*got[:5]), back=back), got[-1]


def last_y(plan, state, arriving, before):
    stored = state.back.y_last
    return pl.pallas_call(
        functools.partial(last_y_kernel, plan),
        out_shape=pltpu.VMEM(stored.shape, BF16),
        in_specs=[in_vmem, anywhere, anywhere],
        out_specs=in_vmem,
        scratch_shapes=[pltpu.SemaphoreType.DMA],
    )(pltpu.with_memory_space_constraint(arriving, pltpu.VMEM), in_hbm(stored), before)


def in_hbm(x):
    return pltpu.with_memory_space_constraint(x, pltpu.HBM)


class Pair(NamedTuple):
    left: Any
    share: int
    right: Any
    first: int = 0


def weight_grad_kernel(shares, first_column, width, has_start, skip_ends, *refs):
    count = len(shares)
    lefts, rights = refs[:count], refs[count : 2 * count]
    start = refs[2 * count] if has_start else None
    out, stage, turned, sems = refs[-4:]
    micros, frames, step = rights[0].shape
    chip = lax.axis_index("batch") // CORES
    chips = lax.axis_size("batch") // CORES
    works = (chip > 0) & (chip < chips - 1) if skip_ends else chip >= 0

    @pl.when(works & (pl.program_id(0) == 0))
    def turn_lefts():
        copies = []
        for i, left in enumerate(lefts):
            part = left.at[shares[i], :, :, pl.ds(first_column, width)]
            copies.append(pltpu.make_async_copy(part, stage.at[i], sems.at[i]))
            copies[i].start()
        for i in range(count):
            copies[i].wait()
            for m in range(micros):
                turned[i, :, m * frames : (m + 1) * frames] = stage[i, m].T

    @pl.when(works)
    def add_up():
        total = start[...].astype(F32) if has_start else None
        for i in range(count):
            term = product(turned[i], rights[i][...].reshape(micros * frames, step))
            total = term if total is None else total + term
        out[...] = total.astype(BF16)

    if skip_ends:

        @pl.when(jnp.logical_not(works))
        def nothing():
            out[...] = jnp.zeros(out.shape, BF16)


def weight_grad(pairs, first_column, width, start=None, skip_ends=False, after=()):
    count = len(pairs)
    _, micros, frames, _ = pairs[0].left.shape
    columns = pairs[0].right.shape[2]
    step = min(columns, BLOCK)
    right_specs = [
        pl.BlockSpec((micros, frames, step), lambda j, at=p.first // micros: (at, 0, j))
        for p in pairs
    ]
    block = pl.BlockSpec((width, step), lambda j: (0, j))
    starts = [] if start is None else [start]
    shares = [p.share for p in pairs]
    return pl.pallas_call(
        functools.partial(
            weight_grad_kernel, shares, first_column, width, start is not None, skip_ends
        ),
        grid=(columns // step,),
        out_shape=pltpu.HBM((width, columns), BF16),
        in_specs=[anywhere] * count
        + right_specs
        + [block] * len(starts)
        + [anywhere] * len(after),
        out_specs=block,
        scratch_shapes=[
            pltpu.VMEM((count, micros, frames, width), BF16),
            pltpu.VMEM((count, width, micros * frames), BF16),
            pltpu.SemaphoreType.DMA((count,)),
        ],
        compiler_params=pltpu.CompilerParams(vmem_limit_bytes=10 * 2**20),
        cost_estimate=pl.CostEstimate(
            flops=2 * count * micros * frames * width * columns,
            bytes_accessed=2 * width * columns,
            transcendentals=0,
        ),
    )(
        *[p.left for p in pairs],
        *[p.right for p in pairs],
        *[in_hbm(x) for x in starts],
        *after,
    )


class Part(NamedTuple):
    grad: Any
    column: int
    width: int
    result: int
    place: int
    tall: bool


def fetch_parts(parts, grads, rows, index, target, sems):
    copies, at = [], 0
    first_row = pl.multiple_of(index * rows, rows)
    for i, part in enumerate(parts):
        source = grads[i].at[pl.ds(first_row, rows), pl.ds(part.column, part.width)]
        copies.append(
            pltpu.make_async_copy(source, target.at[:, pl.ds(at, part.width)], sems.at[i])
        )
        copies[i].start()
        at += part.width
    return copies


def send_kernel(parts, rows, hop, adds, *refs):
    grads, refs = refs[: len(parts)], refs[len(parts) :]
    came = refs[:2] if adds else None
    up, down, here, sems = refs[-4:]
    chip = lax.axis_index("batch") // CORES
    last = lax.axis_size("batch") // CORES - 1
    places = (jnp.minimum(chip + last - (hop - 1), last), jnp.maximum(chip - last + (hop - 1), 0))
    targets = (here.at[0], here.at[1]) if adds else (up, down)
    copies = []
    for d in range(2):
        copies += fetch_parts(parts, grads, rows, places[d], targets[d], sems.at[d])
    for copy in copies:
        copy.wait()
    if adds:
        up[...] = (here[0].astype(F32) + came[0][...].astype(F32)).astype(BF16)
        down[...] = (here[1].astype(F32) + came[1][...].astype(F32)).astype(BF16)


def finish_kernel(parts, rows, result_count, *refs):
    grads, refs = refs[: len(parts)], refs[len(parts) :]
    came = refs[:2]
    here, total, turned, sems = refs[-4:]
    results = refs[-5 - result_count : -5]
    refs[-5][...] = jnp.zeros(refs[-5].shape, F32)
    chip = lax.axis_index("batch") // CORES
    for copy in fetch_parts(parts, grads, rows, chip, here, sems):
        copy.wait()
    total[...] = here[...].astype(F32) + came[0][...].astype(F32) + came[1][...].astype(F32)
    copies, at = [], 0
    for i, part in enumerate(parts):
        result = results[part.result]
        if part.tall:
            turned[...] = total[:, at : at + part.width].T
            source, target = turned, result.at[pl.ds(part.place, part.width), :]
        else:
            source = total.at[pl.ds(0, result.shape[0]), pl.ds(at, part.width)]
            target = result.at[:, pl.ds(part.place, part.width)]
        copies.append(pltpu.make_async_copy(source, target, sems.at[i]))
        copies[i].start()
        at += part.width
    for copy in copies:
        copy.wait()


class Piece:
    def __init__(self, parts, first_hop):
        self.parts, self.hop, self.first_hop = parts, first_hop - 1, first_hop
        self.came = None
        self.width = sum(p.width for p in parts)


class Line:
    def __init__(self, exchange, rows, results, before):
        self.chips, self.rows, self.before = exchange.chips, rows, before
        self.results = {}
        self.shapes = results

    def step(self, piece):
        if piece.hop == self.chips - 1:
            self.finish(piece)
        else:
            self.send(piece)

    def send(self, piece):
        adds = piece.came is not None
        piece.hop += 1
        shape = (self.rows, piece.width)
        call = Call()
        call.take([p.grad for p in piece.parts], anywhere, pltpu.HBM)
        if adds:
            call.take(piece.came, in_vmem, pltpu.VMEM)
        call.take([self.before], anywhere)
        call.give([(shape, BF16)] * 2, in_vmem, pltpu.VMEM)
        count = len(piece.parts)
        scratch = [pltpu.VMEM((2,) + shape, BF16), pltpu.SemaphoreType.DMA((2, count))]
        parts = [p._replace(grad=None) for p in piece.parts]
        up, down = call.run(
            functools.partial(send_kernel, parts, self.rows, piece.hop, adds), scratch, 2**20
        )
        self.before = up
        edge = piece.first_hop - 1
        last = self.chips - 1
        piece.came = [
            self.moved(up, [z for z in range(last) if edge <= z < piece.hop], 1),
            self.moved(down, [z for z in range(1, last + 1) if edge <= last - z < piece.hop], -1),
        ]

    def moved(self, value, senders, by):
        pairs = [(CORES * z + c, CORES * (z + by) + c) for z in senders for c in range(CORES)]
        return lax.ppermute(value, "batch", pairs)

    def finish(self, piece):
        names = sorted({p.result for p in piece.parts})
        parts = [p._replace(grad=None, result=names.index(p.result)) for p in piece.parts]
        call = Call()
        call.take([p.grad for p in piece.parts], anywhere, pltpu.HBM)
        call.take(piece.came, in_vmem, pltpu.VMEM)
        call.update(
            [self.results.get(n) for n in names],
            [(self.shapes[n], F32) for n in names],
            [True] * len(names),
        )
        call.take([self.before], anywhere)
        call.give([((8, LANES), F32)], in_vmem, pltpu.VMEM)
        shape = (self.rows, piece.width)
        tall = max([p.width for p in parts if p.tall], default=8)
        scratch = [
            pltpu.VMEM(shape, BF16),
            pltpu.VMEM(shape, F32),
            pltpu.VMEM((tall, self.rows), F32),
            pltpu.SemaphoreType.DMA((len(parts),)),
        ]
        done = call.run(
            functools.partial(finish_kernel, parts, self.rows, len(names)), scratch, 2**20
        )
        self.results.update(zip(names, done))
        piece.hop = self.chips
        self.before = done[-1]


def table_gradient(row_grads, codes, blocks):
    chosen = lax.broadcasted_iota(jnp.int32, (blocks, codes.shape[0]), 0) == codes
    return jnp.sum(jnp.where(chosen[:, :, None, None], row_grads[None], 0.0), axis=1)


class Exchange:
    def __init__(self, batch):
        self.batch = batch
        self.chips = batch // CORES
        self.by_hops = batch % CORES == 0 and 2 <= self.chips <= LINE
        self.ends_hand_over = self.by_hops and self.chips == LINE

    def swap(self, x):
        if not self.by_hops:
            return None
        return lax.ppermute(x, "batch", [(b, b ^ 1) for b in range(self.batch)])

    def inward(self, x):
        if not self.ends_hand_over:
            return None
        top = self.batch - CORES
        pairs = [(c, CORES + c) for c in range(CORES)]
        pairs += [(top + c, top - CORES + c) for c in range(CORES)]
        return lax.ppermute(x, "batch", pairs)

    def sources(self, x):
        if not self.ends_hand_over:
            return [x, self.swap(x)]
        came = self.inward(x)
        return [x, self.swap(x), came, self.swap(came)]


def sums_by_hops(plan, exchange, kept, back, grad_down, lefts, table_grad, before):
    chips, rows = exchange.chips, plan.rows
    features, hidden_units = plan.features, plan.hidden_units
    core = lax.axis_index("batch") % CORES
    share = features // CORES
    swap = exchange.swap
    table_size = table_grad.shape[0]
    results = [
        (rows, 3 * features),
        (rows, features),
        (rows, hidden_units),
        (hidden_units, rows),
        (table_size, rows),
    ]
    line = Line(exchange, rows, results, before)

    def of(right, first_column):
        pairs = [Pair(left, i, r) for i, (left, r) in enumerate(zip(lefts, (right, swap(right))))]
        grad = weight_grad(pairs, first_column, share, after=[line.before])
        line.before = grad
        return grad

    half = hidden_units // 2
    down = grad_down(before)
    line.before = down
    first = 2 if exchange.ends_hand_over else 1
    downs = [Piece([Part(down, c, half, 3, c, True)], first) for c in (0, half)]
    for piece in downs:
        line.step(piece)
    up = of(back.grad_up, 2 * share)
    ups = [Piece([Part(up, c, half, 2, c, False)], 1) for c in (0, half)]
    for piece in ups + downs:
        line.step(piece)
    qkv = of(back.grad_packed, 0)
    for piece in ups:
        line.step(piece)
    out = of(back.grad_attn, share)
    norms = table_grad + swap(table_grad)
    norms = norms.reshape(table_size, chips, CORES, rows)
    norms = lax.dynamic_index_in_dim(norms, core, 2, keepdims=False).transpose(1, 0, 2)
    norms = jnp.pad(norms.astype(BF16), ((0, 0), (0, rows - table_size), (0, 0)))
    norms = norms.reshape(chips * rows, rows)
    cut = 2 * features
    others = [
        Piece([Part(qkv, 0, cut, 0, 0, False)], 1),
        Piece(
            [
                Part(qkv, cut, features, 0, cut, False),
                Part(out, 0, features, 1, 0, False),
                Part(norms, 0, rows, 4, 0, False),
            ],
            1,
        ),
    ]
    order = [downs, ups, others, ups, others, others, others]
    for pieces in order:
        for piece in pieces:
            if piece.hop < chips:
                line.step(piece)
    return [line.results[i] for i in range(len(results))]


def sums_by_scatter(plan, kept, back, table_grad):
    features = plan.features
    share = features // CORES
    core = lax.axis_index("batch") % CORES

    def local(lefts, rights, column):
        start = [None, None]
        for left, right in zip(lefts, rights):
            for i in range(CORES):
                start[i] = weight_grad([Pair(left, i, right)], column, share, start[i])
        mine, other = start
        even, odd = jnp.where(core == 0, mine, other), jnp.where(core == 0, other, mine)
        blocks = [x.reshape(-1, 1, plan.rows, x.shape[1]) for x in (even, odd)]
        return jnp.concatenate(blocks, axis=1).reshape(features, -1)

    def scattered(x, dimension):
        return lax.psum_scatter(
            x, "batch", scatter_dimension=dimension, tiled=True
        ).astype(F32)

    grad_y = [back.y_early, jnp.concatenate([back.y_late, back.y_last], axis=1)]
    down = local(grad_y, [kept.act_early, kept.act_late], 0)
    return (
        scattered(local([kept.left], [back.grad_packed], 0), 0),
        scattered(local([kept.left], [back.grad_attn], share), 0),
        scattered(local([kept.left], [back.grad_up], 2 * share), 0),
        scattered(down, 0).T,
        scattered(table_grad, 1),
    )


def per_device(
    frames_in, cotangent, qkv_weight, out_weight, up_weight, down_weight, norm_table, lengths,
    codebooks,
):
    sections = lax.axis_size("section")
    batch = lax.axis_size("batch")
    section = lax.axis_index("section")
    micros = lengths.shape[0]
    tokens, features = frames_in.shape
    frames = tokens // micros
    plan = Plan(
        sections, micros, frames, features, up_weight.shape[2], max(features // batch, LANES)
    )
    frames_all = frames_in.reshape(micros, frames, features)
    cot_all = cotangent.reshape(micros, frames, features)

    state = State(
        numbers=[lengths, codebooks],
        info=None,
        table=norm_table[0],
        weights=Weights(qkv_weight[0], out_weight[0], up_weight[0], down_weight[0]),
    )
    exchange = Exchange(batch)

    def down_pairs(grad_y, act, first=0):
        return [Pair(y, i % CORES, a, first) for i, (y, a) in enumerate(zip(grad_y, act))]

    def down_grad(pairs, start, before):
        share = features // CORES
        return weight_grad(pairs, 0, share, start, exchange.ends_hand_over, [before])

    after = ()
    incoming = arriving = None
    working = lambda micro: 0 <= micro < micros
    for tick in range(plan.ticks()):
        sent = returned = None
        if tick == plan.ticks() - 1 and exchange.by_hops:
            down = down_grad(down_pairs(y_early, act_early), None, state.back.grad_in)
            y_last = exchange.sources(last_y(plan, state, arriving, down))
            after = act_late[1:3] + y_last[:1]
        elif tick == plan.ticks() - 1:
            y_last = last_y(plan, state, arriving, state.back.grad_in)
            state = state._replace(back=state.back._replace(y_last=y_last))
        if tick < plan.fwd_ticks():
            state, output = run_forward(plan, tick, state, incoming, frames_all)
            onward = [
                (s, s + 1) for s in range(sections - 1) if working(plan.fwd_id(tick, s))
            ]
            if onward:
                sent = lax.ppermute(output, "section", onward)
        if tick >= sections - 1:
            state, output = run_backward(plan, tick, state, arriving, cot_all, after)
            after = ()
            backward = [
                (s, s - 1) for s in range(1, sections) if working(plan.bwd_id(tick, s))
            ]
            if backward:
                returned = lax.ppermute(output, "section", backward)
        incoming, arriving = sent, returned
        if exchange.by_hops:
            if tick == plan.act_spans()[0][1] + sections - 2:
                act_early = exchange.sources(state.kept.act_early)
            if tick == plan.fwd_ticks() - 1:
                act_late = exchange.sources(state.kept.act_late)
                lefts = [state.kept.left, exchange.swap(state.kept.left)]
                after = act_early[1:3]
            if tick == plan.y_spans()[0][1] + 2 * sections - 3:
                y_early = exchange.sources(state.back.y_early)
            if tick == plan.ticks() - 2:
                y_late = exchange.sources(state.back.y_late)

    blocks = norm_table.shape[1] // 4
    codes = codebooks * (section % 2)
    table_grad = table_gradient(state.back.row_grads, codes, blocks).reshape(norm_table.shape[1:])
    if exchange.by_hops:
        late_pairs = down_pairs(y_late, act_late) + down_pairs(y_last, act_late, micros // 2 - 1)
        sums = sums_by_hops(
            plan, exchange, state.kept, state.back,
            lambda before: down_grad(late_pairs, down, before), lefts, table_grad, output,
        )
    else:
        sums = sums_by_scatter(plan, state.kept, state.back, table_grad)
    return (
        state.kept.layer_out.reshape(1, tokens, features),
        state.back.grad_in.reshape(1, tokens, features),
    ) + tuple(x[None] for x in sums)


def solution(mesh):
    section, batch = mesh.axis_names
    over_batch = P(batch)
    over_section = P(section)
    both = P(section, batch, None)
    columns = P(section, None, batch)
    in_specs = (over_batch,) * 2 + (over_section,) * 5 + (over_batch,) * 2
    out_specs = (both,) * 5 + (columns,) * 2
    return jax.shard_map(
        per_device, mesh=mesh, in_specs=in_specs, out_specs=out_specs, check_vma=False
    )
```

```python
import functools
from typing import Any, NamedTuple

import jax
import jax.numpy as jnp
from jax import lax
from jax.experimental import pallas as pl
from jax.experimental.pallas import tpu as pltpu
from jax.sharding import PartitionSpec as P

HEADS = 16
GROUP = 4
BLOCK = 512
LANES = 128
CORES = 2
VMEM_LIMIT = 14 * 2**20
WHOLE, FIRST, SECOND = 0, 1, 2
LINE = 4

epsilon = 1e-05
masked_score = -1e30
BF16 = jnp.bfloat16
F32 = jnp.float32

in_vmem = pl.BlockSpec(memory_space=pltpu.VMEM)
in_smem = pl.BlockSpec(memory_space=pltpu.SMEM)
anywhere = pl.BlockSpec(memory_space=pl.ANY)


class Weights(NamedTuple):
    qkv: Any
    out: Any
    up: Any
    down: Any


class Reread(NamedTuple):
    entry: Any
    packed: Any
    probs: Any
    hidden: Any
    slope: Any


class Kept(NamedTuple):
    layer_out: Any
    left: Any
    second: Any
    act: Any


class Back(NamedTuple):
    grad_in: Any
    y_early: Any
    y_late: Any
    y_last: Any
    up_early: Any
    up_last: Any
    grad_attn: Any
    grad_packed: Any
    row_grads: Any


def product(left, right):
    return lax.dot_general(left, right, (((1,), (0,)), ((), ())), preferred_element_type=F32)


def product_last(left, right):
    return lax.dot_general(left, right, (((1,), (1,)), ((), ())), preferred_element_type=F32)


def product_first(left, right):
    return lax.dot_general(left, right, (((0,), (0,)), ((), ())), preferred_element_type=F32)


def normalize(values):
    centre = values - jnp.mean(values, axis=-1, keepdims=True)
    reciprocal = lax.rsqrt(jnp.mean(centre * centre, axis=-1, keepdims=True) + epsilon)
    return centre * reciprocal, reciprocal


def normalize_back(gradient, normal_part, reciprocal, gain_row):
    scaled = gradient * (1.0 + gain_row)
    centred = scaled - jnp.mean(scaled, axis=-1, keepdims=True)
    return reciprocal * (
        centred - normal_part * jnp.mean(scaled * normal_part, axis=-1, keepdims=True)
    )


def gelu_and_slope(u):
    root = 0.7978845608028654
    square = u * u
    bent = jnp.tanh(root * u * (1.0 + 0.044715 * square))
    half = 0.5 * (1.0 + bent)
    slope = half + 0.5 * u * (1.0 - bent * bent) * (root * (1.0 + 3 * 0.044715 * square))
    return u * half, slope


def stacked_heads(block, head_size):
    owner = lax.broadcasted_iota(jnp.int32, block.shape, 1) // head_size
    zero = jnp.zeros_like(block)
    return jnp.concatenate([jnp.where(owner == h, block, zero) for h in range(GROUP)], axis=0)


def beside(stack, frames):
    return jnp.concatenate([stack[h * frames : (h + 1) * frames] for h in range(GROUP)], axis=1)


def table_rows(table, code):
    pair = table[pl.ds(pl.multiple_of((code // 2) * 8, 8), 8), :]
    return jnp.where(code % 2 == 1, pair[4:8], pair[0:4])


class Saver:
    def __init__(self, sems, base):
        self.sems, self.base, self.pending = sems, base, []

    def __call__(self, source, target):
        copy = pltpu.make_async_copy(source, target, self.sems.at[self.base + len(self.pending)])
        copy.start()
        self.pending.append(copy)

    def spread(self, source, buffers, spans, slot):
        sem = self.sems.at[self.base + len(self.pending)]
        copies = []
        for buffer, (first, end) in zip(buffers, spans):
            if buffer is None:
                continue
            place = jnp.clip(slot - first, 0, end - first - 1)
            copies.append(pltpu.make_async_copy(source, buffer.at[place], sem))
            pl.when((slot >= first) & (slot < end))(copies[-1].start)
        self.pending.append(copies[0])

    def wait(self):
        for copy in self.pending:
            copy.wait()


def turn(source, target, row0, col0, side_by, strips, sems, base):
    side = 256
    ones = (
        lax.broadcasted_iota(jnp.int32, (side, side), 0)
        == lax.broadcasted_iota(jnp.int32, (side, side), 1)
    ).astype(BF16)

    slots = strips.shape[0]
    count = side_by // side

    def strip(i):
        r = pl.multiple_of(row0 + i * side, side)
        return pltpu.make_async_copy(
            strips.at[i % slots],
            target.at[pl.ds(col0, side_by), pl.ds(r, side)],
            sems.at[base + i % slots],
        )

    def one_strip(i, carry):
        @pl.when(i >= slots)
        def slot_is_free():
            strip(i - slots).wait()

        r = pl.multiple_of(row0 + i * side, side)
        for c in range(0, side_by, side):
            strips[i % slots, c : c + side, :] = product_last(
                ones, source[pl.ds(r, side), col0 + c : col0 + c + side]
            ).astype(BF16)
        strip(i).start()
        return carry

    lax.fori_loop(0, count, one_strip, 0)
    for i in range(count - slots, count):
        strip(i).wait()


class Plan(NamedTuple):
    sections: int
    micros: int
    frames: int
    features: int
    hidden_units: int
    rows: int

    def fwd_ticks(self):
        return self.micros + self.sections - 1

    def ticks(self):
        return self.micros + 2 * (self.sections - 1)

    def y_spans(self):
        half = self.micros // 2
        return (0, half), (half, self.micros - 1), (self.micros - 1, self.micros)

    def up_spans(self):
        return (0, self.micros - 1), (self.micros - 1, self.micros)

    def bwd_reaches(self, tick):
        low, high = tick - 2 * (self.sections - 1), tick - (self.sections - 1)
        grad_y = tuple(low < end and high >= first for first, end in self.y_spans())
        grad_up = tuple(low < end and high >= first for first, end in self.up_spans())
        return (True,) + grad_y + grad_up + (True,) * 3

    def bwd_uses(self, tick, part):
        first = (False,) + (True,) * 6 + (False, False)
        halves = {WHOLE: (True,) * 9, FIRST: first, SECOND: tuple(not f for f in first)}
        return tuple(r and h for r, h in zip(self.bwd_reaches(tick), halves[part]))

    def fwd_id(self, tick, section):
        return tick - section

    def bwd_id(self, tick, section):
        return tick - 2 * (self.sections - 1) + section


def forward_kernel(plan, tick, has_incoming, loads_weights, *refs):
    refs = list(refs)
    take = lambda n: [refs.pop(0) for _ in range(n)]
    if loads_weights:
        lengths, codebooks, given_table = take(3)
        given = Weights(*take(4))
    else:
        info, table = take(2)
        weight = Weights(*take(4))
        take(4)
    incoming = take(1)[0] if has_incoming else None
    (frames_in,) = take(1)
    if loads_weights:
        info, table = take(2)
        weight = Weights(*take(4))
    else:
        take(len(Reread._fields) + len(Kept._fields))
    turned = Weights(*take(4))
    reread = Reread(*take(5))
    kept = Kept(*take(4))
    (outgoing,) = take(1)
    entry, packed, probs, hidden, slope, normed, left, attended, act, strips, sems = refs

    micros, frames, features, hidden_units, rows_kept = plan[1:]
    head_size = features // HEADS
    group_width = GROUP * head_size
    section = lax.axis_index("section")
    core = lax.axis_index("batch") % CORES
    is_nar = section % 2
    micro = plan.fwd_id(tick, section)
    active = (micro >= 0) & (micro < micros)
    slot = jnp.clip(micro, 0, micros - 1)

    loads = []
    if loads_weights:
        for i in range(micros):
            info[i] = lengths[i]
            info[micros + i] = codebooks[i]
        pairs = [(given_table, table)] + list(zip(given, weight))
        for i, (source, target) in enumerate(pairs):
            loads.append(pltpu.make_async_copy(source, target, sems.at[i]))
            loads[i].start()
    base = len(loads)

    def ready(i):
        if loads_weights:
            loads[i].wait()

    @pl.when(active)
    def forward():
        save = Saver(sems, base)
        length = info[slot]
        code = info[micros + slot] * is_nar

        def own_input():
            pltpu.sync_copy(frames_in.at[slot], entry)

        if has_incoming:
            pl.when(section == 0)(own_input)

            @pl.when(section != 0)
            def passed_input():
                entry[...] = incoming[...]

        else:
            own_input()

        save(entry, reread.entry.at[slot])
        share = features // CORES

        def share_columns(source, first):
            for b in range(features // rows_kept):
                at = first + (b // CORES) * rows_kept
                left[b % CORES, :, at : at + rows_kept] = source[
                    :, b * rows_kept : (b + 1) * rows_kept
                ]

        ready(0)
        rows = table_rows(table, code)
        residual = entry[...].astype(F32)
        normal_one, _ = normalize(residual)
        normed[...] = (normal_one * (1.0 + rows[0:1]) + rows[1:2]).astype(BF16)
        share_columns(normed, 0)
        ready(1)
        for j in range(0, 3 * features, BLOCK):
            packed[:, j : j + BLOCK] = product(normed[...], weight.qkv[:, j : j + BLOCK]).astype(
                BF16
            )
        save(packed, reread.packed.at[slot])
        tall = (GROUP * frames, frames)
        query_ids = lax.rem(lax.broadcasted_iota(jnp.int32, tall, 0), frames)
        key_ids = lax.broadcasted_iota(jnp.int32, tall, 1)
        allowed = (key_ids < length) & (key_ids <= query_ids + is_nar * frames)
        inv_root = head_size ** (-0.5)
        for g in range(HEADS // GROUP):
            lo, hi = g * group_width, (g + 1) * group_width
            queries = stacked_heads(packed[:, lo:hi], head_size)
            keys = packed[:, features + lo : features + hi]
            values = stacked_heads(packed[:, 2 * features + lo : 2 * features + hi], head_size)
            scores = jnp.where(allowed, product_last(queries, keys) * inv_root, masked_score)
            exp_scores = jnp.exp(scores - jnp.max(scores, axis=-1, keepdims=True))
            total = jnp.sum(exp_scores, axis=-1, keepdims=True)
            group_probs = (exp_scores / total).astype(BF16)
            probs[g * GROUP * frames : (g + 1) * GROUP * frames, :] = group_probs
            attended[:, lo:hi] = product(beside(group_probs, frames), values).astype(BF16)
        save(probs, reread.probs.at[slot])
        share_columns(attended, share)
        ready(2)
        for j in range(0, features, BLOCK):
            hidden[:, j : j + BLOCK] = residual[:, j : j + BLOCK] + product(
                attended[...], weight.out[:, j : j + BLOCK]
            )
        save(hidden, reread.hidden.at[slot])
        normal_two, _ = normalize(hidden[...])
        normed[...] = (normal_two * (1.0 + rows[2:3]) + rows[3:4]).astype(BF16)
        share_columns(normed, 2 * share)
        save(normed, kept.second.at[slot])
        save(left.at[core], kept.left.at[0, slot])
        save(left.at[1 - core], kept.left.at[1, slot])
        ready(3)
        for j in range(0, hidden_units, BLOCK):
            value, gradient = gelu_and_slope(product(normed[...], weight.up[:, j : j + BLOCK]))
            act[:, j : j + BLOCK] = value.astype(BF16)
            slope[:, j : j + BLOCK] = gradient.astype(BF16)
        save(slope, reread.slope.at[slot])
        save(act, kept.act.at[slot])
        ready(4)
        for j in range(0, features, BLOCK):
            outgoing[:, j : j + BLOCK] = (
                hidden[:, j : j + BLOCK] + product(act[...], weight.down[:, j : j + BLOCK])
            ).astype(BF16)
        save(outgoing, kept.layer_out.at[slot])
        save.wait()

    units = []
    for source, target in zip(weight, turned):
        total_rows, total_cols = source.shape
        for r in range(0, total_rows, features):
            for c in range(0, total_cols, features):
                units.append((source, target, r, c))
    pieces = 2
    piece = jnp.where(micro < 0, tick, micro - micros + section)

    @pl.when(jnp.logical_not(active))
    def wait_for_weights():
        for i in range(base):
            ready(i)

    for k in range(pieces):

        @pl.when(jnp.logical_not(active) & (piece == k))
        def one_piece(k=k):
            for source, target, r, c in units[k::pieces]:
                turn(source, target, r, c, features, strips, sems, base)


def backward_kernel(plan, tick, part, has_arriving, present, unread, *refs):
    refs = list(refs)
    take = lambda n: [refs.pop(0) for _ in range(n)]
    info, table = take(2)
    turned = Weights(*(take(1) + [None] * 3 if part == SECOND else take(4)))
    take(unread)
    arriving = take(1)[0] if has_arriving else None
    (cotangent,) = take(1)
    take(len(Reread._fields))
    used = plan.bwd_uses(tick, part)
    take(sum(u and p for u, p in zip(used, present)))
    halfway = take(3) if part == SECOND else None
    reread = Reread(*take(5))
    back = Back(*[take(1)[0] if u else None for u in used])
    if part == FIRST:
        halfway = take(3)
    else:
        (returning,) = take(1)
    (entry, packed, probs, hidden, slope, grad_y, grad_up, wide, grad_hidden, grad_attn, mixed,
     grad_packed, row_grads, sems) = refs

    micros, frames, features, hidden_units, _ = plan[1:]
    head_size = features // HEADS
    group_width = GROUP * head_size
    section = lax.axis_index("section")
    is_nar = section % 2
    micro = plan.bwd_id(tick, section)
    active = (micro >= 0) & (micro < micros)
    slot = jnp.clip(micro, 0, micros - 1)

    def start_fetches(wanted):
        fetches = []
        for i, target in enumerate((entry, packed, probs, hidden, slope)):
            fetches.append(pltpu.make_async_copy(reread[i].at[slot], target, sems.at[i]))
        for i in (4, 3, 1, 2, 0):
            if i in wanted:
                fetches[i].start()
        return fetches

    def first_half():
        length = info[slot]
        code = info[micros + slot] * is_nar
        fetches = start_fetches((3, 4) if part == FIRST else range(5))
        save = Saver(sems, len(fetches))

        def own_cotangent():
            pltpu.sync_copy(cotangent.at[slot], grad_y)
            live = lax.broadcasted_iota(jnp.int32, (frames, features), 0) < length
            grad_y[...] = jnp.where(live, grad_y[...], jnp.zeros((frames, features), BF16))

        if has_arriving:
            pl.when(section == plan.sections - 1)(own_cotangent)

            @pl.when(section != plan.sections - 1)
            def passed_gradient():
                grad_y[...] = arriving[...]

        else:
            own_cotangent()

        save.spread(grad_y, back[1:4], plan.y_spans(), slot)
        rows = table_rows(table, code)
        fetches[4].wait()
        for j in range(0, hidden_units, BLOCK):
            grad_act = product(grad_y[...], turned.down[:, j : j + BLOCK])
            grad_up[:, j : j + BLOCK] = (
                grad_act * slope[:, j : j + BLOCK].astype(F32)
            ).astype(BF16)
        save.spread(grad_up, (back.up_early, back.up_last), plan.up_spans(), slot)
        for j in range(0, features, BLOCK):
            wide[:, j : j + BLOCK] = product(grad_up[...], turned.up[:, j : j + BLOCK])
        fetches[3].wait()
        normal_two, recip_two = normalize(hidden[...])
        grad_two = wide[...]
        row_grads[2:3, :] = jnp.sum(grad_two * normal_two, axis=0, keepdims=True)
        row_grads[3:4, :] = jnp.sum(grad_two, axis=0, keepdims=True)
        grad_hidden[...] = grad_y[...].astype(F32) + normalize_back(
            grad_two, normal_two, recip_two, rows[2:3]
        )
        grad_attn[...] = grad_hidden[...].astype(BF16)
        save(grad_attn, back.grad_attn.at[slot])
        for j in range(0, features, BLOCK):
            mixed[:, j : j + BLOCK] = product(
                grad_attn[...], turned.out[:, j : j + BLOCK]
            ).astype(BF16)
        return fetches, save

    def second_half(fetches, save):
        code = info[micros + slot] * is_nar
        rows = table_rows(table, code)
        fetches[1].wait()
        fetches[2].wait()
        inv_root = head_size ** (-0.5)
        for g in range(HEADS // GROUP):
            lo, hi = g * group_width, (g + 1) * group_width
            queries = stacked_heads(packed[:, lo:hi], head_size)
            keys = stacked_heads(packed[:, features + lo : features + hi], head_size)
            values = packed[:, 2 * features + lo : 2 * features + hi]
            group_mixed = stacked_heads(mixed[:, lo:hi], head_size)
            group_probs = probs[g * GROUP * frames : (g + 1) * GROUP * frames, :]
            wide_probs = group_probs.astype(F32)
            grad_probs = product_last(group_mixed, values)
            inner = jnp.sum(wide_probs * grad_probs, axis=-1, keepdims=True)
            grad_scores = (wide_probs * (grad_probs - inner)).astype(BF16)
            grad_packed[:, lo:hi] = (
                product(beside(grad_scores, frames), keys) * inv_root
            ).astype(BF16)
            grad_packed[:, features + lo : features + hi] = (
                product_first(grad_scores, queries) * inv_root
            ).astype(BF16)
            grad_packed[:, 2 * features + lo : 2 * features + hi] = product_first(
                group_probs, group_mixed
            ).astype(BF16)
        save(grad_packed, back.grad_packed.at[slot])
        for j in range(0, features, BLOCK):
            wide[:, j : j + BLOCK] = product(grad_packed[...], turned.qkv[:, j : j + BLOCK])
        fetches[0].wait()
        normal_one, recip_one = normalize(entry[...].astype(F32))
        grad_one = wide[...]
        row_grads[0:1, :] = jnp.sum(grad_one * normal_one, axis=0, keepdims=True)
        row_grads[1:2, :] = jnp.sum(grad_one, axis=0, keepdims=True)
        save(row_grads, back.row_grads.at[slot])
        returning[...] = (
            grad_hidden[...] + normalize_back(grad_one, normal_one, recip_one, rows[0:1])
        ).astype(BF16)
        save(returning, back.grad_in.at[slot])
        save.wait()

    @pl.when(active)
    def backward():
        if part == SECOND:
            fetches = start_fetches((0, 1, 2))
            load = Saver(sems, 5)
            for source, target in zip(halfway, (grad_hidden, mixed, row_grads)):
                load(source, target)
            load.wait()
            second_half(fetches, Saver(sems, 5))
            return
        fetches, save = first_half()
        if part == FIRST:
            for source, target in zip((grad_hidden, mixed, row_grads), halfway):
                save(source, target)
            save.wait()
        else:
            second_half(fetches, save)


def shapes_of(plan):
    micros, frames, features, hidden_units, _ = plan[1:]
    own = (micros, frames)
    reread = Reread(
        entry=(own + (features,), BF16),
        packed=(own + (3 * features,), BF16),
        probs=((micros, HEADS * frames, frames), BF16),
        hidden=(own + (features,), F32),
        slope=(own + (hidden_units,), BF16),
    )
    def buffers(spans, columns):
        return [((end - first, frames, columns), BF16) for first, end in spans]

    left = ((CORES,) + own + (3 * features // CORES,), BF16)
    wide = (own + (features,), BF16)
    kept = Kept(wide, left, wide, (own + (hidden_units,), BF16))
    back = Back(
        wide,
        *buffers(plan.y_spans(), features),
        *buffers(plan.up_spans(), hidden_units),
        grad_attn=wide,
        grad_packed=(own + (3 * features,), BF16),
        row_grads=((micros, 4, features), F32),
    )
    return reread, kept, back


def scratch_of(shapes):
    return [pltpu.VMEM(shape[1:], dtype) for shape, dtype in shapes]


class Call:
    def __init__(self):
        self.args, self.in_specs, self.out_shape, self.out_specs = [], [], [], []
        self.aliases = {}

    def take(self, values, spec, space=None):
        for value in values:
            if space is not None:
                value = pltpu.with_memory_space_constraint(value, space)
            self.args.append(value)
            self.in_specs.append(spec)

    def give(self, shapes, spec, space, updates=None):
        for i, (shape, dtype) in enumerate(shapes):
            if updates is not None:
                self.aliases[updates + i] = len(self.out_shape)
            self.out_shape.append(space(shape, dtype))
            self.out_specs.append(spec)

    def update(self, arrays, shapes, used):
        arrays = arrays or (None,) * len(shapes)
        for array, shape, use in zip(arrays, shapes, used):
            if use and array is not None:
                self.take([array], anywhere, pltpu.HBM)
                self.give([shape], anywhere, pltpu.HBM, len(self.args) - 1)
            elif use:
                self.give([shape], anywhere, pltpu.HBM)

    def run(self, body, scratch, flops, limit=VMEM_LIMIT):
        return list(
            pl.pallas_call(
                body,
                out_shape=self.out_shape,
                in_specs=self.in_specs,
                out_specs=self.out_specs,
                scratch_shapes=scratch,
                input_output_aliases=self.aliases,
                compiler_params=pltpu.CompilerParams(vmem_limit_bytes=limit),
                cost_estimate=pl.CostEstimate(
                    flops=flops, bytes_accessed=0, transcendentals=0
                ),
            )(*self.args)
        )


def updated(old, used, new):
    new = list(new)
    old = old or (None,) * len(used)
    return [new.pop(0) if u else o for o, u in zip(old, used)]


def like(arrays):
    return [(x.shape, x.dtype) for x in arrays]


class State(NamedTuple):
    numbers: Any
    info: Any
    table: Any
    weights: Any
    turned: Any = None
    reread: Any = None
    kept: Any = None
    back: Any = None


def run_forward(plan, tick, state, incoming, frames_in):
    reread_shapes, kept_shapes, _ = shapes_of(plan)
    first = state.turned is None
    at_turned = at_kept = None
    call = Call()
    if first:
        call.take(state.numbers, in_smem)
        call.take([state.table], anywhere)
        call.take(state.weights, anywhere)
    else:
        call.take([state.info], in_smem, pltpu.SMEM)
        call.take([state.table], in_vmem, pltpu.VMEM)
        call.take(state.weights, in_vmem, pltpu.VMEM)
        at_turned = len(call.args)
        call.take(state.turned, anywhere, pltpu.VMEM)
    if incoming is not None:
        call.take([incoming], in_vmem, pltpu.VMEM)
    call.take([frames_in], anywhere)
    if first:
        call.give([((2 * plan.micros,), jnp.int32)], in_smem, pltpu.SMEM)
        call.give(like([state.table]), in_vmem, pltpu.VMEM)
        call.give(like(state.weights), in_vmem, pltpu.VMEM)
    else:
        at_kept = len(call.args)
        call.take(state.reread + state.kept, anywhere, pltpu.HBM)
    call.give([(w.shape[::-1], BF16) for w in state.weights], anywhere, pltpu.VMEM, at_turned)
    call.give(reread_shapes + kept_shapes, anywhere, pltpu.HBM, at_kept)
    call.give([((plan.frames, plan.features), BF16)], in_vmem, pltpu.VMEM)
    scratch = scratch_of(reread_shapes) + [
        pltpu.VMEM((plan.frames, plan.features), BF16),
        pltpu.VMEM((CORES, plan.frames, 3 * plan.features // CORES), BF16),
        pltpu.VMEM((plan.frames, plan.features), BF16),
        pltpu.VMEM((plan.frames, plan.hidden_units), BF16),
        pltpu.VMEM((2, plan.features, 256), BF16),
        pltpu.SemaphoreType.DMA((24,)),
    ]
    flops = 8 * plan.frames * sum(w.size for w in state.weights)
    body = functools.partial(forward_kernel, plan, tick, incoming is not None, first)
    got = call.run(body, scratch, flops)
    if first:
        state = state._replace(info=got[0], table=got[1], weights=Weights(*got[2:6]))
        got = got[6:]
    kept = Kept(*got[9:13])
    return state._replace(turned=Weights(*got[:4]), reread=Reread(*got[4:9]), kept=kept), got[-1]


def run_backward(plan, tick, state, arriving, cotangent, after, part=WHOLE, halfway=()):
    reread_shapes, _, back_shapes = shapes_of(plan)
    call = Call()
    call.take([state.info], in_smem, pltpu.SMEM)
    call.take([state.table], in_vmem, pltpu.VMEM)
    call.take(state.turned[:1] if part == SECOND else state.turned, in_vmem, pltpu.VMEM)
    staying = () if part == SECOND else state.weights
    call.take(staying, anywhere, pltpu.VMEM)
    call.take(after, anywhere)
    unread = len(staying) + len(after)
    if arriving is not None:
        call.take([arriving], in_vmem, pltpu.VMEM)
    call.take([cotangent], anywhere)
    at_reread = len(call.args)
    call.take(state.reread, anywhere, pltpu.HBM)
    call.give(reread_shapes, anywhere, pltpu.HBM, at_reread)
    used = plan.bwd_uses(tick, part)
    present = [b is not None for b in state.back or (None,) * len(used)]
    call.update(state.back, back_shapes, used)
    narrow = ((plan.frames, plan.features), BF16)
    full = ((plan.frames, plan.features), F32)
    between = [full, narrow, ((4, plan.features), F32)]
    call.take(halfway, anywhere, pltpu.HBM)
    results = between if part == FIRST else [narrow]
    if part == FIRST:
        call.give(results, anywhere, pltpu.HBM)
    else:
        call.give(results, in_vmem, pltpu.VMEM)
    scratch = scratch_of(reread_shapes) + [
        pltpu.VMEM(*narrow),
        pltpu.VMEM((plan.frames, plan.hidden_units), BF16),
        pltpu.VMEM(*full),
        pltpu.VMEM(*full),
        pltpu.VMEM(*narrow),
        pltpu.VMEM(*narrow),
        pltpu.VMEM((plan.frames, 3 * plan.features), BF16),
        pltpu.VMEM((4, plan.features), F32),
        pltpu.SemaphoreType.DMA((16,)),
    ]
    flops = 8 * plan.frames * sum(w.size for w in state.turned)
    body = functools.partial(
        backward_kernel, plan, tick, part, arriving is not None, present, unread
    )
    got = call.run(body, scratch, flops if part == WHOLE else flops // 2)
    got, last = got[: -len(results)], got[-len(results) :]
    back = Back(*updated(state.back, used, got[5:]))
    return state._replace(reread=Reread(*got[:5]), back=back), last


def in_hbm(x):
    return pltpu.with_memory_space_constraint(x, pltpu.HBM)


class Pair(NamedTuple):
    left: Any
    share: Any
    right: Any
    count: int
    left_first: int = 0
    right_first: int = 0


def weight_grad_kernel(pairs, first_column, rows, step, outputs, remade, *refs):
    lefts, rights = refs[: len(pairs)], refs[len(pairs) : len(pairs) + len(pairs) - remade]
    if remade:
        normed_in, weight_in = refs[2 * len(pairs) - remade : 2 * len(pairs) - remade + 2]
        normed, weight_slots, refs = refs[-2], refs[-1], refs[:-2]
    outs = refs[-5 - outputs : -5]
    stage, turned, right_slots, sems, right_sems = refs[-5:]
    frames, width = stage.shape[1:]
    share = width // outputs
    steps = outs[0].shape[1] // step
    core = lax.axis_index("batch") % CORES
    chip = lax.axis_index("batch") // CORES
    chips = lax.axis_size("batch") // CORES
    works = (chip > 0) & (chip < chips - 1) if remade else chip >= 0
    firsts = [sum(p.count for p in pairs[:i]) for i in range(len(pairs))]
    columns = lambda j: pl.ds(pl.multiple_of(j * step, step), step)

    given = list(enumerate(pairs))[: len(rights)]
    remade_from = sum(p.count for _, p in given)

    def right_copies(j, slot):
        copies = [
            pltpu.make_async_copy(
                rights[i].at[pl.ds(p.right_first, p.count), :, columns(j)],
                right_slots.at[slot, pl.ds(firsts[i], p.count)],
                right_sems.at[slot, i],
            )
            for i, p in given
        ]
        if remade:
            copies.append(
                pltpu.make_async_copy(
                    weight_in.at[:, columns(j)], weight_slots.at[slot], right_sems.at[slot, len(given)]
                )
            )
        return copies

    def turn_in(m, at):
        if outputs == 1:
            turned[0, :, at : at + frames] = stage[m].T
            return
        for b in range(width // rows):
            which = jnp.where(core == b % CORES, 0, 1)
            place = (b // CORES) * rows
            block = stage[m, :, b * rows : (b + 1) * rows].T
            turned[which, place : place + rows, at : at + frames] = block

    @pl.when(works)
    def add_up():
        copies = []
        for i, p in enumerate(pairs):
            left = lefts[i] if p.share is None else lefts[i].at[p.share]
            source = left.at[pl.ds(p.left_first, p.count), :, pl.ds(first_column, width)]
            copies.append(
                pltpu.make_async_copy(source, stage.at[pl.ds(firsts[i], p.count)], sems.at[i])
            )
            copies[i].start()
        for copy in right_copies(0, 0):
            copy.start()
        if remade:
            load = pltpu.make_async_copy(normed_in, normed, sems.at[len(pairs)])
            load.start()
        for i, p in enumerate(pairs):
            copies[i].wait()
            for m in range(firsts[i], firsts[i] + p.count):
                turn_in(m, m * frames)
        if remade:
            load.wait()

        def one_step(j, carry):
            slot = j % 2

            @pl.when(j + 1 < steps)
            def next_block():
                for copy in right_copies(j + 1, 1 - slot):
                    copy.start()

            for copy in right_copies(j, slot):
                copy.wait()
            if remade:
                frames_all = normed.shape[0] * frames
                upward = product(normed[...].reshape(frames_all, -1), weight_slots[slot])
                act = gelu_and_slope(upward)[0].astype(BF16)
                right_slots[slot, remade_from:] = act.reshape(-1, frames, step)

            right = right_slots[slot].reshape(-1, step)
            for i in range(outputs):
                outs[i][:, columns(j)] = product(turned[i], right).astype(BF16)
            return carry

        lax.fori_loop(0, steps, one_step, 0)

    if remade:

        @pl.when(jnp.logical_not(works))
        def nothing():
            for out in outs:
                out[...] = jnp.zeros(out.shape, BF16)


def weight_grad(
    pairs, first_column, width, rows, after=(), outputs=1, staying=(), remade=(), sources=()
):
    columns = pairs[0].right.shape[2]
    frames = pairs[0].right.shape[1]
    step = min(columns, 2 * BLOCK // outputs)
    every = [*pairs, *remade]
    micros = sum(p.count for p in every)
    call = Call()
    call.take([p.left for p in every], anywhere)
    call.take([p.right for p in pairs], anywhere)
    call.take(sources, anywhere)
    call.take(after, anywhere)
    call.take(staying, anywhere, pltpu.VMEM)
    call.give([((width // outputs, columns), BF16)] * outputs, in_vmem, pltpu.VMEM)
    scratch = [
        pltpu.VMEM((micros, frames, width), BF16),
        pltpu.VMEM((outputs, width // outputs, micros * frames), BF16),
        pltpu.VMEM((2, micros, frames, step), BF16),
        pltpu.SemaphoreType.DMA((len(every) + 1,)),
        pltpu.SemaphoreType.DMA((2, len(pairs) + 1)),
    ]
    if remade:
        normed, weight = sources
        scratch.append(pltpu.VMEM(normed.shape, BF16))
        scratch.append(pltpu.VMEM((2, weight.shape[0], step), BF16))
    bare = [p._replace(left=None, right=None) for p in every]
    body = functools.partial(
        weight_grad_kernel, bare, first_column, rows, step, outputs, len(remade)
    )
    return call.run(body, scratch, 0, limit=(24 if remade else 14) * 2**20)


class Part(NamedTuple):
    grads: Any
    column: int
    width: int
    result: int
    place: int
    tall: bool


def added_terms(part, grads, rows, index):
    block = pl.ds(pl.multiple_of(index * rows, rows), rows)
    total = None
    for grad in grads:
        term = grad[block, part.column : part.column + part.width].astype(F32)
        total = term if total is None else total + term
    return total


def send_kernel(parts, rows, hop, adds, *refs):
    refs = list(refs)
    grads = [[refs.pop(0) for _ in range(p.grads)] for p in parts]
    came = refs[:2] if adds else None
    sends = refs[-2:]
    chip = lax.axis_index("batch") // CORES
    last = lax.axis_size("batch") // CORES - 1
    places = (jnp.minimum(chip + last - (hop - 1), last), jnp.maximum(chip - last + (hop - 1), 0))
    for d in range(2):
        at = 0
        for part, terms in zip(parts, grads):
            total = added_terms(part, terms, rows, places[d])
            if adds:
                total = total + came[d][:, at : at + part.width].astype(F32)
            sends[d][:, at : at + part.width] = total.astype(BF16)
            at += part.width


def finish_kernel(parts, rows, result_count, *refs):
    refs = list(refs)
    grads = [[refs.pop(0) for _ in range(p.grads)] for p in parts]
    came = refs[:2]
    total, turned, sems = refs[-3:]
    results = refs[-4 - result_count : -4]
    refs[-4][...] = jnp.zeros(refs[-4].shape, F32)
    chip = lax.axis_index("batch") // CORES
    copies, at = [], 0
    for i, (part, terms) in enumerate(zip(parts, grads)):
        own = slice(at, at + part.width)
        total[:, own] = (
            added_terms(part, terms, rows, chip)
            + came[0][:, own].astype(F32)
            + came[1][:, own].astype(F32)
        )
        result = results[part.result]
        if part.tall:
            turned[...] = total[:, own].T
            source, target = turned, result.at[pl.ds(part.place, part.width), :]
        else:
            source = total.at[pl.ds(0, result.shape[0]), pl.ds(at, part.width)]
            target = result.at[:, pl.ds(part.place, part.width)]
        copies.append(pltpu.make_async_copy(source, target, sems.at[i]))
        copies[i].start()
        at += part.width
    for copy in copies:
        copy.wait()


class Piece:
    def __init__(self, parts, first_hop):
        self.parts, self.hop, self.first_hop = parts, first_hop - 1, first_hop
        self.came = None
        self.width = sum(p.width for p in parts)


class Line:
    def __init__(self, exchange, rows, results, before):
        self.chips, self.rows, self.before = exchange.chips, rows, before
        self.results = {}
        self.shapes = results

    def bare(self, piece, names=None):
        parts = [p._replace(grads=len(p.grads)) for p in piece.parts]
        return parts if names is None else [
            p._replace(result=names.index(p.result)) for p in parts
        ]

    def send(self, piece, after=()):
        adds = piece.came is not None
        piece.hop += 1
        shape = (self.rows, piece.width)
        call = Call()
        call.take([g for p in piece.parts for g in p.grads], in_vmem, pltpu.VMEM)
        if adds:
            call.take(piece.came, in_vmem, pltpu.VMEM)
        call.take([self.before, *after], anywhere)
        call.give([(shape, BF16)] * 2, in_vmem, pltpu.VMEM)
        parts = self.bare(piece)
        up, down = call.run(
            functools.partial(send_kernel, parts, self.rows, piece.hop, adds), [], 0
        )
        self.before = up
        edge = piece.first_hop - 1
        last = self.chips - 1
        piece.came = [
            self.moved(up, [z for z in range(last) if edge <= z < piece.hop], 1),
            self.moved(down, [z for z in range(1, last + 1) if edge <= last - z < piece.hop], -1),
        ]

    def moved(self, value, senders, by):
        pairs = [(CORES * z + c, CORES * (z + by) + c) for z in senders for c in range(CORES)]
        return lax.ppermute(value, "batch", pairs)

    def finish(self, piece):
        names = sorted({p.result for p in piece.parts})
        parts = self.bare(piece, names)
        call = Call()
        call.take([g for p in piece.parts for g in p.grads], in_vmem, pltpu.VMEM)
        call.take(piece.came, in_vmem, pltpu.VMEM)
        call.take([self.before], anywhere)
        call.give([(self.shapes[n], F32) for n in names], anywhere, pltpu.HBM)
        call.give([((8, LANES), F32)], in_vmem, pltpu.VMEM)
        shape = (self.rows, piece.width)
        tall = max([p.width for p in parts if p.tall], default=8)
        scratch = [
            pltpu.VMEM(shape, F32),
            pltpu.VMEM((tall, self.rows), F32),
            pltpu.SemaphoreType.DMA((len(parts),)),
        ]
        done = call.run(
            functools.partial(finish_kernel, parts, self.rows, len(names)), scratch, 0
        )
        self.results.update(zip(names, done))
        self.before = done[-1]


def table_gradient(row_grads, codes, blocks):
    chosen = lax.broadcasted_iota(jnp.int32, (blocks, codes.shape[0]), 0) == codes
    return jnp.sum(jnp.where(chosen[:, :, None, None], row_grads[None], 0.0), axis=1)


class Exchange:
    def __init__(self, batch):
        self.batch = batch
        self.chips = batch // CORES
        self.by_hops = batch % CORES == 0 and 2 <= self.chips <= LINE
        self.ends_hand_over = self.by_hops and self.chips == LINE

    def swap(self, x):
        if not self.by_hops:
            return None
        return lax.ppermute(x, "batch", [(b, b ^ 1) for b in range(self.batch)])

    def both(self, x):
        return [in_hbm(x), self.swap(x)]

    def inward(self, x):
        if not self.ends_hand_over:
            return None
        top = self.batch - CORES
        pairs = [(c, CORES + c) for c in range(CORES)]
        pairs += [(top + c, top - CORES + c) for c in range(CORES)]
        return lax.ppermute(x, "batch", pairs)

    def sources(self, x):
        return [in_hbm(x), self.inward(x)] if self.ends_hand_over else [in_hbm(x)]


def sums_by_hops(plan, exchange, back, downs, grad_up, lefts, table_grad, before):
    chips, rows = exchange.chips, plan.rows
    features, hidden_units = plan.features, plan.hidden_units
    core = lax.axis_index("batch") % CORES
    share = features // CORES
    swap = exchange.swap
    table_size = table_grad.shape[0]
    results = [
        (rows, 3 * features),
        (rows, features),
        (rows, hidden_units),
        (hidden_units, rows),
        (table_size, rows),
    ]
    line = Line(exchange, rows, results, before)

    def of(right, first_column):
        rights = exchange.both(right)
        pairs = [Pair(left, i, rights[i], plan.micros) for i, left in enumerate(lefts)]
        (grad,) = weight_grad(pairs, first_column, share, rows, [line.before])
        line.before = grad
        return grad

    up = line.before = grad_up(before)
    ups = Piece([Part([up], 0, hidden_units, 2, 0, False)], 1)
    line.send(ups)
    down, down_given = downs
    first = 2 if exchange.ends_hand_over else 1
    downs = Piece([Part([down, swap(down_given)], 0, hidden_units, 3, 0, True)], first)
    line.send(downs)
    qkv = of(back.grad_packed, 0)
    out = of(back.grad_attn, share)
    norms = table_grad + swap(table_grad)
    norms = norms.reshape(table_size, chips, CORES, rows)
    norms = lax.dynamic_index_in_dim(norms, core, 2, keepdims=False).transpose(1, 0, 2)
    norms = jnp.pad(norms.astype(BF16), ((0, 0), (0, rows - table_size), (0, 0)))
    norms = norms.reshape(chips * rows, rows)
    others = Piece(
        [
            Part([qkv], 0, 3 * features, 0, 0, False),
            Part([out], 0, features, 1, 0, False),
            Part([norms], 0, rows, 4, 0, False),
        ],
        1,
    )
    order = [downs, others, ups, others, ups, others]
    gone = [ups.came, downs.came]
    pieces = [ups, downs, others]
    for piece in order:
        if piece.hop < chips - 1:
            line.send(piece, gone.pop(0))
            gone.append(piece.came)
        for done in pieces[:]:
            if done.hop == chips - 1 and done is not piece:
                line.finish(done)
                pieces.remove(done)
    for piece in pieces:
        line.finish(piece)
    return [line.results[i] for i in range(len(results))]


def sums_by_scatter(plan, kept, back, table_grad):
    features = plan.features
    share = features // CORES
    core = lax.axis_index("batch") % CORES

    def local(lefts, rights, column):
        pairs = [Pair(left, None, right, left.shape[0]) for left, right in zip(lefts, rights)]
        if column is None:
            mine, other = weight_grad(pairs, 0, features, plan.rows, outputs=2)
        else:
            (left,), (right,) = lefts, rights
            mine, other = [
                weight_grad(
                    [Pair(left, i, right, left.shape[1])], column, share, plan.rows
                )[0]
                for i in range(CORES)
            ]
        even, odd = jnp.where(core == 0, mine, other), jnp.where(core == 0, other, mine)
        blocks = [x.reshape(-1, 1, plan.rows, x.shape[1]) for x in (even, odd)]
        return jnp.concatenate(blocks, axis=1).reshape(features, -1)

    def scattered(x, dimension):
        return lax.psum_scatter(
            x, "batch", scatter_dimension=dimension, tiled=True
        ).astype(F32)

    grad_y = [back.y_early, back.y_late, back.y_last]
    down = local([jnp.concatenate(grad_y, axis=0)], [kept.act], None)
    grad_up = jnp.concatenate([back.up_early, back.up_last], axis=0)
    return (
        scattered(local([kept.left], [back.grad_packed], 0), 0),
        scattered(local([kept.left], [back.grad_attn], share), 0),
        scattered(local([kept.left], [grad_up], 2 * share), 0),
        scattered(down, 0).T,
        scattered(table_grad, 1),
    )


def per_device(
    frames_in, cotangent, qkv_weight, out_weight, up_weight, down_weight, norm_table, lengths,
    codebooks,
):
    sections = lax.axis_size("section")
    batch = lax.axis_size("batch")
    section = lax.axis_index("section")
    micros = lengths.shape[0]
    tokens, features = frames_in.shape
    frames = tokens // micros
    plan = Plan(
        sections, micros, frames, features, up_weight.shape[2], max(features // batch, LANES)
    )
    frames_all = frames_in.reshape(micros, frames, features)
    cot_all = cotangent.reshape(micros, frames, features)

    state = State(
        numbers=[lengths, codebooks],
        info=None,
        table=norm_table[0],
        weights=Weights(qkv_weight[0], out_weight[0], up_weight[0], down_weight[0]),
    )
    exchange = Exchange(batch)

    share = features // CORES

    def down_pairs(grad_ys, act):
        firsts = [span[0] for span in plan.y_spans()]
        return [Pair(y, None, act, y.shape[0], 0, at) for y, at in zip(grad_ys, firsts)]

    def up_pairs(grad_up, first):
        count = grad_up[0].shape[0]
        return [
            Pair(left, i, g, count, first, 0) for i, (left, g) in enumerate(zip(lefts, grad_up))
        ]

    before_bwd = [[] for _ in range(plan.ticks())]
    incoming = arriving = None
    working = lambda micro: 0 <= micro < micros
    for tick in range(plan.ticks()):
        sent = returned = None
        if tick < plan.fwd_ticks():
            state, output = run_forward(plan, tick, state, incoming, frames_all)
            onward = [
                (s, s + 1) for s in range(sections - 1) if working(plan.fwd_id(tick, s))
            ]
            if onward:
                sent = lax.ppermute(output, "section", onward)
        if tick >= sections - 1:
            late = tick == plan.ticks() - 1
            state, output = run_backward(
                plan, tick, state, arriving, cot_all, before_bwd[tick], FIRST if late else WHOLE
            )
            if late:
                after = []
                if exchange.by_hops:
                    y_last = exchange.sources(state.back.y_last)
                    up_last = exchange.both(state.back.up_last)
                    sides = list(zip(y_early, y_late, y_last))
                    pairs = down_pairs(sides[0], in_hbm(state.kept.act))
                    remade, sources = (), ()
                    if exchange.ends_hand_over:
                        remade = down_pairs(sides[1], None)
                        sources = (second[1], up_weight[0])
                    down = weight_grad(
                        pairs, 0, features, plan.rows, output[:1], 2, state.turned[:1],
                        remade, sources,
                    )
                    after = up_early[1:] + down
                state, output = run_backward(
                    plan, tick, state, arriving, cot_all, after, SECOND, output
                )
            output = output[0]
            backward = [
                (s, s - 1) for s in range(1, sections) if working(plan.bwd_id(tick, s))
            ]
            if backward:
                returned = lax.ppermute(output, "section", backward)
        incoming, arriving = sent, returned
        if exchange.by_hops:
            if tick == plan.fwd_ticks() - 1:
                lefts = exchange.both(state.kept.left)
                before_bwd[tick + 1] += lefts[1:]
                second = exchange.sources(state.kept.second)
                before_bwd[tick + 2] += second[1:]
            if tick == plan.y_spans()[0][1] + 2 * sections - 3:
                y_early = exchange.sources(state.back.y_early)
                before_bwd[plan.ticks() - 1] += y_early[1:]
            if tick == plan.ticks() - 2:
                y_late = exchange.sources(state.back.y_late)
                up_early = exchange.both(state.back.up_early)

    blocks = norm_table.shape[1] // 4
    codes = codebooks * (section % 2)
    table_grad = table_gradient(state.back.row_grads, codes, blocks).reshape(norm_table.shape[1:])
    if exchange.by_hops:
        def grad_up(before):
            pairs = up_pairs(up_early, 0) + up_pairs(up_last, micros - 1)
            return weight_grad(pairs, 2 * share, share, plan.rows, [before])[0]

        sums = sums_by_hops(
            plan, exchange, state.back, down, grad_up, lefts, table_grad, output
        )
    else:
        sums = sums_by_scatter(plan, state.kept, state.back, table_grad)
    return (
        state.kept.layer_out.reshape(1, tokens, features),
        state.back.grad_in.reshape(1, tokens, features),
    ) + tuple(x[None] for x in sums)


def solution(mesh):
    section, batch = mesh.axis_names
    over_batch = P(batch)
    over_section = P(section)
    both = P(section, batch, None)
    columns = P(section, None, batch)
    in_specs = (over_batch,) * 2 + (over_section,) * 5 + (over_batch,) * 2
    out_specs = (both,) * 5 + (columns,) * 2
    return jax.shard_map(
        per_device, mesh=mesh, in_specs=in_specs, out_specs=out_specs, check_vma=False
    )
```

```python
import functools
from typing import Any, NamedTuple

import jax
import jax.numpy as jnp
from jax import lax
from jax.experimental import pallas as pl
from jax.experimental.pallas import tpu as pltpu
from jax.sharding import PartitionSpec as P

HEADS = 16
GROUP = 4
BLOCK = 512
LANES = 128
CORES = 2
VMEM_LIMIT = 14 * 2**20
WHOLE, FIRST, SECOND = 0, 1, 2
LINE = 4

epsilon = 1e-05
masked_score = -1e30
BF16 = jnp.bfloat16
F32 = jnp.float32

in_vmem = pl.BlockSpec(memory_space=pltpu.VMEM)
in_smem = pl.BlockSpec(memory_space=pltpu.SMEM)
anywhere = pl.BlockSpec(memory_space=pl.ANY)


class Weights(NamedTuple):
    qkv: Any
    out: Any
    up: Any
    down: Any


class Reread(NamedTuple):
    entry: Any
    packed: Any
    probs: Any
    hidden: Any
    slope: Any


class Kept(NamedTuple):
    layer_out: Any
    left: Any
    second: Any
    act: Any


class Back(NamedTuple):
    grad_in: Any
    y_early: Any
    y_late: Any
    y_last: Any
    up_early: Any
    up_last: Any
    grad_attn: Any
    grad_packed: Any
    row_grads: Any


def product(left, right):
    return lax.dot_general(left, right, (((1,), (0,)), ((), ())), preferred_element_type=F32)


def product_last(left, right):
    return lax.dot_general(left, right, (((1,), (1,)), ((), ())), preferred_element_type=F32)


def product_first(left, right):
    return lax.dot_general(left, right, (((0,), (0,)), ((), ())), preferred_element_type=F32)


def normalize(values):
    centre = values - jnp.mean(values, axis=-1, keepdims=True)
    reciprocal = lax.rsqrt(jnp.mean(centre * centre, axis=-1, keepdims=True) + epsilon)
    return centre * reciprocal, reciprocal


def normalize_back(gradient, normal_part, reciprocal, gain_row):
    scaled = gradient * (1.0 + gain_row)
    centred = scaled - jnp.mean(scaled, axis=-1, keepdims=True)
    return reciprocal * (
        centred - normal_part * jnp.mean(scaled * normal_part, axis=-1, keepdims=True)
    )


def gelu_and_slope(u):
    root = 0.7978845608028654
    square = u * u
    bent = jnp.tanh(root * u * (1.0 + 0.044715 * square))
    half = 0.5 * (1.0 + bent)
    slope = half + 0.5 * u * (1.0 - bent * bent) * (root * (1.0 + 3 * 0.044715 * square))
    return u * half, slope


def stacked_heads(block, head_size):
    owner = lax.broadcasted_iota(jnp.int32, block.shape, 1) // head_size
    zero = jnp.zeros_like(block)
    return jnp.concatenate([jnp.where(owner == h, block, zero) for h in range(GROUP)], axis=0)


def beside(stack, frames):
    return jnp.concatenate([stack[h * frames : (h + 1) * frames] for h in range(GROUP)], axis=1)


def table_rows(table, code):
    pair = table[pl.ds(pl.multiple_of((code // 2) * 8, 8), 8), :]
    return jnp.where(code % 2 == 1, pair[4:8], pair[0:4])


class Saver:
    def __init__(self, sems, base):
        self.sems, self.base, self.pending = sems, base, []

    def __call__(self, source, target):
        copy = pltpu.make_async_copy(source, target, self.sems.at[self.base + len(self.pending)])
        copy.start()
        self.pending.append(copy)

    def spread(self, source, buffers, spans, slot):
        sem = self.sems.at[self.base + len(self.pending)]
        copies = []
        for buffer, (first, end) in zip(buffers, spans):
            if buffer is None:
                continue
            place = jnp.clip(slot - first, 0, end - first - 1)
            copies.append(pltpu.make_async_copy(source, buffer.at[place], sem))
            pl.when((slot >= first) & (slot < end))(copies[-1].start)
        self.pending.append(copies[0])

    def wait(self):
        for copy in self.pending:
            copy.wait()


def turn(source, target, row0, col0, side_by, strips, sems, base):
    slots, side, _ = strips.shape
    count = side_by // side

    def strip(i):
        c = pl.multiple_of(col0 + i * side, side)
        return pltpu.make_async_copy(
            strips.at[i % slots],
            target.at[pl.ds(c, side), pl.ds(row0, side_by)],
            sems.at[base + i % slots],
        )

    def one_strip(i, carry):
        @pl.when(i >= slots)
        def slot_is_free():
            strip(i - slots).wait()

        c = pl.multiple_of(col0 + i * side, side)
        strips[i % slots] = source[row0 : row0 + side_by, pl.ds(c, side)].T
        strip(i).start()
        return carry

    lax.fori_loop(0, count, one_strip, 0)
    for i in range(count - slots, count):
        strip(i).wait()


class Plan(NamedTuple):
    sections: int
    micros: int
    frames: int
    features: int
    hidden_units: int
    rows: int

    def fwd_ticks(self):
        return self.micros + self.sections - 1

    def ticks(self):
        return self.micros + 2 * (self.sections - 1)

    def y_spans(self):
        half = self.micros // 2
        return (0, half), (half, self.micros - 1), (self.micros - 1, self.micros)

    def up_spans(self):
        return (0, self.micros - 1), (self.micros - 1, self.micros)

    def bwd_reaches(self, tick):
        low, high = tick - 2 * (self.sections - 1), tick - (self.sections - 1)
        grad_y = tuple(low < end and high >= first for first, end in self.y_spans())
        grad_up = tuple(low < end and high >= first for first, end in self.up_spans())
        return (True,) + grad_y + grad_up + (True,) * 3

    def bwd_uses(self, tick, part):
        first = (False,) + (True,) * 6 + (False, False)
        halves = {WHOLE: (True,) * 9, FIRST: first, SECOND: tuple(not f for f in first)}
        return tuple(r and h for r, h in zip(self.bwd_reaches(tick), halves[part]))

    def fwd_id(self, tick, section):
        return tick - section

    def bwd_id(self, tick, section):
        return tick - 2 * (self.sections - 1) + section


def forward_kernel(plan, tick, has_incoming, loads_weights, *refs):
    refs = list(refs)
    take = lambda n: [refs.pop(0) for _ in range(n)]
    if loads_weights:
        lengths, codebooks, given_table = take(3)
        given = Weights(*take(4))
    else:
        info, table = take(2)
        weight = Weights(*take(4))
        take(4)
    incoming = take(1)[0] if has_incoming else None
    (frames_in,) = take(1)
    if loads_weights:
        info, table = take(2)
        weight = Weights(*take(4))
    else:
        take(len(Reread._fields) + len(Kept._fields))
    turned = Weights(*take(4))
    reread = Reread(*take(5))
    kept = Kept(*take(4))
    (outgoing,) = take(1)
    entry, packed, probs, hidden, slope, normed, left, attended, act, strips, sems = refs

    micros, frames, features, hidden_units, rows_kept = plan[1:]
    head_size = features // HEADS
    group_width = GROUP * head_size
    section = lax.axis_index("section")
    core = lax.axis_index("batch") % CORES
    is_nar = section % 2
    micro = plan.fwd_id(tick, section)
    active = (micro >= 0) & (micro < micros)
    slot = jnp.clip(micro, 0, micros - 1)

    loads = []
    if loads_weights:
        for i in range(micros):
            info[i] = lengths[i]
            info[micros + i] = codebooks[i]
        pairs = [(given_table, table)] + list(zip(given, weight))
        for i, (source, target) in enumerate(pairs):
            loads.append(pltpu.make_async_copy(source, target, sems.at[i]))
        loads[0].start()

        @pl.when(core == 1)
        def later():
            loads[4].start()
            loads[4].wait()

        loads[1].start()
    base = len(loads)

    def ready(i):
        if not loads_weights:
            return
        if i == 4:
            pl.when(core != 1)(loads[4].wait)
            return
        loads[i].wait()
        if i == 1:
            loads[2].start()
            loads[3].start()
        if i == 2:
            pl.when(core != 1)(loads[4].start)

    @pl.when(active)
    def forward():
        save = Saver(sems, base)
        length = info[slot]
        code = info[micros + slot] * is_nar

        def own_input():
            pltpu.sync_copy(frames_in.at[slot], entry)

        if has_incoming:
            pl.when(section == 0)(own_input)

            @pl.when(section != 0)
            def passed_input():
                entry[...] = incoming[...]

        else:
            own_input()

        save(entry, reread.entry.at[slot])
        share = features // CORES

        def share_columns(source, first):
            for b in range(features // rows_kept):
                at = first + (b // CORES) * rows_kept
                left[b % CORES, :, at : at + rows_kept] = source[
                    :, b * rows_kept : (b + 1) * rows_kept
                ]

        ready(0)
        rows = table_rows(table, code)
        residual = entry[...].astype(F32)
        normal_one, _ = normalize(residual)
        normed[...] = (normal_one * (1.0 + rows[0:1]) + rows[1:2]).astype(BF16)
        share_columns(normed, 0)
        ready(1)
        for j in range(0, 3 * features, BLOCK):
            packed[:, j : j + BLOCK] = product(normed[...], weight.qkv[:, j : j + BLOCK]).astype(
                BF16
            )
        save(packed, reread.packed.at[slot])
        tall = (GROUP * frames, frames)
        query_ids = lax.rem(lax.broadcasted_iota(jnp.int32, tall, 0), frames)
        key_ids = lax.broadcasted_iota(jnp.int32, tall, 1)
        allowed = (key_ids < length) & (key_ids <= query_ids + is_nar * frames)
        inv_root = head_size ** (-0.5)
        for g in range(HEADS // GROUP):
            lo, hi = g * group_width, (g + 1) * group_width
            queries = stacked_heads(packed[:, lo:hi], head_size)
            keys = packed[:, features + lo : features + hi]
            values = stacked_heads(packed[:, 2 * features + lo : 2 * features + hi], head_size)
            scores = jnp.where(allowed, product_last(queries, keys) * inv_root, masked_score)
            exp_scores = jnp.exp(scores - jnp.max(scores, axis=-1, keepdims=True))
            total = jnp.sum(exp_scores, axis=-1, keepdims=True)
            group_probs = (exp_scores * (1.0 / total)).astype(BF16)
            probs[g * GROUP * frames : (g + 1) * GROUP * frames, :] = group_probs
            attended[:, lo:hi] = product(beside(group_probs, frames), values).astype(BF16)
        save(probs, reread.probs.at[slot])
        share_columns(attended, share)
        ready(2)
        for j in range(0, features, BLOCK):
            hidden[:, j : j + BLOCK] = residual[:, j : j + BLOCK] + product(
                attended[...], weight.out[:, j : j + BLOCK]
            )
        save(hidden, reread.hidden.at[slot])
        normal_two, _ = normalize(hidden[...])
        normed[...] = (normal_two * (1.0 + rows[2:3]) + rows[3:4]).astype(BF16)
        share_columns(normed, 2 * share)
        save(normed, kept.second.at[slot])
        save(left.at[core], kept.left.at[0, slot])
        save(left.at[1 - core], kept.left.at[1, slot])
        ready(3)
        for j in range(0, hidden_units, BLOCK):
            value, gradient = gelu_and_slope(product(normed[...], weight.up[:, j : j + BLOCK]))
            act[:, j : j + BLOCK] = value.astype(BF16)
            slope[:, j : j + BLOCK] = gradient.astype(BF16)
            if (j + BLOCK) % (hidden_units // 2) == 0:
                done = pl.ds(j + BLOCK - hidden_units // 2, hidden_units // 2)
                save(slope.at[:, done], reread.slope.at[slot, :, done])
                save(act.at[:, done], kept.act.at[slot, :, done])
        ready(4)
        for j in range(0, features, BLOCK):
            outgoing[:, j : j + BLOCK] = (
                hidden[:, j : j + BLOCK] + product(act[...], weight.down[:, j : j + BLOCK])
            ).astype(BF16)
        save(outgoing, kept.layer_out.at[slot])
        save.wait()

    units = []
    for source, target in zip(weight, turned):
        total_rows, total_cols = source.shape
        for r in range(0, total_rows, features):
            for c in range(0, total_cols, features):
                units.append((source, target, r, c))
    cut = len(units) // 3
    pieces = (units[:cut], units[cut:])
    piece = jnp.where(micro < 0, tick, micro - micros + section)

    @pl.when(jnp.logical_not(active))
    def wait_for_weights():
        for i in range(base):
            ready(i)

    for k in range(len(pieces)):

        @pl.when(jnp.logical_not(active) & (piece == k))
        def one_piece(k=k):
            for source, target, r, c in pieces[k]:
                turn(source, target, r, c, features, strips, sems, base)


def backward_kernel(plan, tick, part, has_arriving, present, unread, *refs):
    refs = list(refs)
    take = lambda n: [refs.pop(0) for _ in range(n)]
    info, table = take(2)
    turned = Weights(*(take(1) + [None] * 3 if part == SECOND else take(4)))
    take(unread)
    arriving = take(1)[0] if has_arriving else None
    (cotangent,) = take(1)
    take(len(Reread._fields))
    used = plan.bwd_uses(tick, part)
    take(sum(u and p for u, p in zip(used, present)))
    halfway = take(3) if part == SECOND else None
    reread = Reread(*take(5))
    back = Back(*[take(1)[0] if u else None for u in used])
    if part == FIRST:
        halfway = take(3)
    else:
        (returning,) = take(1)
    (entry, packed, probs, hidden, slope, grad_y, grad_up, wide, grad_hidden, grad_attn, mixed,
     grad_packed, row_grads, sems) = refs

    micros, frames, features, hidden_units, _ = plan[1:]
    head_size = features // HEADS
    group_width = GROUP * head_size
    section = lax.axis_index("section")
    is_nar = section % 2
    micro = plan.bwd_id(tick, section)
    active = (micro >= 0) & (micro < micros)
    slot = jnp.clip(micro, 0, micros - 1)

    def start_fetches(wanted):
        fetches = []
        for i, target in enumerate((entry, packed, probs, hidden, slope)):
            fetches.append(pltpu.make_async_copy(reread[i].at[slot], target, sems.at[i]))
        for i in (4, 3, 1, 2, 0):
            if i in wanted:
                fetches[i].start()
        return fetches

    def first_half():
        length = info[slot]
        code = info[micros + slot] * is_nar
        fetches = start_fetches((3, 4) if part == FIRST else range(5))
        save = Saver(sems, len(fetches))

        def own_cotangent():
            pltpu.sync_copy(cotangent.at[slot], grad_y)
            live = lax.broadcasted_iota(jnp.int32, (frames, features), 0) < length
            grad_y[...] = jnp.where(live, grad_y[...], jnp.zeros((frames, features), BF16))

        if has_arriving:
            pl.when(section == plan.sections - 1)(own_cotangent)

            @pl.when(section != plan.sections - 1)
            def passed_gradient():
                grad_y[...] = arriving[...]

        else:
            own_cotangent()

        save.spread(grad_y, back[1:4], plan.y_spans(), slot)
        rows = table_rows(table, code)
        fetches[4].wait()
        for j in range(0, hidden_units, BLOCK):
            grad_act = product(grad_y[...], turned.down[:, j : j + BLOCK])
            grad_up[:, j : j + BLOCK] = (
                grad_act * slope[:, j : j + BLOCK].astype(F32)
            ).astype(BF16)
        save.spread(grad_up, (back.up_early, back.up_last), plan.up_spans(), slot)
        for j in range(0, features, BLOCK):
            wide[:, j : j + BLOCK] = product(grad_up[...], turned.up[:, j : j + BLOCK])
        fetches[3].wait()
        normal_two, recip_two = normalize(hidden[...])
        grad_two = wide[...]
        row_grads[2:3, :] = jnp.sum(grad_two * normal_two, axis=0, keepdims=True)
        row_grads[3:4, :] = jnp.sum(grad_two, axis=0, keepdims=True)
        grad_hidden[...] = grad_y[...].astype(F32) + normalize_back(
            grad_two, normal_two, recip_two, rows[2:3]
        )
        grad_attn[...] = grad_hidden[...].astype(BF16)
        save(grad_attn, back.grad_attn.at[slot])
        for j in range(0, features, BLOCK):
            mixed[:, j : j + BLOCK] = product(
                grad_attn[...], turned.out[:, j : j + BLOCK]
            ).astype(BF16)
        return fetches, save

    def second_half(fetches, save):
        code = info[micros + slot] * is_nar
        rows = table_rows(table, code)
        fetches[1].wait()
        fetches[2].wait()
        inv_root = head_size ** (-0.5)
        for g in range(HEADS // GROUP):
            lo, hi = g * group_width, (g + 1) * group_width
            queries = stacked_heads(packed[:, lo:hi], head_size)
            keys = stacked_heads(packed[:, features + lo : features + hi], head_size)
            values = packed[:, 2 * features + lo : 2 * features + hi]
            group_mixed = stacked_heads(mixed[:, lo:hi], head_size)
            group_probs = probs[g * GROUP * frames : (g + 1) * GROUP * frames, :]
            wide_probs = group_probs.astype(F32)
            grad_probs = product_last(group_mixed, values)
            inner = jnp.sum(wide_probs * grad_probs, axis=-1, keepdims=True)
            grad_scores = (wide_probs * (grad_probs - inner)).astype(BF16)
            grad_packed[:, lo:hi] = (
                product(beside(grad_scores, frames), keys) * inv_root
            ).astype(BF16)
            grad_packed[:, features + lo : features + hi] = (
                product_first(grad_scores, queries) * inv_root
            ).astype(BF16)
            grad_packed[:, 2 * features + lo : 2 * features + hi] = product_first(
                group_probs, group_mixed
            ).astype(BF16)
        save(grad_packed, back.grad_packed.at[slot])
        for j in range(0, features, BLOCK):
            wide[:, j : j + BLOCK] = product(grad_packed[...], turned.qkv[:, j : j + BLOCK])
        fetches[0].wait()
        normal_one, recip_one = normalize(entry[...].astype(F32))
        grad_one = wide[...]
        row_grads[0:1, :] = jnp.sum(grad_one * normal_one, axis=0, keepdims=True)
        row_grads[1:2, :] = jnp.sum(grad_one, axis=0, keepdims=True)
        save(row_grads, back.row_grads.at[slot])
        returning[...] = (
            grad_hidden[...] + normalize_back(grad_one, normal_one, recip_one, rows[0:1])
        ).astype(BF16)
        save(returning, back.grad_in.at[slot])
        save.wait()

    @pl.when(active)
    def backward():
        if part == SECOND:
            fetches = start_fetches((0, 1, 2))
            load = Saver(sems, 5)
            for source, target in zip(halfway, (grad_hidden, mixed, row_grads)):
                load(source, target)
            load.wait()
            second_half(fetches, Saver(sems, 5))
            return
        fetches, save = first_half()
        if part == FIRST:
            for source, target in zip((grad_hidden, mixed, row_grads), halfway):
                save(source, target)
            save.wait()
        else:
            second_half(fetches, save)


def shapes_of(plan):
    micros, frames, features, hidden_units, _ = plan[1:]
    own = (micros, frames)
    reread = Reread(
        entry=(own + (features,), BF16),
        packed=(own + (3 * features,), BF16),
        probs=((micros, HEADS * frames, frames), BF16),
        hidden=(own + (features,), F32),
        slope=(own + (hidden_units,), BF16),
    )
    def buffers(spans, columns):
        return [((end - first, frames, columns), BF16) for first, end in spans]

    left = ((CORES,) + own + (3 * features // CORES,), BF16)
    wide = (own + (features,), BF16)
    kept = Kept(wide, left, wide, (own + (hidden_units,), BF16))
    back = Back(
        wide,
        *buffers(plan.y_spans(), features),
        *buffers(plan.up_spans(), hidden_units),
        grad_attn=wide,
        grad_packed=(own + (3 * features,), BF16),
        row_grads=((micros, 4, features), F32),
    )
    return reread, kept, back


def scratch_of(shapes):
    return [pltpu.VMEM(shape[1:], dtype) for shape, dtype in shapes]


class Call:
    def __init__(self):
        self.args, self.in_specs, self.out_shape, self.out_specs = [], [], [], []
        self.aliases = {}

    def take(self, values, spec, space=None):
        for value in values:
            if space is not None:
                value = pltpu.with_memory_space_constraint(value, space)
            self.args.append(value)
            self.in_specs.append(spec)

    def give(self, shapes, spec, space, updates=None):
        for i, (shape, dtype) in enumerate(shapes):
            if updates is not None:
                self.aliases[updates + i] = len(self.out_shape)
            self.out_shape.append(space(shape, dtype))
            self.out_specs.append(spec)

    def update(self, arrays, shapes, used):
        arrays = arrays or (None,) * len(shapes)
        for array, shape, use in zip(arrays, shapes, used):
            if use and array is not None:
                self.take([array], anywhere, pltpu.HBM)
                self.give([shape], anywhere, pltpu.HBM, len(self.args) - 1)
            elif use:
                self.give([shape], anywhere, pltpu.HBM)

    def run(self, body, scratch, flops, limit=VMEM_LIMIT):
        return list(
            pl.pallas_call(
                body,
                out_shape=self.out_shape,
                in_specs=self.in_specs,
                out_specs=self.out_specs,
                scratch_shapes=scratch,
                input_output_aliases=self.aliases,
                compiler_params=pltpu.CompilerParams(vmem_limit_bytes=limit),
                cost_estimate=pl.CostEstimate(
                    flops=flops, bytes_accessed=0, transcendentals=0
                ),
            )(*self.args)
        )


def updated(old, used, new):
    new = list(new)
    old = old or (None,) * len(used)
    return [new.pop(0) if u else o for o, u in zip(old, used)]


def like(arrays):
    return [(x.shape, x.dtype) for x in arrays]


class State(NamedTuple):
    numbers: Any
    info: Any
    table: Any
    weights: Any
    turned: Any = None
    reread: Any = None
    kept: Any = None
    back: Any = None


def run_forward(plan, tick, state, incoming, frames_in):
    reread_shapes, kept_shapes, _ = shapes_of(plan)
    first = state.turned is None
    at_turned = at_kept = None
    call = Call()
    if first:
        call.take(state.numbers, in_smem)
        call.take([state.table], anywhere)
        call.take(state.weights, anywhere)
    else:
        call.take([state.info], in_smem, pltpu.SMEM)
        call.take([state.table], in_vmem, pltpu.VMEM)
        call.take(state.weights, in_vmem, pltpu.VMEM)
        at_turned = len(call.args)
        call.take(state.turned, anywhere, pltpu.VMEM)
    if incoming is not None:
        call.take([incoming], in_vmem, pltpu.VMEM)
    call.take([frames_in], anywhere)
    if first:
        call.give([((2 * plan.micros,), jnp.int32)], in_smem, pltpu.SMEM)
        call.give(like([state.table]), in_vmem, pltpu.VMEM)
        call.give(like(state.weights), in_vmem, pltpu.VMEM)
    else:
        at_kept = len(call.args)
        call.take(state.reread + state.kept, anywhere, pltpu.HBM)
    call.give([(w.shape[::-1], BF16) for w in state.weights], anywhere, pltpu.VMEM, at_turned)
    call.give(reread_shapes + kept_shapes, anywhere, pltpu.HBM, at_kept)
    call.give([((plan.frames, plan.features), BF16)], in_vmem, pltpu.VMEM)
    scratch = scratch_of(reread_shapes) + [
        pltpu.VMEM((plan.frames, plan.features), BF16),
        pltpu.VMEM((CORES, plan.frames, 3 * plan.features // CORES), BF16),
        pltpu.VMEM((plan.frames, plan.features), BF16),
        pltpu.VMEM((plan.frames, plan.hidden_units), BF16),
        pltpu.VMEM((2, 256, plan.features), BF16),
        pltpu.SemaphoreType.DMA((24,)),
    ]
    flops = 8 * plan.frames * sum(w.size for w in state.weights)
    body = functools.partial(forward_kernel, plan, tick, incoming is not None, first)
    got = call.run(body, scratch, flops)
    if first:
        state = state._replace(info=got[0], table=got[1], weights=Weights(*got[2:6]))
        got = got[6:]
    kept = Kept(*got[9:13])
    return state._replace(turned=Weights(*got[:4]), reread=Reread(*got[4:9]), kept=kept), got[-1]


def run_backward(plan, tick, state, arriving, cotangent, after, part=WHOLE, halfway=()):
    reread_shapes, _, back_shapes = shapes_of(plan)
    call = Call()
    call.take([state.info], in_smem, pltpu.SMEM)
    call.take([state.table], in_vmem, pltpu.VMEM)
    call.take(state.turned[:1] if part == SECOND else state.turned, in_vmem, pltpu.VMEM)
    staying = () if part == SECOND else state.weights
    call.take(staying, anywhere, pltpu.VMEM)
    call.take(after, anywhere)
    unread = len(staying) + len(after)
    if arriving is not None:
        call.take([arriving], in_vmem, pltpu.VMEM)
    call.take([cotangent], anywhere)
    at_reread = len(call.args)
    call.take(state.reread, anywhere, pltpu.HBM)
    call.give(reread_shapes, anywhere, pltpu.HBM, at_reread)
    used = plan.bwd_uses(tick, part)
    present = [b is not None for b in state.back or (None,) * len(used)]
    call.update(state.back, back_shapes, used)
    narrow = ((plan.frames, plan.features), BF16)
    full = ((plan.frames, plan.features), F32)
    between = [full, narrow, ((4, plan.features), F32)]
    call.take(halfway, anywhere, pltpu.HBM)
    results = between if part == FIRST else [narrow]
    if part == FIRST:
        call.give(results, anywhere, pltpu.HBM)
    else:
        call.give(results, in_vmem, pltpu.VMEM)
    scratch = scratch_of(reread_shapes) + [
        pltpu.VMEM(*narrow),
        pltpu.VMEM((plan.frames, plan.hidden_units), BF16),
        pltpu.VMEM(*full),
        pltpu.VMEM(*full),
        pltpu.VMEM(*narrow),
        pltpu.VMEM(*narrow),
        pltpu.VMEM((plan.frames, 3 * plan.features), BF16),
        pltpu.VMEM((4, plan.features), F32),
        pltpu.SemaphoreType.DMA((16,)),
    ]
    flops = 8 * plan.frames * sum(w.size for w in state.turned)
    body = functools.partial(
        backward_kernel, plan, tick, part, arriving is not None, present, unread
    )
    got = call.run(body, scratch, flops if part == WHOLE else flops // 2)
    got, last = got[: -len(results)], got[-len(results) :]
    back = Back(*updated(state.back, used, got[5:]))
    return state._replace(reread=Reread(*got[:5]), back=back), last


def in_hbm(x):
    return pltpu.with_memory_space_constraint(x, pltpu.HBM)


class Pair(NamedTuple):
    left: Any
    share: Any
    right: Any
    count: int
    left_first: int = 0
    right_first: int = 0


def weight_grad_kernel(pairs, first_column, rows, step, outputs, remade, *refs):
    lefts, rights = refs[: len(pairs)], refs[len(pairs) : len(pairs) + len(pairs) - remade]
    if remade:
        normed_in, weight_in = refs[2 * len(pairs) - remade : 2 * len(pairs) - remade + 2]
        normed, weight_slots, refs = refs[-2], refs[-1], refs[:-2]
    outs = refs[-5 - outputs : -5]
    stage, turned, right_slots, sems, right_sems = refs[-5:]
    frames, width = stage.shape[1:]
    share = width // outputs
    steps = outs[0].shape[1] // step
    core = lax.axis_index("batch") % CORES
    chip = lax.axis_index("batch") // CORES
    chips = lax.axis_size("batch") // CORES
    works = (chip > 0) & (chip < chips - 1) if remade else chip >= 0
    firsts = [sum(p.count for p in pairs[:i]) for i in range(len(pairs))]
    columns = lambda j: pl.ds(pl.multiple_of(j * step, step), step)

    given = list(enumerate(pairs))[: len(rights)]
    remade_from = sum(p.count for _, p in given)

    def right_copies(j, slot):
        copies = [
            pltpu.make_async_copy(
                rights[i].at[pl.ds(p.right_first, p.count), :, columns(j)],
                right_slots.at[slot, pl.ds(firsts[i], p.count)],
                right_sems.at[slot, i],
            )
            for i, p in given
        ]
        if remade:
            copies.append(
                pltpu.make_async_copy(
                    weight_in.at[:, columns(j)], weight_slots.at[slot], right_sems.at[slot, len(given)]
                )
            )
        return copies

    def turn_in(m, at):
        if outputs == 1:
            turned[0, :, at : at + frames] = stage[m].T
            return
        for b in range(width // rows):
            which = jnp.where(core == b % CORES, 0, 1)
            place = (b // CORES) * rows
            block = stage[m, :, b * rows : (b + 1) * rows].T
            turned[which, place : place + rows, at : at + frames] = block

    @pl.when(works)
    def add_up():
        copies = []
        for i, p in enumerate(pairs):
            left = lefts[i] if p.share is None else lefts[i].at[p.share]
            source = left.at[pl.ds(p.left_first, p.count), :, pl.ds(first_column, width)]
            copies.append(
                pltpu.make_async_copy(source, stage.at[pl.ds(firsts[i], p.count)], sems.at[i])
            )
            copies[i].start()
        for copy in right_copies(0, 0):
            copy.start()
        if remade:
            load = pltpu.make_async_copy(normed_in, normed, sems.at[len(pairs)])
            load.start()
        for i, p in enumerate(pairs):
            copies[i].wait()
            for m in range(firsts[i], firsts[i] + p.count):
                turn_in(m, m * frames)
        if remade:
            load.wait()

        def fill(j, slot):
            for copy in right_copies(j, slot):
                copy.wait()
            if remade:
                rows = normed[...].reshape(normed.shape[0] * frames, -1)
                act = gelu_and_slope(product(rows, weight_slots[slot]))[0].astype(BF16)
                right_slots[slot, remade_from:] = act.reshape(-1, frames, step)

        def add(j, slot):
            right = right_slots[slot].reshape(-1, step)
            for i in range(outputs):
                outs[i][:, columns(j)] = product(turned[i], right).astype(BF16)

        def start(j, slot):
            for copy in right_copies(j, slot):
                copy.start()

        def two_steps(i, carry):
            j = 2 * i
            fill(j + 1, 1)
            add(j, 0)

            @pl.when(j + 2 < steps)
            def next_block():
                start(j + 2, 0)

            @pl.when(j + 3 < steps)
            def block_after():
                fill(j + 2, 0)
                add(j + 1, 1)
                start(j + 3, 1)

            @pl.when(j + 3 >= steps)
            def last_block():
                add(j + 1, 1)

            return carry

        fill(0, 0)
        if steps == 1:
            add(0, 0)
        else:
            start(1, 1)
            lax.fori_loop(0, steps // 2, two_steps, 0)
            if steps % 2:
                fill(steps - 1, 0)
                add(steps - 1, 0)

    if remade:

        @pl.when(jnp.logical_not(works))
        def nothing():
            for out in outs:
                out[...] = jnp.zeros(out.shape, BF16)


def weight_grad(
    pairs, first_column, width, rows, after=(), outputs=1, staying=(), remade=(), sources=()
):
    columns = pairs[0].right.shape[2]
    frames = pairs[0].right.shape[1]
    step = min(columns, 2 * BLOCK // outputs)
    every = [*pairs, *remade]
    micros = sum(p.count for p in every)
    call = Call()
    call.take([p.left for p in every], anywhere)
    call.take([p.right for p in pairs], anywhere)
    call.take(sources, anywhere)
    call.take(after, anywhere)
    call.take(staying, anywhere, pltpu.VMEM)
    call.give([((width // outputs, columns), BF16)] * outputs, in_vmem, pltpu.VMEM)
    scratch = [
        pltpu.VMEM((micros, frames, width), BF16),
        pltpu.VMEM((outputs, width // outputs, micros * frames), BF16),
        pltpu.VMEM((2, micros, frames, step), BF16),
        pltpu.SemaphoreType.DMA((len(every) + 1,)),
        pltpu.SemaphoreType.DMA((2, len(pairs) + 1)),
    ]
    if remade:
        normed, weight = sources
        scratch.append(pltpu.VMEM(normed.shape, BF16))
        scratch.append(pltpu.VMEM((2, weight.shape[0], step), BF16))
    bare = [p._replace(left=None, right=None) for p in every]
    body = functools.partial(
        weight_grad_kernel, bare, first_column, rows, step, outputs, len(remade)
    )
    return call.run(body, scratch, 0, limit=(24 if remade else 14) * 2**20)


class Part(NamedTuple):
    grads: Any
    column: int
    width: int
    result: int
    place: int
    tall: bool


def added_terms(part, grads, rows, index):
    block = pl.ds(pl.multiple_of(index * rows, rows), rows)
    total = None
    for grad in grads:
        term = grad[block, part.column : part.column + part.width].astype(F32)
        total = term if total is None else total + term
    return total


def arrived(came, side, at, width):
    for pair in came:
        if at < pair[side].shape[1]:
            return pair[side][:, at : at + width].astype(F32)
        at -= pair[side].shape[1]


def send_kernel(parts, rows, hop, joined, *refs):
    refs = list(refs)
    grads = [[refs.pop(0) for _ in range(p.grads)] for p in parts]
    came = [(refs.pop(0), refs.pop(0)) for _ in range(joined)]
    sends = refs[-2:]
    chip = lax.axis_index("batch") // CORES
    last = lax.axis_size("batch") // CORES - 1
    places = (jnp.minimum(chip + last - (hop - 1), last), jnp.maximum(chip - last + (hop - 1), 0))
    for d in range(2):
        at = 0
        for part, terms in zip(parts, grads):
            total = added_terms(part, terms, rows, places[d])
            if joined:
                total = total + arrived(came, d, at, part.width)
            sends[d][:, at : at + part.width] = total.astype(BF16)
            at += part.width


def finish_kernel(parts, rows, result_count, joined, *refs):
    refs = list(refs)
    grads = [[refs.pop(0) for _ in range(p.grads)] for p in parts]
    came = [(refs.pop(0), refs.pop(0)) for _ in range(joined)]
    total, turned, sems = refs[-3:]
    results = refs[-4 - result_count : -4]
    refs[-4][...] = jnp.zeros(refs[-4].shape, F32)
    chip = lax.axis_index("batch") // CORES
    copies, at = [], 0
    for i, (part, terms) in enumerate(zip(parts, grads)):
        own = slice(at, at + part.width)
        total[:, own] = (
            added_terms(part, terms, rows, chip)
            + arrived(came, 0, at, part.width)
            + arrived(came, 1, at, part.width)
        )
        result = results[part.result]
        if part.tall:
            turned[...] = total[:, own].T
            source, target = turned, result.at[pl.ds(part.place, part.width), :]
        else:
            source = total.at[pl.ds(0, result.shape[0]), pl.ds(at, part.width)]
            target = result.at[:, pl.ds(part.place, part.width)]
        copies.append(pltpu.make_async_copy(source, target, sems.at[i]))
        copies[i].start()
        at += part.width
    for copy in copies:
        copy.wait()


class Piece:
    def __init__(self, parts, first_hop):
        self.parts, self.hop, self.first_hop = parts, first_hop - 1, first_hop
        self.came = []
        self.width = sum(p.width for p in parts)

    def arrivals(self):
        return [x for pair in self.came for x in pair]

    def joined(self, other):
        piece = Piece(self.parts + other.parts, self.first_hop)
        piece.hop, piece.came = self.hop, self.came + other.came
        return piece


class Line:
    def __init__(self, exchange, rows, results, before):
        self.chips, self.rows, self.before = exchange.chips, rows, before
        self.results = {}
        self.shapes = results

    def bare(self, piece, names=None):
        parts = [p._replace(grads=len(p.grads)) for p in piece.parts]
        return parts if names is None else [
            p._replace(result=names.index(p.result)) for p in parts
        ]

    def send(self, piece, after=()):
        piece.hop += 1
        shape = (self.rows, piece.width)
        call = Call()
        call.take([g for p in piece.parts for g in p.grads], in_vmem, pltpu.VMEM)
        call.take(piece.arrivals(), in_vmem, pltpu.VMEM)
        call.take([self.before, *after], anywhere)
        call.give([(shape, BF16)] * 2, in_vmem, pltpu.VMEM)
        parts = self.bare(piece)
        up, down = call.run(
            functools.partial(send_kernel, parts, self.rows, piece.hop, len(piece.came)), [], 0
        )
        self.before = up
        edge = piece.first_hop - 1
        last = self.chips - 1
        piece.came = [(
            self.moved(up, [z for z in range(last) if edge <= z < piece.hop], 1),
            self.moved(down, [z for z in range(1, last + 1) if edge <= last - z < piece.hop], -1),
        )]

    def moved(self, value, senders, by):
        pairs = [(CORES * z + c, CORES * (z + by) + c) for z in senders for c in range(CORES)]
        return lax.ppermute(value, "batch", pairs)

    def finish(self, piece):
        names = sorted({p.result for p in piece.parts})
        parts = self.bare(piece, names)
        call = Call()
        call.take([g for p in piece.parts for g in p.grads], in_vmem, pltpu.VMEM)
        call.take(piece.arrivals(), in_vmem, pltpu.VMEM)
        call.take([self.before], anywhere)
        call.give([(self.shapes[n], F32) for n in names], anywhere, pltpu.HBM)
        call.give([((8, LANES), F32)], in_vmem, pltpu.VMEM)
        shape = (self.rows, piece.width)
        tall = max([p.width for p in parts if p.tall], default=8)
        scratch = [
            pltpu.VMEM(shape, F32),
            pltpu.VMEM((tall, self.rows), F32),
            pltpu.SemaphoreType.DMA((len(parts),)),
        ]
        done = call.run(
            functools.partial(finish_kernel, parts, self.rows, len(names), len(piece.came)),
            scratch,
            0,
        )
        self.results.update(zip(names, done))
        self.before = done[-1]


def table_gradient(row_grads, codes, blocks):
    chosen = lax.broadcasted_iota(jnp.int32, (blocks, codes.shape[0]), 0) == codes
    return jnp.sum(jnp.where(chosen[:, :, None, None], row_grads[None], 0.0), axis=1)


class Exchange:
    def __init__(self, batch):
        self.batch = batch
        self.chips = batch // CORES
        self.by_hops = batch % CORES == 0 and 2 <= self.chips <= LINE
        self.ends_hand_over = self.by_hops and self.chips == LINE

    def swap(self, x):
        if not self.by_hops:
            return None
        return lax.ppermute(x, "batch", [(b, b ^ 1) for b in range(self.batch)])

    def both(self, x):
        return [in_hbm(x), self.swap(x)]

    def inward(self, x):
        if not self.ends_hand_over:
            return None
        top = self.batch - CORES
        pairs = [(c, CORES + c) for c in range(CORES)]
        pairs += [(top + c, top - CORES + c) for c in range(CORES)]
        return lax.ppermute(x, "batch", pairs)

    def sources(self, x):
        return [in_hbm(x), self.inward(x)] if self.ends_hand_over else [in_hbm(x)]


def sums_by_hops(plan, exchange, back, down, up, lefts, table_grad):
    chips, rows = exchange.chips, plan.rows
    features, hidden_units = plan.features, plan.hidden_units
    core = lax.axis_index("batch") % CORES
    share = features // CORES
    swap = exchange.swap
    table_size = table_grad.shape[0]
    results = [
        (rows, 3 * features),
        (rows, features),
        (rows, hidden_units),
        (hidden_units, rows),
        (table_size, rows),
    ]
    line = Line(exchange, rows, results, up)

    def of(right, first_column):
        rights = exchange.both(right)
        pairs = [Pair(left, i, rights[i], plan.micros) for i, left in enumerate(lefts)]
        (grad,) = weight_grad(pairs, first_column, share, rows, [line.before])
        line.before = grad
        return grad

    ups = Piece([Part([up], 0, hidden_units, 2, 0, False)], 1)
    line.send(ups)
    first = 2 if exchange.ends_hand_over else 1
    downs = Piece([Part([down[0], swap(down[1])], 0, hidden_units, 3, 0, True)], first)
    line.send(downs)
    qkv = of(back.grad_packed, 0)
    out = of(back.grad_attn, share)
    norms = table_grad + swap(table_grad)
    norms = norms.reshape(table_size, chips, CORES, rows)
    norms = lax.dynamic_index_in_dim(norms, core, 2, keepdims=False).transpose(1, 0, 2)
    norms = jnp.pad(norms.astype(BF16), ((0, 0), (0, rows - table_size), (0, 0)))
    norms = norms.reshape(chips * rows, rows)
    others = Piece(
        [
            Part([qkv], 0, 3 * features, 0, 0, False),
            Part([out], 0, features, 1, 0, False),
            Part([norms], 0, rows, 4, 0, False),
        ],
        1,
    )
    last = chips - 1
    while downs.hop < last:
        line.send(downs)
    line.send(others, ups.arrivals())
    rest = ups.joined(others)
    if rest.hop < last:
        line.send(rest, downs.arrivals())
    line.finish(downs)
    while rest.hop < last:
        line.send(rest)
    line.finish(rest)
    return [line.results[i] for i in range(len(results))]


def sums_by_scatter(plan, kept, back, table_grad):
    features = plan.features
    share = features // CORES
    core = lax.axis_index("batch") % CORES

    def local(lefts, rights, column):
        pairs = [Pair(left, None, right, left.shape[0]) for left, right in zip(lefts, rights)]
        if column is None:
            mine, other = weight_grad(pairs, 0, features, plan.rows, outputs=2)
        else:
            (left,), (right,) = lefts, rights
            mine, other = [
                weight_grad(
                    [Pair(left, i, right, left.shape[1])], column, share, plan.rows
                )[0]
                for i in range(CORES)
            ]
        even, odd = jnp.where(core == 0, mine, other), jnp.where(core == 0, other, mine)
        blocks = [x.reshape(-1, 1, plan.rows, x.shape[1]) for x in (even, odd)]
        return jnp.concatenate(blocks, axis=1).reshape(features, -1)

    def scattered(x, dimension):
        return lax.psum_scatter(
            x, "batch", scatter_dimension=dimension, tiled=True
        ).astype(F32)

    grad_y = [back.y_early, back.y_late, back.y_last]
    down = local([jnp.concatenate(grad_y, axis=0)], [kept.act], None)
    grad_up = jnp.concatenate([back.up_early, back.up_last], axis=0)
    return (
        scattered(local([kept.left], [back.grad_packed], 0), 0),
        scattered(local([kept.left], [back.grad_attn], share), 0),
        scattered(local([kept.left], [grad_up], 2 * share), 0),
        scattered(down, 0).T,
        scattered(table_grad, 1),
    )


def per_device(
    frames_in, cotangent, qkv_weight, out_weight, up_weight, down_weight, norm_table, lengths,
    codebooks,
):
    sections = lax.axis_size("section")
    batch = lax.axis_size("batch")
    section = lax.axis_index("section")
    micros = lengths.shape[0]
    tokens, features = frames_in.shape
    frames = tokens // micros
    plan = Plan(
        sections, micros, frames, features, up_weight.shape[2], max(features // batch, LANES)
    )
    frames_all = frames_in.reshape(micros, frames, features)
    cot_all = cotangent.reshape(micros, frames, features)

    state = State(
        numbers=[lengths, codebooks],
        info=None,
        table=norm_table[0],
        weights=Weights(qkv_weight[0], out_weight[0], up_weight[0], down_weight[0]),
    )
    exchange = Exchange(batch)

    share = features // CORES

    def down_pairs(grad_ys, act):
        firsts = [span[0] for span in plan.y_spans()]
        return [Pair(y, None, act, y.shape[0], 0, at) for y, at in zip(grad_ys, firsts)]

    def up_pairs(grad_up, first):
        count = grad_up[0].shape[0]
        return [
            Pair(left, i, g, count, first, 0) for i, (left, g) in enumerate(zip(lefts, grad_up))
        ]

    before_bwd = [[] for _ in range(plan.ticks())]
    incoming = arriving = None
    working = lambda micro: 0 <= micro < micros
    for tick in range(plan.ticks()):
        sent = returned = None
        if tick < plan.fwd_ticks():
            state, output = run_forward(plan, tick, state, incoming, frames_all)
            onward = [
                (s, s + 1) for s in range(sections - 1) if working(plan.fwd_id(tick, s))
            ]
            if onward:
                sent = lax.ppermute(output, "section", onward)
        if tick >= sections - 1:
            late = tick == plan.ticks() - 1
            state, output = run_backward(
                plan, tick, state, arriving, cot_all, before_bwd[tick], FIRST if late else WHOLE
            )
            if late:
                after = []
                if exchange.by_hops:
                    y_last = exchange.sources(state.back.y_last)
                    up_last = exchange.both(state.back.up_last)
                    after = up_early[1:]
                state, output = run_backward(
                    plan, tick, state, arriving, cot_all, after, SECOND, output
                )
            output = output[0]
            backward = [
                (s, s - 1) for s in range(1, sections) if working(plan.bwd_id(tick, s))
            ]
            if backward:
                returned = lax.ppermute(output, "section", backward)
        incoming, arriving = sent, returned
        if exchange.by_hops:
            if tick == plan.fwd_ticks() - 1:
                lefts = exchange.both(state.kept.left)
                before_bwd[tick + 1] += lefts[1:]
                second = exchange.sources(state.kept.second)
                before_bwd[tick + 2] += second[1:]
            if tick == plan.y_spans()[0][1] + 2 * sections - 3:
                y_early = exchange.sources(state.back.y_early)
                before_bwd[plan.ticks() - 1] += y_early[1:]
            if tick == plan.ticks() - 2:
                y_late = exchange.sources(state.back.y_late)
                up_early = exchange.both(state.back.up_early)

    blocks = norm_table.shape[1] // 4
    codes = codebooks * (section % 2)
    table_grad = table_gradient(state.back.row_grads, codes, blocks).reshape(norm_table.shape[1:])
    if exchange.by_hops:
        sides = list(zip(y_early, y_late, y_last))
        pairs = down_pairs(sides[0], in_hbm(state.kept.act))
        remade, sources = (), ()
        if exchange.ends_hand_over:
            remade = down_pairs(sides[1], None)
            sources = (second[1], in_hbm(up_weight[0]))
        ready = [output, up_last[1], up_early[1]]
        down = weight_grad(pairs, 0, features, plan.rows, ready, 2, (), remade, sources)
        pairs = up_pairs(up_early, 0) + up_pairs(up_last, micros - 1)
        (up,) = weight_grad(pairs, 2 * share, share, plan.rows, down[:1])
        sums = sums_by_hops(plan, exchange, state.back, down, up, lefts, table_grad)
    else:
        sums = sums_by_scatter(plan, state.kept, state.back, table_grad)
    return (
        state.kept.layer_out.reshape(1, tokens, features),
        state.back.grad_in.reshape(1, tokens, features),
    ) + tuple(x[None] for x in sums)


def solution(mesh):
    section, batch = mesh.axis_names
    over_batch = P(batch)
    over_section = P(section)
    both = P(section, batch, None)
    columns = P(section, None, batch)
    in_specs = (over_batch,) * 2 + (over_section,) * 5 + (over_batch,) * 2
    out_specs = (both,) * 5 + (columns,) * 2
    return jax.shard_map(
        per_device, mesh=mesh, in_specs=in_specs, out_specs=out_specs, check_vma=False
    )
```

```python
import functools
from typing import Any, NamedTuple

import jax
import jax.numpy as jnp
from jax import lax
from jax.experimental import pallas as pl
from jax.experimental.pallas import tpu as pltpu
from jax.sharding import PartitionSpec as P

HEADS = 16
GROUP = 4
BLOCK = 512
LANES = 128
CORES = 2
VMEM_LIMIT = 14 * 2**20
WHOLE, FIRST, SECOND = 0, 1, 2
LINE = 4

epsilon = 1e-05
masked_score = -1e30
BF16 = jnp.bfloat16
F32 = jnp.float32

in_vmem = pl.BlockSpec(memory_space=pltpu.VMEM)
in_smem = pl.BlockSpec(memory_space=pltpu.SMEM)
anywhere = pl.BlockSpec(memory_space=pl.ANY)


class Weights(NamedTuple):
    qkv: Any
    out: Any
    up: Any
    down: Any


class Reread(NamedTuple):
    entry: Any
    packed: Any
    probs: Any
    hidden: Any
    slope: Any


class Kept(NamedTuple):
    layer_out: Any
    left: Any
    second: Any
    act: Any


class Back(NamedTuple):
    grad_in: Any
    y_early: Any
    y_last: Any
    up_early: Any
    up_last: Any
    grad_attn: Any
    grad_packed: Any
    row_grads: Any


def product(left, right):
    return lax.dot_general(left, right, (((1,), (0,)), ((), ())), preferred_element_type=F32)


def product_last(left, right):
    return lax.dot_general(left, right, (((1,), (1,)), ((), ())), preferred_element_type=F32)


def product_first(left, right):
    return lax.dot_general(left, right, (((0,), (0,)), ((), ())), preferred_element_type=F32)


def normalize(values):
    centre = values - jnp.mean(values, axis=-1, keepdims=True)
    reciprocal = lax.rsqrt(jnp.mean(centre * centre, axis=-1, keepdims=True) + epsilon)
    return centre * reciprocal, reciprocal


def normalize_back(gradient, normal_part, reciprocal, gain_row):
    scaled = gradient * (1.0 + gain_row)
    centred = scaled - jnp.mean(scaled, axis=-1, keepdims=True)
    return reciprocal * (
        centred - normal_part * jnp.mean(scaled * normal_part, axis=-1, keepdims=True)
    )


def gelu_and_slope(u):
    root = 0.7978845608028654
    square = u * u
    bent = jnp.tanh(root * u * (1.0 + 0.044715 * square))
    half = 0.5 * (1.0 + bent)
    slope = half + 0.5 * u * (1.0 - bent * bent) * (root * (1.0 + 3 * 0.044715 * square))
    return u * half, slope


def stacked_heads(block, head_size):
    owner = lax.broadcasted_iota(jnp.int32, block.shape, 1) // head_size
    zero = jnp.zeros_like(block)
    return jnp.concatenate([jnp.where(owner == h, block, zero) for h in range(GROUP)], axis=0)


def beside(stack, frames):
    return jnp.concatenate([stack[h * frames : (h + 1) * frames] for h in range(GROUP)], axis=1)


def table_rows(table, code):
    pair = table[pl.ds(pl.multiple_of((code // 2) * 8, 8), 8), :]
    return jnp.where(code % 2 == 1, pair[4:8], pair[0:4])


class Saver:
    def __init__(self, sems, base):
        self.sems, self.base, self.pending = sems, base, []

    def __call__(self, source, target):
        copy = pltpu.make_async_copy(source, target, self.sems.at[self.base + len(self.pending)])
        copy.start()
        self.pending.append(copy)

    def spread(self, source, buffers, spans, slot):
        sem = self.sems.at[self.base + len(self.pending)]
        copies = []
        for buffer, (first, end) in zip(buffers, spans):
            if buffer is None:
                continue
            place = jnp.clip(slot - first, 0, end - first - 1)
            copies.append(pltpu.make_async_copy(source, buffer.at[place], sem))
            pl.when((slot >= first) & (slot < end))(copies[-1].start)
        self.pending.append(copies[0])

    def wait(self):
        for copy in self.pending:
            copy.wait()


def turn(source, target, row0, col0, side_by, strips, sems, base):
    slots, side, _ = strips.shape
    count = side_by // side

    def strip(i):
        c = pl.multiple_of(col0 + i * side, side)
        return pltpu.make_async_copy(
            strips.at[i % slots],
            target.at[pl.ds(c, side), pl.ds(row0, side_by)],
            sems.at[base + i % slots],
        )

    def one_strip(i, carry):
        @pl.when(i >= slots)
        def slot_is_free():
            strip(i - slots).wait()

        c = pl.multiple_of(col0 + i * side, side)
        strips[i % slots] = source[row0 : row0 + side_by, pl.ds(c, side)].T
        strip(i).start()
        return carry

    lax.fori_loop(0, count, one_strip, 0)
    for i in range(count - slots, count):
        strip(i).wait()


def redo_activated(normed_in, weight, act_out, normed, act_slots, sems, base):
    micros, frames, _ = normed.shape
    step = act_slots.shape[3]
    load = pltpu.make_async_copy(normed_in, normed, sems.at[base])
    load.start()
    load.wait()
    copies = []
    for j in range(0, weight.shape[1], step):
        slot = (j // step) % 2
        if len(copies) >= 2:
            copies[-2].wait()
        rows = normed[...].reshape(micros * frames, -1)
        act = gelu_and_slope(product(rows, weight[:, j : j + step]))[0].astype(BF16)
        act_slots[slot] = act.reshape(micros, frames, step)
        target = act_out.at[:, :, pl.ds(j, step)]
        copies.append(pltpu.make_async_copy(act_slots.at[slot], target, sems.at[base + slot]))
        copies[-1].start()
    for copy in copies[-2:]:
        copy.wait()


def copy_kernel(source, target, held, sem):
    @pl.when(lax.axis_index("section") == 0)
    def copy():
        for start, end in ((source, held), (held, target)):
            moving = pltpu.make_async_copy(start, end, sem)
            moving.start()
            moving.wait()


def first_sections(x):
    call = Call()
    call.take([x], anywhere, pltpu.HBM)
    call.give(like([x]), anywhere, pltpu.HBM)
    return call.run(copy_kernel, [pltpu.VMEM(x.shape, x.dtype), pltpu.SemaphoreType.DMA], 0)[0]


def redo_scratch(plan):
    lead = (plan.micros, plan.frames)
    return [
        pltpu.VMEM(lead + (plan.features,), BF16),
        pltpu.VMEM((2,) + lead + (2 * BLOCK,), BF16),
    ]


def beside_an_end():
    chip = lax.axis_index("batch") // CORES
    return (chip == 1) | (chip == lax.axis_size("batch") // CORES - 2)


class Plan(NamedTuple):
    sections: int
    micros: int
    frames: int
    features: int
    hidden_units: int
    rows: int

    def fwd_ticks(self):
        return self.micros + self.sections - 1

    def ticks(self):
        return self.micros + 2 * (self.sections - 1)

    def up_spans(self):
        return (0, self.micros - 1), (self.micros - 1, self.micros)

    def bwd_reaches(self, tick):
        low, high = tick - 2 * (self.sections - 1), tick - (self.sections - 1)
        spread = tuple(low < end and high >= first for first, end in self.up_spans())
        return (True,) + spread + spread + (True,) * 3

    def bwd_uses(self, tick, part):
        first = (False,) + (True,) * 5 + (False, False)
        halves = {WHOLE: (True,) * 8, FIRST: first, SECOND: tuple(not f for f in first)}
        return tuple(r and h for r, h in zip(self.bwd_reaches(tick), halves[part]))

    def fwd_id(self, tick, section):
        return tick - section

    def bwd_id(self, tick, section):
        return tick - 2 * (self.sections - 1) + section


def forward_kernel(plan, tick, has_incoming, loads_weights, redoes, *refs):
    refs = list(refs)
    take = lambda n: [refs.pop(0) for _ in range(n)]
    if loads_weights:
        lengths, codebooks, given_table = take(3)
        given = Weights(*take(4))
    else:
        info, table = take(2)
        weight = Weights(*take(4))
        take(4)
    incoming = take(1)[0] if has_incoming else None
    (frames_in,) = take(1)
    if redoes:
        (second_in,) = take(1)
    if loads_weights:
        info, table = take(2)
        weight = Weights(*take(4))
    else:
        take(len(Reread._fields) + len(Kept._fields))
    turned = Weights(*take(4))
    reread = Reread(*take(5))
    kept = Kept(*take(4))
    (outgoing,) = take(1)
    if redoes:
        (act_in,) = take(1)
        redo = (refs.pop(), refs.pop())[::-1]
    entry, packed, probs, hidden, slope, normed, left, attended, act, strips, sems = refs

    micros, frames, features, hidden_units, rows_kept = plan[1:]
    head_size = features // HEADS
    group_width = GROUP * head_size
    section = lax.axis_index("section")
    core = lax.axis_index("batch") % CORES
    is_nar = section % 2
    micro = plan.fwd_id(tick, section)
    active = (micro >= 0) & (micro < micros)
    slot = jnp.clip(micro, 0, micros - 1)

    loads = []
    if loads_weights:
        for i in range(micros):
            info[i] = lengths[i]
            info[micros + i] = codebooks[i]
        pairs = [(given_table, table)] + list(zip(given, weight))
        for i, (source, target) in enumerate(pairs):
            loads.append(pltpu.make_async_copy(source, target, sems.at[i]))
        loads[0].start()

        @pl.when(core == 1)
        def later():
            loads[4].start()
            loads[4].wait()

        loads[1].start()
    base = len(loads)

    def ready(i):
        if not loads_weights:
            return
        if i == 4:
            pl.when(core != 1)(loads[4].wait)
            return
        loads[i].wait()
        if i == 1:
            loads[2].start()
            loads[3].start()
        if i == 2:
            pl.when(core != 1)(loads[4].start)

    @pl.when(active)
    def forward():
        save = Saver(sems, base)
        length = info[slot]
        code = info[micros + slot] * is_nar

        def own_input():
            pltpu.sync_copy(frames_in.at[slot], entry)

        if has_incoming:
            pl.when(section == 0)(own_input)

            @pl.when(section != 0)
            def passed_input():
                entry[...] = incoming[...]

        else:
            own_input()

        save(entry, reread.entry.at[slot])
        share = features // CORES

        def share_columns(source, first):
            for b in range(features // rows_kept):
                at = first + (b // CORES) * rows_kept
                left[b % CORES, :, at : at + rows_kept] = source[
                    :, b * rows_kept : (b + 1) * rows_kept
                ]

        ready(0)
        rows = table_rows(table, code)
        residual = entry[...].astype(F32)
        normal_one, _ = normalize(residual)
        normed[...] = (normal_one * (1.0 + rows[0:1]) + rows[1:2]).astype(BF16)
        share_columns(normed, 0)
        ready(1)
        for j in range(0, 3 * features, BLOCK):
            packed[:, j : j + BLOCK] = product(normed[...], weight.qkv[:, j : j + BLOCK]).astype(
                BF16
            )
        save(packed, reread.packed.at[slot])
        tall = (GROUP * frames, frames)
        query_ids = lax.rem(lax.broadcasted_iota(jnp.int32, tall, 0), frames)
        key_ids = lax.broadcasted_iota(jnp.int32, tall, 1)
        allowed = (key_ids < length) & (key_ids <= query_ids + is_nar * frames)
        inv_root = head_size ** (-0.5)
        for g in range(HEADS // GROUP):
            lo, hi = g * group_width, (g + 1) * group_width
            queries = stacked_heads(packed[:, lo:hi], head_size)
            keys = packed[:, features + lo : features + hi]
            values = stacked_heads(packed[:, 2 * features + lo : 2 * features + hi], head_size)
            scores = jnp.where(allowed, product_last(queries, keys) * inv_root, masked_score)
            exp_scores = jnp.exp(scores - jnp.max(scores, axis=-1, keepdims=True))
            total = jnp.sum(exp_scores, axis=-1, keepdims=True)
            group_probs = (exp_scores * (1.0 / total)).astype(BF16)
            probs[g * GROUP * frames : (g + 1) * GROUP * frames, :] = group_probs
            attended[:, lo:hi] = product(beside(group_probs, frames), values).astype(BF16)
        save(probs, reread.probs.at[slot])
        share_columns(attended, share)
        ready(2)
        for j in range(0, features, BLOCK):
            hidden[:, j : j + BLOCK] = residual[:, j : j + BLOCK] + product(
                attended[...], weight.out[:, j : j + BLOCK]
            )
        save(hidden, reread.hidden.at[slot])
        normal_two, _ = normalize(hidden[...])
        normed[...] = (normal_two * (1.0 + rows[2:3]) + rows[3:4]).astype(BF16)
        share_columns(normed, 2 * share)
        save(normed, kept.second.at[slot])
        save(left.at[core], kept.left.at[0, slot])
        save(left.at[1 - core], kept.left.at[1, slot])
        ready(3)
        for j in range(0, hidden_units, BLOCK):
            value, gradient = gelu_and_slope(product(normed[...], weight.up[:, j : j + BLOCK]))
            act[:, j : j + BLOCK] = value.astype(BF16)
            slope[:, j : j + BLOCK] = gradient.astype(BF16)
            if (j + BLOCK) % (hidden_units // 2) == 0:
                done = pl.ds(j + BLOCK - hidden_units // 2, hidden_units // 2)
                save(slope.at[:, done], reread.slope.at[slot, :, done])
                save(act.at[:, done], kept.act.at[slot, :, done])
        ready(4)
        for j in range(0, features, BLOCK):
            outgoing[:, j : j + BLOCK] = (
                hidden[:, j : j + BLOCK] + product(act[...], weight.down[:, j : j + BLOCK])
            ).astype(BF16)
        save(outgoing, kept.layer_out.at[slot])
        save.wait()

    if redoes:

        @pl.when((section == 0) & beside_an_end())
        def redo_early():
            redo_activated(second_in, weight.up, act_in, *redo, sems, base)

    units = []
    for source, target in zip(weight, turned):
        total_rows, total_cols = source.shape
        for r in range(0, total_rows, features):
            for c in range(0, total_cols, features):
                units.append((source, target, r, c))
    cut = len(units) // 3
    pieces = (units[:cut], units[cut:])
    piece = jnp.where(micro < 0, tick, micro - micros + section)

    @pl.when(jnp.logical_not(active))
    def wait_for_weights():
        for i in range(base):
            ready(i)

    for k in range(len(pieces)):

        @pl.when(jnp.logical_not(active) & (piece == k))
        def one_piece(k=k):
            for source, target, r, c in pieces[k]:
                turn(source, target, r, c, features, strips, sems, base)


def backward_kernel(plan, tick, part, has_arriving, present, unread, redoes, *refs):
    refs = list(refs)
    take = lambda n: [refs.pop(0) for _ in range(n)]
    info, table = take(2)
    turned = Weights(*(take(1) + [None] * 3 if part == SECOND else take(4)))
    take(unread)
    if redoes:
        second_in, up_weight, _ = take(3)
    arriving = take(1)[0] if has_arriving else None
    (cotangent,) = take(1)
    take(len(Reread._fields))
    used = plan.bwd_uses(tick, part)
    take(sum(u and p for u, p in zip(used, present)))
    halfway = take(3) if part == SECOND else None
    reread = Reread(*take(5))
    back = Back(*[take(1)[0] if u else None for u in used])
    if part == FIRST:
        halfway = take(3)
    else:
        (returning,) = take(1)
    if redoes:
        (act_in,) = take(1)
        redo = (refs.pop(), refs.pop())[::-1]
    (entry, packed, probs, hidden, slope, grad_y, grad_up, wide, grad_hidden, grad_attn, mixed,
     grad_packed, row_grads, sems) = refs

    micros, frames, features, hidden_units, _ = plan[1:]
    head_size = features // HEADS
    group_width = GROUP * head_size
    section = lax.axis_index("section")
    is_nar = section % 2
    micro = plan.bwd_id(tick, section)
    active = (micro >= 0) & (micro < micros)
    slot = jnp.clip(micro, 0, micros - 1)

    if redoes:
        through = micro >= micros if part == WHOLE else micro == micros

        @pl.when(through & beside_an_end())
        def redo_late():
            redo_activated(second_in, up_weight, act_in, *redo, sems, 0)

    def start_fetches(wanted):
        fetches = []
        for i, target in enumerate((entry, packed, probs, hidden, slope)):
            fetches.append(pltpu.make_async_copy(reread[i].at[slot], target, sems.at[i]))
        for i in (4, 3, 1, 2, 0):
            if i in wanted:
                fetches[i].start()
        return fetches

    def first_half():
        length = info[slot]
        code = info[micros + slot] * is_nar
        fetches = start_fetches((3, 4) if part == FIRST else range(5))
        save = Saver(sems, len(fetches))

        def own_cotangent():
            pltpu.sync_copy(cotangent.at[slot], grad_y)
            live = lax.broadcasted_iota(jnp.int32, (frames, features), 0) < length
            grad_y[...] = jnp.where(live, grad_y[...], jnp.zeros((frames, features), BF16))

        if has_arriving:
            pl.when(section == plan.sections - 1)(own_cotangent)

            @pl.when(section != plan.sections - 1)
            def passed_gradient():
                grad_y[...] = arriving[...]

        else:
            own_cotangent()

        save.spread(grad_y, back[1:3], plan.up_spans(), slot)
        rows = table_rows(table, code)
        fetches[4].wait()
        for j in range(0, hidden_units, BLOCK):
            grad_act = product(grad_y[...], turned.down[:, j : j + BLOCK])
            grad_up[:, j : j + BLOCK] = (
                grad_act * slope[:, j : j + BLOCK].astype(F32)
            ).astype(BF16)
        save.spread(grad_up, (back.up_early, back.up_last), plan.up_spans(), slot)
        for j in range(0, features, BLOCK):
            wide[:, j : j + BLOCK] = product(grad_up[...], turned.up[:, j : j + BLOCK])
        fetches[3].wait()
        normal_two, recip_two = normalize(hidden[...])
        grad_two = wide[...]
        row_grads[2:3, :] = jnp.sum(grad_two * normal_two, axis=0, keepdims=True)
        row_grads[3:4, :] = jnp.sum(grad_two, axis=0, keepdims=True)
        grad_hidden[...] = grad_y[...].astype(F32) + normalize_back(
            grad_two, normal_two, recip_two, rows[2:3]
        )
        grad_attn[...] = grad_hidden[...].astype(BF16)
        save(grad_attn, back.grad_attn.at[slot])
        for j in range(0, features, BLOCK):
            mixed[:, j : j + BLOCK] = product(
                grad_attn[...], turned.out[:, j : j + BLOCK]
            ).astype(BF16)
        return fetches, save

    def second_half(fetches, save):
        code = info[micros + slot] * is_nar
        rows = table_rows(table, code)
        fetches[1].wait()
        fetches[2].wait()
        inv_root = head_size ** (-0.5)
        for g in range(HEADS // GROUP):
            lo, hi = g * group_width, (g + 1) * group_width
            queries = stacked_heads(packed[:, lo:hi], head_size)
            keys = stacked_heads(packed[:, features + lo : features + hi], head_size)
            values = packed[:, 2 * features + lo : 2 * features + hi]
            group_mixed = stacked_heads(mixed[:, lo:hi], head_size)
            group_probs = probs[g * GROUP * frames : (g + 1) * GROUP * frames, :]
            wide_probs = group_probs.astype(F32)
            grad_probs = product_last(group_mixed, values)
            inner = jnp.sum(wide_probs * grad_probs, axis=-1, keepdims=True)
            grad_scores = (wide_probs * (grad_probs - inner)).astype(BF16)
            grad_packed[:, lo:hi] = (
                product(beside(grad_scores, frames), keys) * inv_root
            ).astype(BF16)
            grad_packed[:, features + lo : features + hi] = (
                product_first(grad_scores, queries) * inv_root
            ).astype(BF16)
            grad_packed[:, 2 * features + lo : 2 * features + hi] = product_first(
                group_probs, group_mixed
            ).astype(BF16)
        save(grad_packed, back.grad_packed.at[slot])
        for j in range(0, features, BLOCK):
            wide[:, j : j + BLOCK] = product(grad_packed[...], turned.qkv[:, j : j + BLOCK])
        fetches[0].wait()
        normal_one, recip_one = normalize(entry[...].astype(F32))
        grad_one = wide[...]
        row_grads[0:1, :] = jnp.sum(grad_one * normal_one, axis=0, keepdims=True)
        row_grads[1:2, :] = jnp.sum(grad_one, axis=0, keepdims=True)
        save(row_grads, back.row_grads.at[slot])
        returning[...] = (
            grad_hidden[...] + normalize_back(grad_one, normal_one, recip_one, rows[0:1])
        ).astype(BF16)
        save(returning, back.grad_in.at[slot])
        save.wait()

    @pl.when(active)
    def backward():
        if part == SECOND:
            fetches = start_fetches((0, 1, 2))
            load = Saver(sems, 5)
            for source, target in zip(halfway, (grad_hidden, mixed, row_grads)):
                load(source, target)
            load.wait()
            second_half(fetches, Saver(sems, 5))
            return
        fetches, save = first_half()
        if part == FIRST:
            for source, target in zip((grad_hidden, mixed, row_grads), halfway):
                save(source, target)
            save.wait()
        else:
            second_half(fetches, save)


def shapes_of(plan):
    micros, frames, features, hidden_units, _ = plan[1:]
    own = (micros, frames)
    reread = Reread(
        entry=(own + (features,), BF16),
        packed=(own + (3 * features,), BF16),
        probs=((micros, HEADS * frames, frames), BF16),
        hidden=(own + (features,), F32),
        slope=(own + (hidden_units,), BF16),
    )
    def buffers(spans, columns):
        return [((end - first, frames, columns), BF16) for first, end in spans]

    left = ((CORES,) + own + (3 * features // CORES,), BF16)
    wide = (own + (features,), BF16)
    kept = Kept(wide, left, wide, (own + (hidden_units,), BF16))
    back = Back(
        wide,
        *buffers(plan.up_spans(), features),
        *buffers(plan.up_spans(), hidden_units),
        grad_attn=wide,
        grad_packed=(own + (3 * features,), BF16),
        row_grads=((micros, 4, features), F32),
    )
    return reread, kept, back


def scratch_of(shapes):
    return [pltpu.VMEM(shape[1:], dtype) for shape, dtype in shapes]


class Call:
    def __init__(self):
        self.args, self.in_specs, self.out_shape, self.out_specs = [], [], [], []
        self.aliases = {}

    def take(self, values, spec, space=None):
        for value in values:
            if space is not None:
                value = pltpu.with_memory_space_constraint(value, space)
            self.args.append(value)
            self.in_specs.append(spec)

    def give(self, shapes, spec, space, updates=None):
        for i, (shape, dtype) in enumerate(shapes):
            if updates is not None:
                self.aliases[updates + i] = len(self.out_shape)
            self.out_shape.append(space(shape, dtype))
            self.out_specs.append(spec)

    def update(self, arrays, shapes, used):
        arrays = arrays or (None,) * len(shapes)
        for array, shape, use in zip(arrays, shapes, used):
            if use and array is not None:
                self.take([array], anywhere, pltpu.HBM)
                self.give([shape], anywhere, pltpu.HBM, len(self.args) - 1)
            elif use:
                self.give([shape], anywhere, pltpu.HBM)

    def run(self, body, scratch, flops, limit=VMEM_LIMIT):
        return list(
            pl.pallas_call(
                body,
                out_shape=self.out_shape,
                in_specs=self.in_specs,
                out_specs=self.out_specs,
                scratch_shapes=scratch,
                input_output_aliases=self.aliases,
                compiler_params=pltpu.CompilerParams(vmem_limit_bytes=limit),
                cost_estimate=pl.CostEstimate(
                    flops=flops, bytes_accessed=0, transcendentals=0
                ),
            )(*self.args)
        )


def updated(old, used, new):
    new = list(new)
    old = old or (None,) * len(used)
    return [new.pop(0) if u else o for o, u in zip(old, used)]


def like(arrays):
    return [(x.shape, x.dtype) for x in arrays]


class State(NamedTuple):
    numbers: Any
    info: Any
    table: Any
    weights: Any
    turned: Any = None
    reread: Any = None
    kept: Any = None
    back: Any = None


def run_forward(plan, tick, state, incoming, frames_in, second_in=None):
    reread_shapes, kept_shapes, _ = shapes_of(plan)
    first = state.turned is None
    at_turned = at_kept = None
    call = Call()
    if first:
        call.take(state.numbers, in_smem)
        call.take([state.table], anywhere)
        call.take(state.weights, anywhere)
    else:
        call.take([state.info], in_smem, pltpu.SMEM)
        call.take([state.table], in_vmem, pltpu.VMEM)
        call.take(state.weights, in_vmem, pltpu.VMEM)
        at_turned = len(call.args)
        call.take(state.turned, anywhere, pltpu.VMEM)
    if incoming is not None:
        call.take([incoming], in_vmem, pltpu.VMEM)
    call.take([frames_in], anywhere)
    if second_in is not None:
        call.take([second_in], anywhere)
    if first:
        call.give([((2 * plan.micros,), jnp.int32)], in_smem, pltpu.SMEM)
        call.give(like([state.table]), in_vmem, pltpu.VMEM)
        call.give(like(state.weights), in_vmem, pltpu.VMEM)
    else:
        at_kept = len(call.args)
        call.take(state.reread + state.kept, anywhere, pltpu.HBM)
    call.give([(w.shape[::-1], BF16) for w in state.weights], anywhere, pltpu.VMEM, at_turned)
    call.give(reread_shapes + kept_shapes, anywhere, pltpu.HBM, at_kept)
    call.give([((plan.frames, plan.features), BF16)], in_vmem, pltpu.VMEM)
    if second_in is not None:
        call.give([kept_shapes.act], anywhere, pltpu.HBM)
    scratch = scratch_of(reread_shapes) + [
        pltpu.VMEM((plan.frames, plan.features), BF16),
        pltpu.VMEM((CORES, plan.frames, 3 * plan.features // CORES), BF16),
        pltpu.VMEM((plan.frames, plan.features), BF16),
        pltpu.VMEM((plan.frames, plan.hidden_units), BF16),
        pltpu.VMEM((2, 256, plan.features), BF16),
        pltpu.SemaphoreType.DMA((24,)),
    ]
    flops = 8 * plan.frames * sum(w.size for w in state.weights)
    if second_in is not None:
        scratch += redo_scratch(plan)
    body = functools.partial(
        forward_kernel, plan, tick, incoming is not None, first, second_in is not None
    )
    got = call.run(body, scratch, flops)
    if first:
        state = state._replace(info=got[0], table=got[1], weights=Weights(*got[2:6]))
        got = got[6:]
    kept = Kept(*got[9:13])
    state = state._replace(turned=Weights(*got[:4]), reread=Reread(*got[4:9]), kept=kept)
    return state, got[13], got[14:]


def run_backward(
    plan, tick, state, arriving, cotangent, after, part=WHOLE, halfway=(), redo=None
):
    reread_shapes, _, back_shapes = shapes_of(plan)
    call = Call()
    call.take([state.info], in_smem, pltpu.SMEM)
    call.take([state.table], in_vmem, pltpu.VMEM)
    call.take(state.turned[:1] if part == SECOND else state.turned, in_vmem, pltpu.VMEM)
    staying = () if part == SECOND else state.weights
    call.take(staying, anywhere, pltpu.VMEM)
    call.take(after, anywhere)
    unread = len(staying) + len(after)
    if redo is not None:
        second_in, act_in = redo
        call.take([second_in], anywhere)
        call.take([state.weights.up], in_vmem, pltpu.VMEM)
        at_act = len(call.args)
        call.take([act_in], anywhere, pltpu.HBM)
    if arriving is not None:
        call.take([arriving], in_vmem, pltpu.VMEM)
    call.take([cotangent], anywhere)
    at_reread = len(call.args)
    call.take(state.reread, anywhere, pltpu.HBM)
    call.give(reread_shapes, anywhere, pltpu.HBM, at_reread)
    used = plan.bwd_uses(tick, part)
    present = [b is not None for b in state.back or (None,) * len(used)]
    call.update(state.back, back_shapes, used)
    narrow = ((plan.frames, plan.features), BF16)
    full = ((plan.frames, plan.features), F32)
    between = [full, narrow, ((4, plan.features), F32)]
    call.take(halfway, anywhere, pltpu.HBM)
    results = between if part == FIRST else [narrow]
    if part == FIRST:
        call.give(results, anywhere, pltpu.HBM)
    else:
        call.give(results, in_vmem, pltpu.VMEM)
    if redo is not None:
        call.give(like([act_in]), anywhere, pltpu.HBM, at_act)
    scratch = scratch_of(reread_shapes) + [
        pltpu.VMEM(*narrow),
        pltpu.VMEM((plan.frames, plan.hidden_units), BF16),
        pltpu.VMEM(*full),
        pltpu.VMEM(*full),
        pltpu.VMEM(*narrow),
        pltpu.VMEM(*narrow),
        pltpu.VMEM((plan.frames, 3 * plan.features), BF16),
        pltpu.VMEM((4, plan.features), F32),
        pltpu.SemaphoreType.DMA((16,)),
    ]
    flops = 8 * plan.frames * sum(w.size for w in state.turned)
    if redo is not None:
        scratch += redo_scratch(plan)
    body = functools.partial(
        backward_kernel, plan, tick, part, arriving is not None, present, unread, redo is not None
    )
    got = call.run(body, scratch, flops if part == WHOLE else flops // 2)
    act_in = got.pop() if redo is not None else None
    got, last = got[: -len(results)], got[-len(results) :]
    back = Back(*updated(state.back, used, got[5:]))
    return state._replace(reread=Reread(*got[:5]), back=back), last, act_in


def in_hbm(x):
    return pltpu.with_memory_space_constraint(x, pltpu.HBM)


class Pair(NamedTuple):
    left: Any
    share: Any
    right: Any
    count: int
    left_first: int = 0
    right_first: int = 0


def weight_grad_kernel(pairs, first_column, rows, step, outputs, skip_ends, *refs):
    lefts, rights = refs[: len(pairs)], refs[len(pairs) : 2 * len(pairs)]
    outs = refs[-5 - outputs : -5]
    stage, turned, right_slots, sems, right_sems = refs[-5:]
    frames, width = stage.shape[1:]
    share = width // outputs
    steps = outs[0].shape[1] // step
    core = lax.axis_index("batch") % CORES
    chip = lax.axis_index("batch") // CORES
    chips = lax.axis_size("batch") // CORES
    works = (chip > 0) & (chip < chips - 1) if skip_ends else chip >= 0
    firsts = [sum(p.count for p in pairs[:i]) for i in range(len(pairs))]
    columns = lambda j: pl.ds(pl.multiple_of(j * step, step), step)

    def right_copies(j, slot):
        return [
            pltpu.make_async_copy(
                rights[i].at[pl.ds(p.right_first, p.count), :, columns(j)],
                right_slots.at[slot, pl.ds(firsts[i], p.count)],
                right_sems.at[slot, i],
            )
            for i, p in enumerate(pairs)
        ]

    def turn_in(m, at):
        if outputs == 1:
            turned[0, :, at : at + frames] = stage[m].T
            return
        for b in range(width // rows):
            which = jnp.where(core == b % CORES, 0, 1)
            place = (b // CORES) * rows
            block = stage[m, :, b * rows : (b + 1) * rows].T
            turned[which, place : place + rows, at : at + frames] = block

    @pl.when(works)
    def add_up():
        copies = []
        for i, p in enumerate(pairs):
            left = lefts[i] if p.share is None else lefts[i].at[p.share]
            source = left.at[pl.ds(p.left_first, p.count), :, pl.ds(first_column, width)]
            copies.append(
                pltpu.make_async_copy(source, stage.at[pl.ds(firsts[i], p.count)], sems.at[i])
            )
            copies[i].start()
        for copy in right_copies(0, 0):
            copy.start()
        for i, p in enumerate(pairs):
            copies[i].wait()
            for m in range(firsts[i], firsts[i] + p.count):
                turn_in(m, m * frames)

        def fill(j, slot):
            for copy in right_copies(j, slot):
                copy.wait()

        def add(j, slot):
            right = right_slots[slot].reshape(-1, step)
            for i in range(outputs):
                outs[i][:, columns(j)] = product(turned[i], right).astype(BF16)

        def start(j, slot):
            for copy in right_copies(j, slot):
                copy.start()

        def two_steps(i, carry):
            j = 2 * i
            fill(j + 1, 1)
            add(j, 0)

            @pl.when(j + 2 < steps)
            def next_block():
                start(j + 2, 0)

            @pl.when(j + 3 < steps)
            def block_after():
                fill(j + 2, 0)
                add(j + 1, 1)
                start(j + 3, 1)

            @pl.when(j + 3 >= steps)
            def last_block():
                add(j + 1, 1)

            return carry

        fill(0, 0)
        if steps == 1:
            add(0, 0)
        else:
            start(1, 1)
            lax.fori_loop(0, steps // 2, two_steps, 0)
            if steps % 2:
                fill(steps - 1, 0)
                add(steps - 1, 0)

    if skip_ends:

        @pl.when(jnp.logical_not(works))
        def nothing():
            for out in outs:
                out[...] = jnp.zeros(out.shape, BF16)


def weight_grad(pairs, first_column, width, rows, after=(), outputs=1, skip_ends=False):
    columns = pairs[0].right.shape[2]
    frames = pairs[0].right.shape[1]
    step = min(columns, 2 * BLOCK // outputs)
    micros = sum(p.count for p in pairs)
    call = Call()
    call.take([p.left for p in pairs], anywhere)
    call.take([p.right for p in pairs], anywhere)
    call.take(after, anywhere)
    call.give([((width // outputs, columns), BF16)] * outputs, in_vmem, pltpu.VMEM)
    scratch = [
        pltpu.VMEM((micros, frames, width), BF16),
        pltpu.VMEM((outputs, width // outputs, micros * frames), BF16),
        pltpu.VMEM((2, micros, frames, step), BF16),
        pltpu.SemaphoreType.DMA((len(pairs),)),
        pltpu.SemaphoreType.DMA((2, len(pairs))),
    ]
    bare = [p._replace(left=None, right=None) for p in pairs]
    body = functools.partial(
        weight_grad_kernel, bare, first_column, rows, step, outputs, skip_ends
    )
    return call.run(body, scratch, 0, limit=20 * 2**20)


class Part(NamedTuple):
    grads: Any
    column: int
    width: int
    result: int
    place: int
    tall: bool


def added_terms(part, grads, rows, index):
    block = pl.ds(pl.multiple_of(index * rows, rows), rows)
    total = None
    for grad in grads:
        term = grad[block, part.column : part.column + part.width].astype(F32)
        total = term if total is None else total + term
    return total


def arrived(came, side, at, width):
    for pair in came:
        if at < pair[side].shape[1]:
            return pair[side][:, at : at + width].astype(F32)
        at -= pair[side].shape[1]


def send_kernel(parts, rows, hop, joined, *refs):
    refs = list(refs)
    grads = [[refs.pop(0) for _ in range(p.grads)] for p in parts]
    came = [(refs.pop(0), refs.pop(0)) for _ in range(joined)]
    sends = refs[-2:]
    chip = lax.axis_index("batch") // CORES
    last = lax.axis_size("batch") // CORES - 1
    places = (jnp.minimum(chip + last - (hop - 1), last), jnp.maximum(chip - last + (hop - 1), 0))
    for d in range(2):
        at = 0
        for part, terms in zip(parts, grads):
            total = added_terms(part, terms, rows, places[d])
            if joined:
                total = total + arrived(came, d, at, part.width)
            sends[d][:, at : at + part.width] = total.astype(BF16)
            at += part.width


def finish_kernel(parts, rows, result_count, joined, *refs):
    refs = list(refs)
    grads = [[refs.pop(0) for _ in range(p.grads)] for p in parts]
    came = [(refs.pop(0), refs.pop(0)) for _ in range(joined)]
    total, turned, sems = refs[-3:]
    results = refs[-4 - result_count : -4]
    refs[-4][...] = jnp.zeros(refs[-4].shape, F32)
    chip = lax.axis_index("batch") // CORES
    copies, at = [], 0
    for i, (part, terms) in enumerate(zip(parts, grads)):
        own = slice(at, at + part.width)
        total[:, own] = (
            added_terms(part, terms, rows, chip)
            + arrived(came, 0, at, part.width)
            + arrived(came, 1, at, part.width)
        )
        result = results[part.result]
        if part.tall:
            turned[...] = total[:, own].T
            source, target = turned, result.at[pl.ds(part.place, part.width), :]
        else:
            source = total.at[pl.ds(0, result.shape[0]), pl.ds(at, part.width)]
            target = result.at[:, pl.ds(part.place, part.width)]
        copies.append(pltpu.make_async_copy(source, target, sems.at[i]))
        copies[i].start()
        at += part.width
    for copy in copies:
        copy.wait()


class Piece:
    def __init__(self, parts, first_hop):
        self.parts, self.hop, self.first_hop = parts, first_hop - 1, first_hop
        self.came = []
        self.width = sum(p.width for p in parts)

    def arrivals(self):
        return [x for pair in self.came for x in pair]

    def joined(self, other):
        piece = Piece(self.parts + other.parts, self.first_hop)
        piece.hop, piece.came = self.hop, self.came + other.came
        return piece


class Line:
    def __init__(self, exchange, rows, results, before):
        self.chips, self.rows, self.before = exchange.chips, rows, before
        self.results = {}
        self.shapes = results

    def bare(self, piece, names=None):
        parts = [p._replace(grads=len(p.grads)) for p in piece.parts]
        return parts if names is None else [
            p._replace(result=names.index(p.result)) for p in parts
        ]

    def send(self, piece, after=()):
        piece.hop += 1
        shape = (self.rows, piece.width)
        call = Call()
        call.take([g for p in piece.parts for g in p.grads], in_vmem, pltpu.VMEM)
        call.take(piece.arrivals(), in_vmem, pltpu.VMEM)
        call.take([self.before, *after], anywhere)
        call.give([(shape, BF16)] * 2, in_vmem, pltpu.VMEM)
        parts = self.bare(piece)
        up, down = call.run(
            functools.partial(send_kernel, parts, self.rows, piece.hop, len(piece.came)), [], 0
        )
        self.before = up
        edge = piece.first_hop - 1
        last = self.chips - 1
        piece.came = [(
            self.moved(up, [z for z in range(last) if edge <= z < piece.hop], 1),
            self.moved(down, [z for z in range(1, last + 1) if edge <= last - z < piece.hop], -1),
        )]

    def moved(self, value, senders, by):
        pairs = [(CORES * z + c, CORES * (z + by) + c) for z in senders for c in range(CORES)]
        return lax.ppermute(value, "batch", pairs)

    def finish(self, piece):
        names = sorted({p.result for p in piece.parts})
        parts = self.bare(piece, names)
        call = Call()
        call.take([g for p in piece.parts for g in p.grads], in_vmem, pltpu.VMEM)
        call.take(piece.arrivals(), in_vmem, pltpu.VMEM)
        call.take([self.before], anywhere)
        call.give([(self.shapes[n], F32) for n in names], anywhere, pltpu.HBM)
        call.give([((8, LANES), F32)], in_vmem, pltpu.VMEM)
        shape = (self.rows, piece.width)
        tall = max([p.width for p in parts if p.tall], default=8)
        scratch = [
            pltpu.VMEM(shape, F32),
            pltpu.VMEM((tall, self.rows), F32),
            pltpu.SemaphoreType.DMA((len(parts),)),
        ]
        done = call.run(
            functools.partial(finish_kernel, parts, self.rows, len(names), len(piece.came)),
            scratch,
            0,
        )
        self.results.update(zip(names, done))
        self.before = done[-1]


def table_gradient(row_grads, codes, blocks):
    chosen = lax.broadcasted_iota(jnp.int32, (blocks, codes.shape[0]), 0) == codes
    return jnp.sum(jnp.where(chosen[:, :, None, None], row_grads[None], 0.0), axis=1)


class Exchange:
    def __init__(self, batch):
        self.batch = batch
        self.chips = batch // CORES
        self.by_hops = batch % CORES == 0 and 2 <= self.chips <= LINE
        self.ends_hand_over = self.by_hops and self.chips == LINE

    def swap(self, x):
        if not self.by_hops:
            return None
        return lax.ppermute(x, "batch", [(b, b ^ 1) for b in range(self.batch)])

    def both(self, x):
        return [in_hbm(x), self.swap(x)]

    def inward(self, x, sections=None):
        top = self.batch - CORES
        pairs = [(c, CORES + c) for c in range(CORES)]
        pairs += [(top + c, top - CORES + c) for c in range(CORES)]
        if sections is None:
            return lax.ppermute(x, "batch", pairs)
        pairs = [(s * self.batch + a, s * self.batch + b) for s in sections for a, b in pairs]
        return lax.ppermute(x, ("section", "batch"), pairs)

    def sources(self, x):
        return [in_hbm(x), self.inward(x)] if self.ends_hand_over else [in_hbm(x)]


def sums_by_hops(plan, exchange, back, down, up, lefts, table_grad):
    chips, rows = exchange.chips, plan.rows
    features, hidden_units = plan.features, plan.hidden_units
    core = lax.axis_index("batch") % CORES
    share = features // CORES
    swap = exchange.swap
    table_size = table_grad.shape[0]
    results = [
        (rows, 3 * features),
        (rows, features),
        (rows, hidden_units),
        (hidden_units, rows),
        (table_size, rows),
    ]
    line = Line(exchange, rows, results, up)

    def of(right, first_column):
        rights = exchange.both(right)
        pairs = [Pair(left, i, rights[i], plan.micros) for i, left in enumerate(lefts)]
        (grad,) = weight_grad(pairs, first_column, share, rows, [line.before])
        line.before = grad
        return grad

    ups = Piece([Part([up], 0, hidden_units, 2, 0, False)], 1)
    line.send(ups)
    first = 2 if exchange.ends_hand_over else 1
    downs = Piece([Part([down[0], swap(down[1])], 0, hidden_units, 3, 0, True)], first)
    line.send(downs)
    qkv = of(back.grad_packed, 0)
    out = of(back.grad_attn, share)
    norms = table_grad + swap(table_grad)
    norms = norms.reshape(table_size, chips, CORES, rows)
    norms = lax.dynamic_index_in_dim(norms, core, 2, keepdims=False).transpose(1, 0, 2)
    norms = jnp.pad(norms.astype(BF16), ((0, 0), (0, rows - table_size), (0, 0)))
    norms = norms.reshape(chips * rows, rows)
    others = Piece(
        [
            Part([qkv], 0, 3 * features, 0, 0, False),
            Part([out], 0, features, 1, 0, False),
            Part([norms], 0, rows, 4, 0, False),
        ],
        1,
    )
    last = chips - 1
    while downs.hop < last:
        line.send(downs)
    line.send(others, ups.arrivals())
    rest = ups.joined(others)
    if rest.hop < last:
        line.send(rest, downs.arrivals())
    line.finish(downs)
    while rest.hop < last:
        line.send(rest)
    line.finish(rest)
    return [line.results[i] for i in range(len(results))]


def sums_by_scatter(plan, kept, back, table_grad):
    features = plan.features
    share = features // CORES
    core = lax.axis_index("batch") % CORES

    def local(lefts, rights, column):
        pairs = [Pair(left, None, right, left.shape[0]) for left, right in zip(lefts, rights)]
        if column is None:
            mine, other = weight_grad(pairs, 0, features, plan.rows, outputs=2)
        else:
            (left,), (right,) = lefts, rights
            mine, other = [
                weight_grad(
                    [Pair(left, i, right, left.shape[1])], column, share, plan.rows
                )[0]
                for i in range(CORES)
            ]
        even, odd = jnp.where(core == 0, mine, other), jnp.where(core == 0, other, mine)
        blocks = [x.reshape(-1, 1, plan.rows, x.shape[1]) for x in (even, odd)]
        return jnp.concatenate(blocks, axis=1).reshape(features, -1)

    def scattered(x, dimension):
        return lax.psum_scatter(
            x, "batch", scatter_dimension=dimension, tiled=True
        ).astype(F32)

    grad_y = [back.y_early, back.y_last]
    down = local([jnp.concatenate(grad_y, axis=0)], [kept.act], None)
    grad_up = jnp.concatenate([back.up_early, back.up_last], axis=0)
    return (
        scattered(local([kept.left], [back.grad_packed], 0), 0),
        scattered(local([kept.left], [back.grad_attn], share), 0),
        scattered(local([kept.left], [grad_up], 2 * share), 0),
        scattered(down, 0).T,
        scattered(table_grad, 1),
    )


def per_device(
    frames_in, cotangent, qkv_weight, out_weight, up_weight, down_weight, norm_table, lengths,
    codebooks,
):
    sections = lax.axis_size("section")
    batch = lax.axis_size("batch")
    section = lax.axis_index("section")
    micros = lengths.shape[0]
    tokens, features = frames_in.shape
    frames = tokens // micros
    plan = Plan(
        sections, micros, frames, features, up_weight.shape[2], max(features // batch, LANES)
    )
    frames_all = frames_in.reshape(micros, frames, features)
    cot_all = cotangent.reshape(micros, frames, features)

    state = State(
        numbers=[lengths, codebooks],
        info=None,
        table=norm_table[0],
        weights=Weights(qkv_weight[0], out_weight[0], up_weight[0], down_weight[0]),
    )
    exchange = Exchange(batch)

    share = features // CORES

    def down_pairs(grad_ys, act):
        firsts = [span[0] for span in plan.up_spans()]
        return [Pair(y, None, act, y.shape[0], 0, at) for y, at in zip(grad_ys, firsts)]

    def up_pairs(grad_up, first):
        count = grad_up[0].shape[0]
        return [
            Pair(left, i, g, count, first, 0) for i, (left, g) in enumerate(zip(lefts, grad_up))
        ]

    before_bwd = [[] for _ in range(plan.ticks())]
    incoming = arriving = None
    working = lambda micro: 0 <= micro < micros
    for tick in range(plan.ticks()):
        sent = returned = None
        if tick < plan.fwd_ticks():
            last_fwd = tick == plan.fwd_ticks() - 1 and exchange.ends_hand_over
            state, output, act_in = run_forward(
                plan, tick, state, incoming, frames_all, second_first if last_fwd else None
            )
            if tick == micros - 1 and exchange.ends_hand_over:
                second_first = exchange.inward(first_sections(state.kept.second), [0])
            onward = [
                (s, s + 1) for s in range(sections - 1) if working(plan.fwd_id(tick, s))
            ]
            if onward:
                sent = lax.ppermute(output, "section", onward)
        if tick >= sections - 1:
            late = tick == plan.ticks() - 1
            redo = None
            if tick >= plan.ticks() - 2 and exchange.ends_hand_over:
                redo = (second_rest, act_in)
            state, output, redone = run_backward(
                plan, tick, state, arriving, cot_all, before_bwd[tick], FIRST if late else WHOLE,
                (), redo,
            )
            act_in = act_in if redone is None else redone
            if late:
                after = []
                if exchange.by_hops:
                    y_last = exchange.sources(state.back.y_last)
                    up_last = exchange.both(state.back.up_last)
                    after = up_early[1:] + y_early[1:]
                state, output, _ = run_backward(
                    plan, tick, state, arriving, cot_all, after, SECOND, output
                )
            output = output[0]
            backward = [
                (s, s - 1) for s in range(1, sections) if working(plan.bwd_id(tick, s))
            ]
            if backward:
                returned = lax.ppermute(output, "section", backward)
        incoming, arriving = sent, returned
        if exchange.by_hops:
            if tick == plan.fwd_ticks() - 1:
                lefts = exchange.both(state.kept.left)
                before_bwd[tick + 1] += lefts[1:]
                if exchange.ends_hand_over:
                    (act_in,) = act_in
                    second_rest = exchange.inward(state.kept.second, range(1, sections))
            if tick == plan.ticks() - 2:
                y_early = exchange.sources(state.back.y_early)
                up_early = exchange.both(state.back.up_early)

    blocks = norm_table.shape[1] // 4
    codes = codebooks * (section % 2)
    table_grad = table_gradient(state.back.row_grads, codes, blocks).reshape(norm_table.shape[1:])
    if exchange.by_hops:
        sides = list(zip(y_early, y_last))
        pairs = down_pairs(sides[0], in_hbm(state.kept.act))
        if exchange.ends_hand_over:
            pairs += down_pairs(sides[1], act_in)
        ready = [output, up_last[1], up_early[1]]
        down = weight_grad(
            pairs, 0, features, plan.rows, ready, 2, exchange.ends_hand_over
        )
        pairs = up_pairs(up_early, 0) + up_pairs(up_last, micros - 1)
        (up,) = weight_grad(pairs, 2 * share, share, plan.rows, down[:1])
        sums = sums_by_hops(plan, exchange, state.back, down, up, lefts, table_grad)
    else:
        sums = sums_by_scatter(plan, state.kept, state.back, table_grad)
    return (
        state.kept.layer_out.reshape(1, tokens, features),
        state.back.grad_in.reshape(1, tokens, features),
    ) + tuple(x[None] for x in sums)


def solution(mesh):
    section, batch = mesh.axis_names
    over_batch = P(batch)
    over_section = P(section)
    both = P(section, batch, None)
    columns = P(section, None, batch)
    in_specs = (over_batch,) * 2 + (over_section,) * 5 + (over_batch,) * 2
    out_specs = (both,) * 5 + (columns,) * 2
    return jax.shard_map(
        per_device, mesh=mesh, in_specs=in_specs, out_specs=out_specs, check_vma=False
    )
```

```python
import functools
from typing import Any, NamedTuple

import jax
import jax.numpy as jnp
from jax import lax
from jax.experimental import pallas as pl
from jax.experimental.pallas import tpu as pltpu
from jax.sharding import PartitionSpec as P

HEADS = 16
GROUP = 4
BLOCK = 512
LANES = 128
CORES = 2
VMEM_LIMIT = 14 * 2**20
WHOLE, FIRST, SECOND = 0, 1, 2
LINE = 4

epsilon = 1e-05
masked_score = -1e30
BF16 = jnp.bfloat16
F32 = jnp.float32

in_vmem = pl.BlockSpec(memory_space=pltpu.VMEM)
in_smem = pl.BlockSpec(memory_space=pltpu.SMEM)
anywhere = pl.BlockSpec(memory_space=pl.ANY)


class Weights(NamedTuple):
    qkv: Any
    out: Any
    up: Any
    down: Any


class Reread(NamedTuple):
    entry: Any
    packed: Any
    probs: Any
    hidden: Any
    slope: Any


class Kept(NamedTuple):
    layer_out: Any
    left: Any
    second: Any
    act: Any


class Back(NamedTuple):
    grad_in: Any
    y_early: Any
    y_last: Any
    up_early: Any
    up_last: Any
    grad_attn: Any
    grad_packed: Any
    row_grads: Any


def product(left, right):
    return lax.dot_general(left, right, (((1,), (0,)), ((), ())), preferred_element_type=F32)


def product_last(left, right):
    return lax.dot_general(left, right, (((1,), (1,)), ((), ())), preferred_element_type=F32)


def product_first(left, right):
    return lax.dot_general(left, right, (((0,), (0,)), ((), ())), preferred_element_type=F32)


def normalize(values):
    centre = values - jnp.mean(values, axis=-1, keepdims=True)
    reciprocal = lax.rsqrt(jnp.mean(centre * centre, axis=-1, keepdims=True) + epsilon)
    return centre * reciprocal, reciprocal


def normalize_back(gradient, normal_part, reciprocal, gain_row):
    scaled = gradient * (1.0 + gain_row)
    centred = scaled - jnp.mean(scaled, axis=-1, keepdims=True)
    return reciprocal * (
        centred - normal_part * jnp.mean(scaled * normal_part, axis=-1, keepdims=True)
    )


def gelu_and_slope(u):
    root = 0.7978845608028654
    square = u * u
    bent = jnp.tanh(root * u * (1.0 + 0.044715 * square))
    half = 0.5 * (1.0 + bent)
    slope = half + 0.5 * u * (1.0 - bent * bent) * (root * (1.0 + 3 * 0.044715 * square))
    return u * half, slope


def stacked_heads(block, head_size):
    owner = lax.broadcasted_iota(jnp.int32, block.shape, 1) // head_size
    zero = jnp.zeros_like(block)
    return jnp.concatenate([jnp.where(owner == h, block, zero) for h in range(GROUP)], axis=0)


def beside(stack, frames):
    return jnp.concatenate([stack[h * frames : (h + 1) * frames] for h in range(GROUP)], axis=1)


def table_rows(table, code):
    pair = table[pl.ds(pl.multiple_of((code // 2) * 8, 8), 8), :]
    return jnp.where(code % 2 == 1, pair[4:8], pair[0:4])


class Saver:
    def __init__(self, sems, base):
        self.sems, self.base, self.pending = sems, base, []

    def __call__(self, source, target):
        copy = pltpu.make_async_copy(source, target, self.sems.at[self.base + len(self.pending)])
        copy.start()
        self.pending.append(copy)

    def spread(self, source, buffers, spans, slot):
        sem = self.sems.at[self.base + len(self.pending)]
        copies = []
        for buffer, (first, end) in zip(buffers, spans):
            if buffer is None:
                continue
            place = jnp.clip(slot - first, 0, end - first - 1)
            copies.append(pltpu.make_async_copy(source, buffer.at[place], sem))
            pl.when((slot >= first) & (slot < end))(copies[-1].start)
        self.pending.append(copies[0])

    def wait(self):
        for copy in self.pending:
            copy.wait()


def turn(source, target, row0, col0, side_by, strips, sems, base):
    slots, side, _ = strips.shape
    count = side_by // side

    def strip(i):
        c = pl.multiple_of(col0 + i * side, side)
        return pltpu.make_async_copy(
            strips.at[i % slots],
            target.at[pl.ds(c, side), pl.ds(row0, side_by)],
            sems.at[base + i % slots],
        )

    def one_strip(i, carry):
        @pl.when(i >= slots)
        def slot_is_free():
            strip(i - slots).wait()

        c = pl.multiple_of(col0 + i * side, side)
        strips[i % slots] = source[row0 : row0 + side_by, pl.ds(c, side)].T
        strip(i).start()
        return carry

    lax.fori_loop(0, count, one_strip, 0)
    for i in range(count - slots, count):
        strip(i).wait()


def redo_activated(normed_in, weight, act_out, normed, act_slots, sems, base):
    micros, frames, _ = normed.shape
    step = act_slots.shape[3]
    load = pltpu.make_async_copy(normed_in, normed, sems.at[base])
    load.start()
    load.wait()
    copies = []
    for j in range(0, weight.shape[1], step):
        slot = (j // step) % 2
        if len(copies) >= 2:
            copies[-2].wait()
        rows = normed[...].reshape(micros * frames, -1)
        act = gelu_and_slope(product(rows, weight[:, j : j + step]))[0].astype(BF16)
        act_slots[slot] = act.reshape(micros, frames, step)
        target = act_out.at[:, :, pl.ds(j, step)]
        copies.append(pltpu.make_async_copy(act_slots.at[slot], target, sems.at[base + slot]))
        copies[-1].start()
    for copy in copies[-2:]:
        copy.wait()


def copy_kernel(source, target, held, sem):
    @pl.when(lax.axis_index("section") == 0)
    def copy():
        for start, end in ((source, held), (held, target)):
            moving = pltpu.make_async_copy(start, end, sem)
            moving.start()
            moving.wait()


def first_sections(x):
    call = Call()
    call.take([x], anywhere, pltpu.HBM)
    call.give(like([x]), anywhere, pltpu.HBM)
    return call.run(copy_kernel, [pltpu.VMEM(x.shape, x.dtype), pltpu.SemaphoreType.DMA], 0)[0]


def redo_scratch(plan):
    lead = (plan.micros, plan.frames)
    return [
        pltpu.VMEM(lead + (plan.features,), BF16),
        pltpu.VMEM((2,) + lead + (2 * BLOCK,), BF16),
    ]


def beside_an_end():
    chip = lax.axis_index("batch") // CORES
    return (chip == 1) | (chip == lax.axis_size("batch") // CORES - 2)


class Plan(NamedTuple):
    sections: int
    micros: int
    frames: int
    features: int
    hidden_units: int
    rows: int

    def fwd_ticks(self):
        return self.micros + self.sections - 1

    def ticks(self):
        return self.micros + 2 * (self.sections - 1)

    def up_spans(self):
        return (0, self.micros - 1), (self.micros - 1, self.micros)

    def bwd_reaches(self, tick):
        low, high = tick - 2 * (self.sections - 1), tick - (self.sections - 1)
        spread = tuple(low < end and high >= first for first, end in self.up_spans())
        return (True,) + spread + spread + (True,) * 3

    def bwd_uses(self, tick, part):
        first = (False,) + (True,) * 5 + (False, False)
        halves = {WHOLE: (True,) * 8, FIRST: first, SECOND: tuple(not f for f in first)}
        return tuple(r and h for r, h in zip(self.bwd_reaches(tick), halves[part]))

    def fwd_id(self, tick, section):
        return tick - section

    def bwd_id(self, tick, section):
        return tick - 2 * (self.sections - 1) + section


def forward_kernel(plan, tick, has_incoming, loads_weights, redoes, *refs):
    refs = list(refs)
    take = lambda n: [refs.pop(0) for _ in range(n)]
    if loads_weights:
        lengths, codebooks, given_table = take(3)
        given = Weights(*take(4))
    else:
        info, table = take(2)
        weight = Weights(*take(4))
        take(4)
    incoming = take(1)[0] if has_incoming else None
    (frames_in,) = take(1)
    if redoes:
        (second_in,) = take(1)
    if loads_weights:
        info, table = take(2)
        weight = Weights(*take(4))
    else:
        take(len(Reread._fields) + len(Kept._fields))
    turned = Weights(*take(4))
    reread = Reread(*take(5))
    kept = Kept(*take(4))
    (outgoing,) = take(1)
    if redoes:
        (act_in,) = take(1)
        redo = (refs.pop(), refs.pop())[::-1]
    entry, packed, probs, hidden, slope, normed, left, attended, act, strips, sems = refs

    micros, frames, features, hidden_units, rows_kept = plan[1:]
    head_size = features // HEADS
    group_width = GROUP * head_size
    section = lax.axis_index("section")
    core = lax.axis_index("batch") % CORES
    is_nar = section % 2
    micro = plan.fwd_id(tick, section)
    active = (micro >= 0) & (micro < micros)
    slot = jnp.clip(micro, 0, micros - 1)

    loads = []
    if loads_weights:
        for i in range(micros):
            info[i] = lengths[i]
            info[micros + i] = codebooks[i]
        pairs = [(given_table, table)] + list(zip(given, weight))
        for i, (source, target) in enumerate(pairs):
            loads.append(pltpu.make_async_copy(source, target, sems.at[i]))
        loads[0].start()
        loads[1].start()
    base = len(loads)

    def ready(i):
        if not loads_weights:
            return
        loads[i].wait()
        if i == 1:
            loads[2].start()
            loads[3].start()
        if i == 2:
            loads[4].start()

    @pl.when(active)
    def forward():
        save = Saver(sems, base)
        length = info[slot]
        code = info[micros + slot] * is_nar

        def own_input():
            pltpu.sync_copy(frames_in.at[slot], entry)

        if has_incoming:
            pl.when(section == 0)(own_input)

            @pl.when(section != 0)
            def passed_input():
                entry[...] = incoming[...]

        else:
            own_input()

        save(entry, reread.entry.at[slot])
        share = features // CORES

        def share_columns(source, first):
            for b in range(features // rows_kept):
                at = first + (b // CORES) * rows_kept
                left[b % CORES, :, at : at + rows_kept] = source[
                    :, b * rows_kept : (b + 1) * rows_kept
                ]

        ready(0)
        rows = table_rows(table, code)
        residual = entry[...].astype(F32)
        normal_one, _ = normalize(residual)
        normed[...] = (normal_one * (1.0 + rows[0:1]) + rows[1:2]).astype(BF16)
        share_columns(normed, 0)
        ready(1)
        for j in range(0, 3 * features, BLOCK):
            packed[:, j : j + BLOCK] = product(normed[...], weight.qkv[:, j : j + BLOCK]).astype(
                BF16
            )
        save(packed, reread.packed.at[slot])
        tall = (GROUP * frames, frames)
        query_ids = lax.rem(lax.broadcasted_iota(jnp.int32, tall, 0), frames)
        key_ids = lax.broadcasted_iota(jnp.int32, tall, 1)
        allowed = (key_ids < length) & (key_ids <= query_ids + is_nar * frames)
        inv_root = head_size ** (-0.5)
        for g in range(HEADS // GROUP):
            lo, hi = g * group_width, (g + 1) * group_width
            queries = stacked_heads(packed[:, lo:hi], head_size)
            keys = packed[:, features + lo : features + hi]
            values = stacked_heads(packed[:, 2 * features + lo : 2 * features + hi], head_size)
            scores = jnp.where(allowed, product_last(queries, keys) * inv_root, masked_score)
            exp_scores = jnp.exp(scores - jnp.max(scores, axis=-1, keepdims=True))
            total = jnp.sum(exp_scores, axis=-1, keepdims=True)
            group_probs = (exp_scores * (1.0 / total)).astype(BF16)
            probs[g * GROUP * frames : (g + 1) * GROUP * frames, :] = group_probs
            attended[:, lo:hi] = product(beside(group_probs, frames), values).astype(BF16)
        save(probs, reread.probs.at[slot])
        share_columns(attended, share)
        ready(2)
        for j in range(0, features, BLOCK):
            hidden[:, j : j + BLOCK] = residual[:, j : j + BLOCK] + product(
                attended[...], weight.out[:, j : j + BLOCK]
            )
        save(hidden, reread.hidden.at[slot])
        normal_two, _ = normalize(hidden[...])
        normed[...] = (normal_two * (1.0 + rows[2:3]) + rows[3:4]).astype(BF16)
        share_columns(normed, 2 * share)
        save(normed, kept.second.at[slot])
        save(left.at[core], kept.left.at[0, slot])
        save(left.at[1 - core], kept.left.at[1, slot])
        ready(3)
        for j in range(0, hidden_units, BLOCK):
            value, gradient = gelu_and_slope(product(normed[...], weight.up[:, j : j + BLOCK]))
            act[:, j : j + BLOCK] = value.astype(BF16)
            slope[:, j : j + BLOCK] = gradient.astype(BF16)
            if (j + BLOCK) % (hidden_units // 2) == 0:
                done = pl.ds(j + BLOCK - hidden_units // 2, hidden_units // 2)
                save(slope.at[:, done], reread.slope.at[slot, :, done])
                save(act.at[:, done], kept.act.at[slot, :, done])
        ready(4)
        for j in range(0, features, BLOCK):
            outgoing[:, j : j + BLOCK] = (
                hidden[:, j : j + BLOCK] + product(act[...], weight.down[:, j : j + BLOCK])
            ).astype(BF16)
        save(outgoing, kept.layer_out.at[slot])
        save.wait()

    if redoes:

        @pl.when((section == 0) & beside_an_end())
        def redo_early():
            redo_activated(second_in, weight.up, act_in, *redo, sems, base)

    units = []
    for source, target in zip(weight, turned):
        total_rows, total_cols = source.shape
        for r in range(0, total_rows, features):
            for c in range(0, total_cols, features):
                units.append((source, target, r, c))
    cut = len(units) // 3
    pieces = (units[:cut], units[cut:])
    piece = jnp.where(micro < 0, tick, micro - micros + section)

    @pl.when(jnp.logical_not(active))
    def wait_for_weights():
        for i in range(base):
            ready(i)

    for k in range(len(pieces)):

        @pl.when(jnp.logical_not(active) & (piece == k))
        def one_piece(k=k):
            for source, target, r, c in pieces[k]:
                turn(source, target, r, c, features, strips, sems, base)


def backward_kernel(plan, tick, part, has_arriving, present, unread, redoes, *refs):
    refs = list(refs)
    take = lambda n: [refs.pop(0) for _ in range(n)]
    info, table = take(2)
    turned = Weights(*(take(1) + [None] * 3 if part == SECOND else take(4)))
    take(unread)
    if redoes:
        second_in, up_weight, _ = take(3)
    arriving = take(1)[0] if has_arriving else None
    (cotangent,) = take(1)
    take(len(Reread._fields))
    used = plan.bwd_uses(tick, part)
    take(sum(u and p for u, p in zip(used, present)))
    halfway = take(3) if part == SECOND else None
    reread = Reread(*take(5))
    back = Back(*[take(1)[0] if u else None for u in used])
    if part == FIRST:
        halfway = take(3)
    else:
        (returning,) = take(1)
    if redoes:
        (act_in,) = take(1)
        redo = (refs.pop(), refs.pop())[::-1]
    (entry, packed, probs, hidden, slope, grad_y, grad_up, wide, grad_hidden, grad_attn, mixed,
     grad_packed, row_grads, sems) = refs

    micros, frames, features, hidden_units, _ = plan[1:]
    head_size = features // HEADS
    group_width = GROUP * head_size
    section = lax.axis_index("section")
    is_nar = section % 2
    micro = plan.bwd_id(tick, section)
    active = (micro >= 0) & (micro < micros)
    slot = jnp.clip(micro, 0, micros - 1)

    if redoes:
        through = micro >= micros if part == WHOLE else micro == micros

        @pl.when(through & beside_an_end())
        def redo_late():
            redo_activated(second_in, up_weight, act_in, *redo, sems, 0)

    def start_fetches(wanted):
        fetches = []
        for i, target in enumerate((entry, packed, probs, hidden, slope)):
            fetches.append(pltpu.make_async_copy(reread[i].at[slot], target, sems.at[i]))
        for i in (4, 3, 1, 2, 0):
            if i in wanted:
                fetches[i].start()
        return fetches

    def first_half():
        length = info[slot]
        code = info[micros + slot] * is_nar
        fetches = start_fetches((3, 4) if part == FIRST else range(5))
        save = Saver(sems, len(fetches))

        def own_cotangent():
            pltpu.sync_copy(cotangent.at[slot], grad_y)
            live = lax.broadcasted_iota(jnp.int32, (frames, features), 0) < length
            grad_y[...] = jnp.where(live, grad_y[...], jnp.zeros((frames, features), BF16))

        if has_arriving:
            pl.when(section == plan.sections - 1)(own_cotangent)

            @pl.when(section != plan.sections - 1)
            def passed_gradient():
                grad_y[...] = arriving[...]

        else:
            own_cotangent()

        save.spread(grad_y, back[1:3], plan.up_spans(), slot)
        rows = table_rows(table, code)
        fetches[4].wait()
        for j in range(0, hidden_units, BLOCK):
            grad_act = product(grad_y[...], turned.down[:, j : j + BLOCK])
            grad_up[:, j : j + BLOCK] = (
                grad_act * slope[:, j : j + BLOCK].astype(F32)
            ).astype(BF16)
        save.spread(grad_up, (back.up_early, back.up_last), plan.up_spans(), slot)
        for j in range(0, features, BLOCK):
            wide[:, j : j + BLOCK] = product(grad_up[...], turned.up[:, j : j + BLOCK])
        fetches[3].wait()
        normal_two, recip_two = normalize(hidden[...])
        grad_two = wide[...]
        row_grads[2:3, :] = jnp.sum(grad_two * normal_two, axis=0, keepdims=True)
        row_grads[3:4, :] = jnp.sum(grad_two, axis=0, keepdims=True)
        grad_hidden[...] = grad_y[...].astype(F32) + normalize_back(
            grad_two, normal_two, recip_two, rows[2:3]
        )
        grad_attn[...] = grad_hidden[...].astype(BF16)
        save(grad_attn, back.grad_attn.at[slot])
        for j in range(0, features, BLOCK):
            mixed[:, j : j + BLOCK] = product(
                grad_attn[...], turned.out[:, j : j + BLOCK]
            ).astype(BF16)
        return fetches, save

    def second_half(fetches, save):
        code = info[micros + slot] * is_nar
        rows = table_rows(table, code)
        fetches[1].wait()
        fetches[2].wait()
        inv_root = head_size ** (-0.5)
        for g in range(HEADS // GROUP):
            lo, hi = g * group_width, (g + 1) * group_width
            queries = stacked_heads(packed[:, lo:hi], head_size)
            keys = stacked_heads(packed[:, features + lo : features + hi], head_size)
            values = packed[:, 2 * features + lo : 2 * features + hi]
            group_mixed = stacked_heads(mixed[:, lo:hi], head_size)
            group_probs = probs[g * GROUP * frames : (g + 1) * GROUP * frames, :]
            wide_probs = group_probs.astype(F32)
            grad_probs = product_last(group_mixed, values)
            inner = jnp.sum(wide_probs * grad_probs, axis=-1, keepdims=True)
            grad_scores = (wide_probs * (grad_probs - inner)).astype(BF16)
            grad_packed[:, lo:hi] = (
                product(beside(grad_scores, frames), keys) * inv_root
            ).astype(BF16)
            grad_packed[:, features + lo : features + hi] = (
                product_first(grad_scores, queries) * inv_root
            ).astype(BF16)
            grad_packed[:, 2 * features + lo : 2 * features + hi] = product_first(
                group_probs, group_mixed
            ).astype(BF16)
        save(grad_packed, back.grad_packed.at[slot])
        for j in range(0, features, BLOCK):
            wide[:, j : j + BLOCK] = product(grad_packed[...], turned.qkv[:, j : j + BLOCK])
        fetches[0].wait()
        normal_one, recip_one = normalize(entry[...].astype(F32))
        grad_one = wide[...]
        row_grads[0:1, :] = jnp.sum(grad_one * normal_one, axis=0, keepdims=True)
        row_grads[1:2, :] = jnp.sum(grad_one, axis=0, keepdims=True)
        save(row_grads, back.row_grads.at[slot])
        returning[...] = (
            grad_hidden[...] + normalize_back(grad_one, normal_one, recip_one, rows[0:1])
        ).astype(BF16)
        save(returning, back.grad_in.at[slot])
        save.wait()

    @pl.when(active)
    def backward():
        if part == SECOND:
            fetches = start_fetches((0, 1, 2))
            load = Saver(sems, 5)
            for source, target in zip(halfway, (grad_hidden, mixed, row_grads)):
                load(source, target)
            load.wait()
            second_half(fetches, Saver(sems, 5))
            return
        fetches, save = first_half()
        if part == FIRST:
            for source, target in zip((grad_hidden, mixed, row_grads), halfway):
                save(source, target)
            save.wait()
        else:
            second_half(fetches, save)


def shapes_of(plan):
    micros, frames, features, hidden_units, _ = plan[1:]
    own = (micros, frames)
    reread = Reread(
        entry=(own + (features,), BF16),
        packed=(own + (3 * features,), BF16),
        probs=((micros, HEADS * frames, frames), BF16),
        hidden=(own + (features,), F32),
        slope=(own + (hidden_units,), BF16),
    )
    def buffers(spans, columns):
        return [((end - first, frames, columns), BF16) for first, end in spans]

    left = ((CORES,) + own + (3 * features // CORES,), BF16)
    wide = (own + (features,), BF16)
    kept = Kept(wide, left, wide, (own + (hidden_units,), BF16))
    back = Back(
        wide,
        *buffers(plan.up_spans(), features),
        *buffers(plan.up_spans(), hidden_units),
        grad_attn=wide,
        grad_packed=(own + (3 * features,), BF16),
        row_grads=((micros, 4, features), F32),
    )
    return reread, kept, back


def scratch_of(shapes):
    return [pltpu.VMEM(shape[1:], dtype) for shape, dtype in shapes]


class Call:
    def __init__(self):
        self.args, self.in_specs, self.out_shape, self.out_specs = [], [], [], []
        self.aliases = {}

    def take(self, values, spec, space=None):
        for value in values:
            if space is not None:
                value = pltpu.with_memory_space_constraint(value, space)
            self.args.append(value)
            self.in_specs.append(spec)

    def give(self, shapes, spec, space, updates=None):
        for i, (shape, dtype) in enumerate(shapes):
            if updates is not None:
                self.aliases[updates + i] = len(self.out_shape)
            self.out_shape.append(space(shape, dtype))
            self.out_specs.append(spec)

    def update(self, arrays, shapes, used):
        arrays = arrays or (None,) * len(shapes)
        for array, shape, use in zip(arrays, shapes, used):
            if use and array is not None:
                self.take([array], anywhere, pltpu.HBM)
                self.give([shape], anywhere, pltpu.HBM, len(self.args) - 1)
            elif use:
                self.give([shape], anywhere, pltpu.HBM)

    def run(self, body, scratch, flops, limit=VMEM_LIMIT):
        return list(
            pl.pallas_call(
                body,
                out_shape=self.out_shape,
                in_specs=self.in_specs,
                out_specs=self.out_specs,
                scratch_shapes=scratch,
                input_output_aliases=self.aliases,
                compiler_params=pltpu.CompilerParams(vmem_limit_bytes=limit),
                cost_estimate=pl.CostEstimate(
                    flops=flops, bytes_accessed=0, transcendentals=0
                ),
            )(*self.args)
        )


def updated(old, used, new):
    new = list(new)
    old = old or (None,) * len(used)
    return [new.pop(0) if u else o for o, u in zip(old, used)]


def like(arrays):
    return [(x.shape, x.dtype) for x in arrays]


class State(NamedTuple):
    numbers: Any
    info: Any
    table: Any
    weights: Any
    turned: Any = None
    reread: Any = None
    kept: Any = None
    back: Any = None


def run_forward(plan, tick, state, incoming, frames_in, second_in=None):
    reread_shapes, kept_shapes, _ = shapes_of(plan)
    first = state.turned is None
    at_turned = at_kept = None
    call = Call()
    if first:
        call.take(state.numbers, in_smem)
        call.take([state.table], anywhere)
        call.take(state.weights, anywhere)
    else:
        call.take([state.info], in_smem, pltpu.SMEM)
        call.take([state.table], in_vmem, pltpu.VMEM)
        call.take(state.weights, in_vmem, pltpu.VMEM)
        at_turned = len(call.args)
        call.take(state.turned, anywhere, pltpu.VMEM)
    if incoming is not None:
        call.take([incoming], in_vmem, pltpu.VMEM)
    call.take([frames_in], anywhere)
    if second_in is not None:
        call.take([second_in], anywhere)
    if first:
        call.give([((2 * plan.micros,), jnp.int32)], in_smem, pltpu.SMEM)
        call.give(like([state.table]), in_vmem, pltpu.VMEM)
        call.give(like(state.weights), in_vmem, pltpu.VMEM)
    else:
        at_kept = len(call.args)
        call.take(state.reread + state.kept, anywhere, pltpu.HBM)
    call.give([(w.shape[::-1], BF16) for w in state.weights], anywhere, pltpu.VMEM, at_turned)
    call.give(reread_shapes + kept_shapes, anywhere, pltpu.HBM, at_kept)
    call.give([((plan.frames, plan.features), BF16)], in_vmem, pltpu.VMEM)
    if second_in is not None:
        call.give([kept_shapes.act], anywhere, pltpu.HBM)
    scratch = scratch_of(reread_shapes) + [
        pltpu.VMEM((plan.frames, plan.features), BF16),
        pltpu.VMEM((CORES, plan.frames, 3 * plan.features // CORES), BF16),
        pltpu.VMEM((plan.frames, plan.features), BF16),
        pltpu.VMEM((plan.frames, plan.hidden_units), BF16),
        pltpu.VMEM((2, 256, plan.features), BF16),
        pltpu.SemaphoreType.DMA((24,)),
    ]
    flops = 8 * plan.frames * sum(w.size for w in state.weights)
    if second_in is not None:
        scratch += redo_scratch(plan)
    body = functools.partial(
        forward_kernel, plan, tick, incoming is not None, first, second_in is not None
    )
    got = call.run(body, scratch, flops)
    if first:
        state = state._replace(info=got[0], table=got[1], weights=Weights(*got[2:6]))
        got = got[6:]
    kept = Kept(*got[9:13])
    state = state._replace(turned=Weights(*got[:4]), reread=Reread(*got[4:9]), kept=kept)
    return state, got[13], got[14:]


def run_backward(
    plan, tick, state, arriving, cotangent, after, part=WHOLE, halfway=(), redo=None
):
    reread_shapes, _, back_shapes = shapes_of(plan)
    call = Call()
    call.take([state.info], in_smem, pltpu.SMEM)
    call.take([state.table], in_vmem, pltpu.VMEM)
    call.take(state.turned[:1] if part == SECOND else state.turned, in_vmem, pltpu.VMEM)
    staying = () if part == SECOND else state.weights
    call.take(staying, anywhere, pltpu.VMEM)
    call.take(after, anywhere)
    unread = len(staying) + len(after)
    if redo is not None:
        second_in, act_in = redo
        call.take([second_in], anywhere)
        call.take([state.weights.up], in_vmem, pltpu.VMEM)
        at_act = len(call.args)
        call.take([act_in], anywhere, pltpu.HBM)
    if arriving is not None:
        call.take([arriving], in_vmem, pltpu.VMEM)
    call.take([cotangent], anywhere)
    at_reread = len(call.args)
    call.take(state.reread, anywhere, pltpu.HBM)
    call.give(reread_shapes, anywhere, pltpu.HBM, at_reread)
    used = plan.bwd_uses(tick, part)
    present = [b is not None for b in state.back or (None,) * len(used)]
    call.update(state.back, back_shapes, used)
    narrow = ((plan.frames, plan.features), BF16)
    full = ((plan.frames, plan.features), F32)
    between = [full, narrow, ((4, plan.features), F32)]
    call.take(halfway, anywhere, pltpu.HBM)
    results = between if part == FIRST else [narrow]
    if part == FIRST:
        call.give(results, anywhere, pltpu.HBM)
    else:
        call.give(results, in_vmem, pltpu.VMEM)
    if redo is not None:
        call.give(like([act_in]), anywhere, pltpu.HBM, at_act)
    scratch = scratch_of(reread_shapes) + [
        pltpu.VMEM(*narrow),
        pltpu.VMEM((plan.frames, plan.hidden_units), BF16),
        pltpu.VMEM(*full),
        pltpu.VMEM(*full),
        pltpu.VMEM(*narrow),
        pltpu.VMEM(*narrow),
        pltpu.VMEM((plan.frames, 3 * plan.features), BF16),
        pltpu.VMEM((4, plan.features), F32),
        pltpu.SemaphoreType.DMA((16,)),
    ]
    flops = 8 * plan.frames * sum(w.size for w in state.turned)
    if redo is not None:
        scratch += redo_scratch(plan)
    body = functools.partial(
        backward_kernel, plan, tick, part, arriving is not None, present, unread, redo is not None
    )
    got = call.run(body, scratch, flops if part == WHOLE else flops // 2)
    act_in = got.pop() if redo is not None else None
    got, last = got[: -len(results)], got[-len(results) :]
    back = Back(*updated(state.back, used, got[5:]))
    return state._replace(reread=Reread(*got[:5]), back=back), last, act_in


def in_hbm(x):
    return pltpu.with_memory_space_constraint(x, pltpu.HBM)


class Pair(NamedTuple):
    left: Any
    share: Any
    right: Any
    count: int
    left_first: int = 0
    right_first: int = 0


def weight_grad_kernel(pairs, first_column, rows, step, outputs, skip_ends, *refs):
    lefts, rights = refs[: len(pairs)], refs[len(pairs) : 2 * len(pairs)]
    outs = refs[-5 - outputs : -5]
    stage, turned, right_slots, sems, right_sems = refs[-5:]
    frames, width = stage.shape[1:]
    share = width // outputs
    steps = outs[0].shape[1] // step
    core = lax.axis_index("batch") % CORES
    chip = lax.axis_index("batch") // CORES
    chips = lax.axis_size("batch") // CORES
    works = (chip > 0) & (chip < chips - 1) if skip_ends else chip >= 0
    firsts = [sum(p.count for p in pairs[:i]) for i in range(len(pairs))]
    columns = lambda j: pl.ds(pl.multiple_of(j * step, step), step)

    def right_copies(j, slot):
        return [
            pltpu.make_async_copy(
                rights[i].at[pl.ds(p.right_first, p.count), :, columns(j)],
                right_slots.at[slot, pl.ds(firsts[i], p.count)],
                right_sems.at[slot, i],
            )
            for i, p in enumerate(pairs)
        ]

    def turn_in(m, at):
        if outputs == 1:
            turned[0, :, at : at + frames] = stage[m].T
            return
        for b in range(width // rows):
            which = jnp.where(core == b % CORES, 0, 1)
            place = (b // CORES) * rows
            block = stage[m, :, b * rows : (b + 1) * rows].T
            turned[which, place : place + rows, at : at + frames] = block

    @pl.when(works)
    def add_up():
        copies = []
        for i, p in enumerate(pairs):
            left = lefts[i] if p.share is None else lefts[i].at[p.share]
            source = left.at[pl.ds(p.left_first, p.count), :, pl.ds(first_column, width)]
            copies.append(
                pltpu.make_async_copy(source, stage.at[pl.ds(firsts[i], p.count)], sems.at[i])
            )
            copies[i].start()
        for copy in right_copies(0, 0):
            copy.start()
        for i, p in enumerate(pairs):
            copies[i].wait()
            for m in range(firsts[i], firsts[i] + p.count):
                turn_in(m, m * frames)

        def fill(j, slot):
            for copy in right_copies(j, slot):
                copy.wait()

        def add(j, slot):
            right = right_slots[slot].reshape(-1, step)
            for i in range(outputs):
                outs[i][:, columns(j)] = product(turned[i], right).astype(BF16)

        def start(j, slot):
            for copy in right_copies(j, slot):
                copy.start()

        def two_steps(i, carry):
            j = 2 * i
            fill(j + 1, 1)
            add(j, 0)

            @pl.when(j + 2 < steps)
            def next_block():
                start(j + 2, 0)

            @pl.when(j + 3 < steps)
            def block_after():
                fill(j + 2, 0)
                add(j + 1, 1)
                start(j + 3, 1)

            @pl.when(j + 3 >= steps)
            def last_block():
                add(j + 1, 1)

            return carry

        fill(0, 0)
        if steps == 1:
            add(0, 0)
        else:
            start(1, 1)
            lax.fori_loop(0, steps // 2, two_steps, 0)
            if steps % 2:
                fill(steps - 1, 0)
                add(steps - 1, 0)

    if skip_ends:

        @pl.when(jnp.logical_not(works))
        def nothing():
            for out in outs:
                out[...] = jnp.zeros(out.shape, BF16)


def weight_grad(pairs, first_column, width, rows, after=(), outputs=1, skip_ends=False):
    columns = pairs[0].right.shape[2]
    frames = pairs[0].right.shape[1]
    step = min(columns, 2 * BLOCK // outputs)
    micros = sum(p.count for p in pairs)
    call = Call()
    call.take([p.left for p in pairs], anywhere)
    call.take([p.right for p in pairs], anywhere)
    call.take(after, anywhere)
    call.give([((width // outputs, columns), BF16)] * outputs, in_vmem, pltpu.VMEM)
    scratch = [
        pltpu.VMEM((micros, frames, width), BF16),
        pltpu.VMEM((outputs, width // outputs, micros * frames), BF16),
        pltpu.VMEM((2, micros, frames, step), BF16),
        pltpu.SemaphoreType.DMA((len(pairs),)),
        pltpu.SemaphoreType.DMA((2, len(pairs))),
    ]
    bare = [p._replace(left=None, right=None) for p in pairs]
    body = functools.partial(
        weight_grad_kernel, bare, first_column, rows, step, outputs, skip_ends
    )
    return call.run(body, scratch, 0, limit=(20 if outputs == 2 else 14) * 2**20)


class Part(NamedTuple):
    grads: Any
    column: int
    width: int
    result: int
    place: int
    tall: bool


def added_terms(part, grads, rows, index):
    block = pl.ds(pl.multiple_of(index * rows, rows), rows)
    total = None
    for grad in grads:
        term = grad[block, part.column : part.column + part.width].astype(F32)
        total = term if total is None else total + term
    return total


def arrived(came, side, at, width):
    for pair in came:
        if at < pair[side].shape[1]:
            return pair[side][:, at : at + width].astype(F32)
        at -= pair[side].shape[1]


def send_kernel(parts, rows, hop, joined, *refs):
    refs = list(refs)
    grads = [[refs.pop(0) for _ in range(p.grads)] for p in parts]
    came = [(refs.pop(0), refs.pop(0)) for _ in range(joined)]
    sends = refs[-2:]
    chip = lax.axis_index("batch") // CORES
    last = lax.axis_size("batch") // CORES - 1
    places = (jnp.minimum(chip + last - (hop - 1), last), jnp.maximum(chip - last + (hop - 1), 0))
    for d in range(2):
        at = 0
        for part, terms in zip(parts, grads):
            total = added_terms(part, terms, rows, places[d])
            if joined:
                total = total + arrived(came, d, at, part.width)
            sends[d][:, at : at + part.width] = total.astype(BF16)
            at += part.width


def finish_kernel(parts, rows, result_count, joined, *refs):
    refs = list(refs)
    grads = [[refs.pop(0) for _ in range(p.grads)] for p in parts]
    came = [(refs.pop(0), refs.pop(0)) for _ in range(joined)]
    total, turned, sems = refs[-3:]
    results = refs[-4 - result_count : -4]
    refs[-4][...] = jnp.zeros(refs[-4].shape, F32)
    chip = lax.axis_index("batch") // CORES
    copies, at = [], 0
    for i, (part, terms) in enumerate(zip(parts, grads)):
        own = slice(at, at + part.width)
        total[:, own] = (
            added_terms(part, terms, rows, chip)
            + arrived(came, 0, at, part.width)
            + arrived(came, 1, at, part.width)
        )
        result = results[part.result]
        if part.tall:
            turned[...] = total[:, own].T
            source, target = turned, result.at[pl.ds(part.place, part.width), :]
        else:
            source = total.at[pl.ds(0, result.shape[0]), pl.ds(at, part.width)]
            target = result.at[:, pl.ds(part.place, part.width)]
        copies.append(pltpu.make_async_copy(source, target, sems.at[i]))
        copies[i].start()
        at += part.width
    for copy in copies:
        copy.wait()


class Piece:
    def __init__(self, parts, first_hop):
        self.parts, self.hop, self.first_hop = parts, first_hop - 1, first_hop
        self.came = []
        self.width = sum(p.width for p in parts)

    def arrivals(self):
        return [x for pair in self.came for x in pair]

    def joined(self, other):
        piece = Piece(self.parts + other.parts, self.first_hop)
        piece.hop, piece.came = self.hop, self.came + other.came
        return piece


class Line:
    def __init__(self, exchange, rows, results, before):
        self.chips, self.rows, self.before = exchange.chips, rows, before
        self.results = {}
        self.shapes = results

    def bare(self, piece, names=None):
        parts = [p._replace(grads=len(p.grads)) for p in piece.parts]
        return parts if names is None else [
            p._replace(result=names.index(p.result)) for p in parts
        ]

    def send(self, piece, after=()):
        piece.hop += 1
        shape = (self.rows, piece.width)
        call = Call()
        call.take([g for p in piece.parts for g in p.grads], in_vmem, pltpu.VMEM)
        call.take(piece.arrivals(), in_vmem, pltpu.VMEM)
        call.take([self.before, *after], anywhere)
        call.give([(shape, BF16)] * 2, in_vmem, pltpu.VMEM)
        parts = self.bare(piece)
        up, down = call.run(
            functools.partial(send_kernel, parts, self.rows, piece.hop, len(piece.came)), [], 0
        )
        self.before = up
        edge = piece.first_hop - 1
        last = self.chips - 1
        piece.came = [(
            self.moved(up, [z for z in range(last) if edge <= z < piece.hop], 1),
            self.moved(down, [z for z in range(1, last + 1) if edge <= last - z < piece.hop], -1),
        )]

    def moved(self, value, senders, by):
        pairs = [(CORES * z + c, CORES * (z + by) + c) for z in senders for c in range(CORES)]
        return lax.ppermute(value, "batch", pairs)

    def finish(self, piece):
        names = sorted({p.result for p in piece.parts})
        parts = self.bare(piece, names)
        call = Call()
        call.take([g for p in piece.parts for g in p.grads], in_vmem, pltpu.VMEM)
        call.take(piece.arrivals(), in_vmem, pltpu.VMEM)
        call.take([self.before], anywhere)
        call.give([(self.shapes[n], F32) for n in names], anywhere, pltpu.HBM)
        call.give([((8, LANES), F32)], in_vmem, pltpu.VMEM)
        shape = (self.rows, piece.width)
        tall = max([p.width for p in parts if p.tall], default=8)
        scratch = [
            pltpu.VMEM(shape, F32),
            pltpu.VMEM((tall, self.rows), F32),
            pltpu.SemaphoreType.DMA((len(parts),)),
        ]
        done = call.run(
            functools.partial(finish_kernel, parts, self.rows, len(names), len(piece.came)),
            scratch,
            0,
        )
        self.results.update(zip(names, done))
        self.before = done[-1]


def table_gradient(row_grads, codes, blocks):
    chosen = lax.broadcasted_iota(jnp.int32, (blocks, codes.shape[0]), 0) == codes
    return jnp.sum(jnp.where(chosen[:, :, None, None], row_grads[None], 0.0), axis=1)


class Exchange:
    def __init__(self, batch):
        self.batch = batch
        self.chips = batch // CORES
        self.by_hops = batch % CORES == 0 and 2 <= self.chips <= LINE
        self.ends_hand_over = self.by_hops and self.chips == LINE

    def swap(self, x):
        if not self.by_hops:
            return None
        return lax.ppermute(x, "batch", [(b, b ^ 1) for b in range(self.batch)])

    def both(self, x):
        return [in_hbm(x), self.swap(x)]

    def inward(self, x, sections=None):
        top = self.batch - CORES
        pairs = [(c, CORES + c) for c in range(CORES)]
        pairs += [(top + c, top - CORES + c) for c in range(CORES)]
        if sections is None:
            return lax.ppermute(x, "batch", pairs)
        pairs = [(s * self.batch + a, s * self.batch + b) for s in sections for a, b in pairs]
        return lax.ppermute(x, ("section", "batch"), pairs)

    def sources(self, x):
        return [in_hbm(x), self.inward(x)] if self.ends_hand_over else [in_hbm(x)]


def sums_by_hops(plan, exchange, back, down, up, lefts, table_grad):
    chips, rows = exchange.chips, plan.rows
    features, hidden_units = plan.features, plan.hidden_units
    core = lax.axis_index("batch") % CORES
    share = features // CORES
    swap = exchange.swap
    table_size = table_grad.shape[0]
    results = [
        (rows, 3 * features),
        (rows, features),
        (rows, hidden_units),
        (hidden_units, rows),
        (table_size, rows),
    ]
    line = Line(exchange, rows, results, up)

    def of(right, first_column):
        rights = exchange.both(right)
        pairs = [Pair(left, i, rights[i], plan.micros) for i, left in enumerate(lefts)]
        (grad,) = weight_grad(pairs, first_column, share, rows, [line.before])
        line.before = grad
        return grad

    ups = Piece([Part([up], 0, hidden_units, 2, 0, False)], 1)
    line.send(ups)
    first = 2 if exchange.ends_hand_over else 1
    downs = Piece([Part([down[0], swap(down[1])], 0, hidden_units, 3, 0, True)], first)
    line.send(downs)
    qkv = of(back.grad_packed, 0)
    out = of(back.grad_attn, share)
    norms = table_grad + swap(table_grad)
    norms = norms.reshape(table_size, chips, CORES, rows)
    norms = lax.dynamic_index_in_dim(norms, core, 2, keepdims=False).transpose(1, 0, 2)
    norms = jnp.pad(norms.astype(BF16), ((0, 0), (0, rows - table_size), (0, 0)))
    norms = norms.reshape(chips * rows, rows)
    others = Piece(
        [
            Part([qkv], 0, 3 * features, 0, 0, False),
            Part([out], 0, features, 1, 0, False),
            Part([norms], 0, rows, 4, 0, False),
        ],
        1,
    )
    last = chips - 1
    while downs.hop < last:
        line.send(downs)
    line.send(others, ups.arrivals())
    rest = ups.joined(others)
    if rest.hop < last:
        line.send(rest, downs.arrivals())
    line.finish(downs)
    while rest.hop < last:
        line.send(rest)
    line.finish(rest)
    return [line.results[i] for i in range(len(results))]


def sums_by_scatter(plan, kept, back, table_grad):
    features = plan.features
    share = features // CORES
    core = lax.axis_index("batch") % CORES

    def local(lefts, rights, column):
        pairs = [Pair(left, None, right, left.shape[0]) for left, right in zip(lefts, rights)]
        if column is None:
            mine, other = weight_grad(pairs, 0, features, plan.rows, outputs=2)
        else:
            (left,), (right,) = lefts, rights
            mine, other = [
                weight_grad(
                    [Pair(left, i, right, left.shape[1])], column, share, plan.rows
                )[0]
                for i in range(CORES)
            ]
        even, odd = jnp.where(core == 0, mine, other), jnp.where(core == 0, other, mine)
        blocks = [x.reshape(-1, 1, plan.rows, x.shape[1]) for x in (even, odd)]
        return jnp.concatenate(blocks, axis=1).reshape(features, -1)

    def scattered(x, dimension):
        return lax.psum_scatter(
            x, "batch", scatter_dimension=dimension, tiled=True
        ).astype(F32)

    grad_y = [back.y_early, back.y_last]
    down = local([jnp.concatenate(grad_y, axis=0)], [kept.act], None)
    grad_up = jnp.concatenate([back.up_early, back.up_last], axis=0)
    return (
        scattered(local([kept.left], [back.grad_packed], 0), 0),
        scattered(local([kept.left], [back.grad_attn], share), 0),
        scattered(local([kept.left], [grad_up], 2 * share), 0),
        scattered(down, 0).T,
        scattered(table_grad, 1),
    )


def per_device(
    frames_in, cotangent, qkv_weight, out_weight, up_weight, down_weight, norm_table, lengths,
    codebooks,
):
    sections = lax.axis_size("section")
    batch = lax.axis_size("batch")
    section = lax.axis_index("section")
    micros = lengths.shape[0]
    tokens, features = frames_in.shape
    frames = tokens // micros
    plan = Plan(
        sections, micros, frames, features, up_weight.shape[2], max(features // batch, LANES)
    )
    frames_all = frames_in.reshape(micros, frames, features)
    cot_all = cotangent.reshape(micros, frames, features)

    state = State(
        numbers=[lengths, codebooks],
        info=None,
        table=norm_table[0],
        weights=Weights(qkv_weight[0], out_weight[0], up_weight[0], down_weight[0]),
    )
    exchange = Exchange(batch)

    share = features // CORES

    def down_pairs(grad_ys, act):
        firsts = [span[0] for span in plan.up_spans()]
        return [Pair(y, None, act, y.shape[0], 0, at) for y, at in zip(grad_ys, firsts)]

    def up_pairs(grad_up, first):
        count = grad_up[0].shape[0]
        return [
            Pair(left, i, g, count, first, 0) for i, (left, g) in enumerate(zip(lefts, grad_up))
        ]

    before_bwd = [[] for _ in range(plan.ticks())]
    incoming = arriving = None
    working = lambda micro: 0 <= micro < micros
    for tick in range(plan.ticks()):
        sent = returned = None
        if tick < plan.fwd_ticks():
            last_fwd = tick == plan.fwd_ticks() - 1 and exchange.ends_hand_over
            state, output, act_in = run_forward(
                plan, tick, state, incoming, frames_all, second_first if last_fwd else None
            )
            if tick == micros - 1 and exchange.ends_hand_over:
                second_first = exchange.inward(first_sections(state.kept.second), [0])
            onward = [
                (s, s + 1) for s in range(sections - 1) if working(plan.fwd_id(tick, s))
            ]
            if onward:
                sent = lax.ppermute(output, "section", onward)
        if tick >= sections - 1:
            late = tick == plan.ticks() - 1
            redo = None
            if tick >= plan.ticks() - 2 and exchange.ends_hand_over:
                redo = (second_rest, act_in)
            state, output, redone = run_backward(
                plan, tick, state, arriving, cot_all, before_bwd[tick], FIRST if late else WHOLE,
                (), redo,
            )
            act_in = act_in if redone is None else redone
            if late:
                after = []
                if exchange.by_hops:
                    y_last = exchange.sources(state.back.y_last)
                    up_last = exchange.both(state.back.up_last)
                    after = up_early[1:] + y_early[1:]
                state, output, _ = run_backward(
                    plan, tick, state, arriving, cot_all, after, SECOND, output
                )
            output = output[0]
            backward = [
                (s, s - 1) for s in range(1, sections) if working(plan.bwd_id(tick, s))
            ]
            if backward:
                returned = lax.ppermute(output, "section", backward)
        incoming, arriving = sent, returned
        if exchange.by_hops:
            if tick == plan.fwd_ticks() - 1:
                lefts = [in_hbm(x) for x in exchange.both(state.kept.left)]
                before_bwd[tick + 1] += lefts[1:]
                if exchange.ends_hand_over:
                    (act_in,) = act_in
                    second_rest = exchange.inward(state.kept.second, range(1, sections))
            if tick == plan.ticks() - 2:
                y_early = exchange.sources(state.back.y_early)
                up_early = exchange.both(state.back.up_early)

    blocks = norm_table.shape[1] // 4
    codes = codebooks * (section % 2)
    table_grad = table_gradient(state.back.row_grads, codes, blocks).reshape(norm_table.shape[1:])
    if exchange.by_hops:
        sides = list(zip(y_early, y_last))
        pairs = down_pairs(sides[0], in_hbm(state.kept.act))
        if exchange.ends_hand_over:
            pairs += down_pairs(sides[1], act_in)
        ready = [output, up_last[1], up_early[1]]
        down = weight_grad(
            pairs, 0, features, plan.rows, ready, 2, exchange.ends_hand_over
        )
        pairs = up_pairs(up_early, 0) + up_pairs(up_last, micros - 1)
        (up,) = weight_grad(pairs, 2 * share, share, plan.rows, down[:1])
        sums = sums_by_hops(plan, exchange, state.back, down, up, lefts, table_grad)
    else:
        sums = sums_by_scatter(plan, state.kept, state.back, table_grad)
    return (
        state.kept.layer_out.reshape(1, tokens, features),
        state.back.grad_in.reshape(1, tokens, features),
    ) + tuple(x[None] for x in sums)


def solution(mesh):
    section, batch = mesh.axis_names
    over_batch = P(batch)
    over_section = P(section)
    both = P(section, batch, None)
    columns = P(section, None, batch)
    in_specs = (over_batch,) * 2 + (over_section,) * 5 + (over_batch,) * 2
    out_specs = (both,) * 5 + (columns,) * 2
    return jax.shard_map(
        per_device, mesh=mesh, in_specs=in_specs, out_specs=out_specs, check_vma=False
    )
```
